32 devices in a mesh: blk: 8 (over z, x), ulysses: 4 (over y, core).
Axes of the slice: x: 2, y: 2, z: 4, core: 2. Of those that a mesh axis runs over, the one named last changes fastest.
Arguments:
- tokens: bfloat16 [2, 2048, 2048], P(None, ('blk', 'ulysses')), may hold values from -6 to 6
- attn_gain: bfloat16 [2048], P('blk'), may hold values from 0.25 to 1.75
- w_query: bfloat16 [2048, 3072], P('blk', 'ulysses'), may hold values from -0.125 to 0.125
- w_latent: bfloat16 [2048, 576], P('blk'), may hold values from -0.125 to 0.125
- latent_gain: bfloat16 [512], P('blk'), may hold values from 0.25 to 1.75
- w_expand: bfloat16 [512, 4096], P('blk', 'ulysses'), may hold values from -0.25 to 0.25
- w_output: bfloat16 [2048, 2048], P('ulysses', 'blk'), may hold values from -2 to 2
- ffn_gain: bfloat16 [2048], P('blk'), may hold values from 0.25 to 1.75
- w_router: bfloat16 [2048, 64], P('blk'), may hold values from -0.0625 to 0.0625
- w_shared_gate: bfloat16 [2048, 2816], P('blk', 'ulysses'), may hold values from -0.125 to 0.125
- w_shared_up: bfloat16 [2048, 2816], P('blk', 'ulysses'), may hold values from -0.125 to 0.125
- w_shared_down: bfloat16 [2816, 2048], P('ulysses', 'blk'), may hold values from -0.15625 to 0.15625
- w_gate: bfloat16 [64, 2048, 1408], P(('blk', 'ulysses')), may hold values from -0.125 to 0.125
- w_up: bfloat16 [64, 2048, 1408], P(('blk', 'ulysses')), may hold values from -0.125 to 0.125
- w_down: bfloat16 [64, 1408, 2048], P(('blk', 'ulysses')), may hold values from -0.3125 to 0.3125
- routes: int32 [2048, 2, 6], P(('blk', 'ulysses')), may hold values from 0 to 63, all different within a row; in each aligned block of 128 rows (0 to 127, 128 to 255, ..., all dimensions but the last counted through in order) at most 14 rows name the same one
- clip_limit: float32 [1], replicated, may hold values from 1 to 2
- out_grad: bfloat16 [2, 2048, 2048], P(None, ('blk', 'ulysses')), may hold values from -6 to 6
Outputs:
- block_out: bfloat16 [2, 2048, 2048], P(None, ('blk', 'ulysses'))
- tokens_grad: bfloat16 [2, 2048, 2048], P(None, ('blk', 'ulysses'))
- attn_gain_grad: float32 [2048], P('blk')
- w_query_grad: float32 [2048, 3072], P('blk', 'ulysses')
- w_latent_grad: float32 [2048, 576], P('blk')
- latent_gain_grad: float32 [512], P('blk')
- w_expand_grad: float32 [512, 4096], P('blk', 'ulysses')
- w_output_grad: float32 [2048, 2048], P('ulysses', 'blk')
- ffn_gain_grad: float32 [2048], P('blk')
- w_router_grad: float32 [2048, 64], P('blk')
- w_shared_gate_grad: float32 [2048, 2816], P('blk', 'ulysses')
- w_shared_up_grad: float32 [2048, 2816], P('blk', 'ulysses')
- w_shared_down_grad: float32 [2816, 2048], P('ulysses', 'blk')
- w_gate_grad: float32 [64, 2048, 1408], P(('blk', 'ulysses'))
- w_up_grad: float32 [64, 2048, 1408], P(('blk', 'ulysses'))
- w_down_grad: float32 [64, 1408, 2048], P(('blk', 'ulysses'))
- clip_factor: float32 [16], P('ulysses')
The draws below stay inside these ranges and needn't reach their ends.
Inputs may be any that keep to these rules, and one draw needn't show every extreme that they name: `routes`: among the rows of one device no expert is named more than 14 times, a bound that some block reaches; the 6 experts of a row differ.
All inputs are finite; a program needn't handle non-finite values.
Results may differ from the reference program's by a relative error of at most 0.017.
Values may be sent and summed in bfloat16 or wider, within the bound.
A program may use at most 448 MiB of HBM per device.

```python
import math
import jax
import jax.numpy as jnp
import numpy as np
from jax import lax

D = 2048
H = 16
NOPE = 128
RD = 64
VH = 128
KVR = 512
EXPERTS = 64
TOP = 6
FFE = 1408
SFF = 2816
SEQS = 2
SEQ_DEV = 64
LEN = 2048
CAP = 14
SPLIT = 1
UNITS = 64
N_BLK = 8
N_ULYSSES = 4


def shard_levels(stream_key, shape, shards, smallest, largest):
    level, own = 1.0, jax.random.fold_in(stream_key, 6)
    for dim, shards_of in shards:
        draws = jnp.exp(jax.random.uniform(jax.random.fold_in(own, dim), (shards_of,), jnp.float32, smallest / len(shards), largest / len(shards)))
        level = level * jnp.repeat(draws, shape[dim] // shards_of).reshape([-1 if axis == dim else 1 for axis in range(len(shape))])
    return level


def shared_out(stream_key, own, number, rows, count, top, most, skew):
    order = jax.random.permutation(stream_key, count)
    crowded, usual = portions_of(count, rows * top, most, skew, True), portions_of(count, rows * top, most, skew, False)
    places = jnp.arange(count)

    def named(tallies, turn):
        used = int((tallies > 0).sum())
        fixed = max(1, used // 4)
        moved = fixed + (places - fixed + turn * (used - fixed)) % max(1, count - fixed)
        return jnp.zeros((count,), jnp.int32).at[order[jnp.where(places < fixed, places, moved)]].set(jnp.asarray(tallies, jnp.int32))

    tallies = jnp.where(number % 4 == 0, named(crowded, number // 4), named(usual, number - number // 4 - 1))
    mixed = jax.random.permutation(jax.random.fold_in(own, 3), count)
    donor, taker = mixed[0:count // 2 * 2:2], mixed[1:count // 2 * 2:2]
    margin = jnp.minimum(tallies[donor] - 1, most - tallies[taker]) // 2
    margin = jnp.where((donor == order[0]) | (taker == order[0]) | (tallies[taker] == 0), 0, jnp.maximum(margin, 0))
    moved = jax.random.randint(jax.random.fold_in(own, 4), (count // 2,), 0, 1 << 20) % (margin + 1)
    tallies = tallies.at[donor].add(-moved).at[taker].add(moved)
    labels = jnp.searchsorted(jnp.cumsum(tallies), jnp.arange(rows * top), side="right").astype(jnp.int32)
    table = labels.reshape(top, rows).T
    table = table[jax.random.permutation(jax.random.fold_in(own, 1), rows)]
    turn = jax.random.randint(jax.random.fold_in(own, 2), (rows, 1), 0, top)
    return jnp.take_along_axis(table, (jnp.arange(top)[None, :] + turn) % top, axis=1)


def portions_of(number_of, total, reach, slope, full):
    weights = [(1 << 20) // math.isqrt(rank ** slope) + 1 for rank in range(1, number_of + 1)]
    largest = reach if full else min(reach, max(-(-total // number_of), total * weights[0] // sum(weights)))
    least = 1 if total - largest >= number_of - 1 else 0
    counts, rest = [largest] + [least] * (number_of - 1), total - largest - least * (number_of - 1)
    while rest > 0:
        candidates = [i for i in range(1, number_of) if counts[i] < largest] or [i for i in range(1, number_of) if counts[i] < reach]
        mass, left = sum([weights[i] for i in candidates]), rest
        for i in candidates:
            addition = min(reach - counts[i], max(1, left * weights[i] // mass), rest)
            counts[i] = counts[i] + addition
            rest = rest - addition
    return np.array(counts)


def bell_draw(rng, shape, scale, limit, pieces=(), held_as=jnp.bfloat16):
    level = shard_levels(rng, shape, pieces, -0.22, 0.18) if pieces else 1.0
    values = jax.random.normal(rng, shape, jnp.float32) * scale * level
    return jnp.minimum(jnp.maximum(values, -limit), limit).astype(held_as)


def setup_inputs(seed: int = 0) -> dict:
    streams_of = jax.random.split(jax.random.key(seed), 19)
    tokens = bell_draw(streams_of[0], (SEQS, LEN, D), 1.0, 6.0, ((1, 32),))
    attn_gain = jnp.clip(1.0 + 0.15 * jax.random.normal(streams_of[1], (D,), jnp.float32), 0.25, 1.75).astype(jnp.bfloat16)
    w_query = bell_draw(streams_of[2], (D, H * (NOPE + RD)), D ** -0.5, 0.125, ((0, 8), (1, 4)))
    w_latent = bell_draw(streams_of[3], (D, KVR + RD), D ** -0.5, 0.125, ((0, 8),))
    latent_gain = jnp.clip(1.0 + 0.15 * jax.random.normal(streams_of[4], (KVR,), jnp.float32), 0.25, 1.75).astype(jnp.bfloat16)
    w_expand = bell_draw(streams_of[5], (KVR, H * (NOPE + VH)), KVR ** -0.5, 0.25, ((0, 8), (1, 4)))
    w_output = bell_draw(streams_of[6], (H * VH, D), (max(1, H * VH * 8 // LEN)) ** -0.5, 2.0, ((0, 4), (1, 8)))
    ffn_gain = jnp.clip(1.0 + 0.15 * jax.random.normal(streams_of[7], (D,), jnp.float32), 0.25, 1.75).astype(jnp.bfloat16)
    w_router = bell_draw(streams_of[8], (D, EXPERTS), (4 * D) ** -0.5, 0.0625, ((0, 8),))
    w_shared_gate = bell_draw(streams_of[9], (D, SFF), D ** -0.5, 0.125, ((0, 8), (1, 4)))
    w_shared_up = bell_draw(streams_of[10], (D, SFF), D ** -0.5, 0.125, ((0, 8), (1, 4)))
    w_shared_down = bell_draw(streams_of[11], (SFF, D), (SFF // 2) ** -0.5, 0.15625, ((0, 4), (1, 8)))
    w_gate = bell_draw(streams_of[12], (UNITS, D, FFE // SPLIT), D ** -0.5, 0.125, ((0, 32),))
    w_up = bell_draw(streams_of[13], (UNITS, D, FFE // SPLIT), D ** -0.5, 0.125, ((0, 32),))
    w_down = bell_draw(streams_of[14], (UNITS, FFE // SPLIT, D), (FFE // 4) ** -0.5, 0.3125, ((0, 32),))
    routes_keys = jax.random.split(jax.random.fold_in(streams_of[15], 1), LEN * SEQS // (2 * SEQ_DEV))
    routes_turns = jax.random.permutation(jax.random.fold_in(streams_of[15], 3), LEN * SEQS // (2 * SEQ_DEV))
    routes = jax.vmap(lambda own, number: shared_out(jax.random.fold_in(streams_of[15], 2), own, number, 2 * SEQ_DEV, EXPERTS, TOP, CAP, 1))(routes_keys, routes_turns).reshape((LEN, SEQS, TOP))
    clip_limit = jnp.clip(jax.random.uniform(streams_of[16], (1,), jnp.float32, 1.0, 2.0), 1.0, 2.0)
    out_grad = bell_draw(streams_of[17], (SEQS, LEN, D), 1.0, 6.0, ((1, 32),))
    return dict(tokens=tokens, attn_gain=attn_gain, w_query=w_query, w_latent=w_latent, latent_gain=latent_gain, w_expand=w_expand, w_output=w_output, ffn_gain=ffn_gain, w_router=w_router, w_shared_gate=w_shared_gate, w_shared_up=w_shared_up, w_shared_down=w_shared_down, w_gate=w_gate, w_up=w_up, w_down=w_down, routes=routes, clip_limit=clip_limit, out_grad=out_grad)


@jax.custom_vjp
def low(v):
    return lax.optimization_barrier(v.astype(jnp.bfloat16)).astype(jnp.float32)

@jax.custom_vjp
def low_back(v):
    return v

def low_keep(v):
    return (low(v), None)

def low_pass(kept, grad):
    return (grad,)

def back_keep(v):
    return (v, None)

def back_low(kept, grad):
    return (low(grad),)
low.defvjp(low_keep, low_pass)
low_back.defvjp(back_keep, back_low)
epsilon = 1e-06
rope_base = 10000.0

def matmul(left, right):
    return jnp.dot(left, right, precision=lax.Precision.HIGHEST, preferred_element_type=jnp.float32)

def rms_norm(values, gain):
    return values * lax.rsqrt(lax.optimization_barrier(jnp.mean(values * values, axis=-1, keepdims=True)) + epsilon) * gain

def rotary_tables(positions):
    half_width = RD // 2
    frequency = rope_base ** (-2.0 * jnp.arange(half_width).astype(jnp.float32) / RD)
    angles = positions.astype(jnp.float32)[:, None] * frequency[None, :]
    return (jnp.cos(angles), jnp.sin(angles))

def rotate(values, cosine, sine_table):
    half_width = RD // 2
    first_half = values[..., :half_width]
    second_half = values[..., half_width:]
    return jnp.concatenate([first_half * cosine - second_half * sine_table, second_half * cosine + first_half * sine_table], axis=-1)

def slot_tables(route_rows):
    flat_routes = route_rows.reshape(-1).astype(jnp.int32)
    onehot = (flat_routes[:, None] == jnp.arange(EXPERTS, dtype=jnp.int32)[None, :]).astype(jnp.int32)
    slot_rank = lax.optimization_barrier(jnp.sum((jnp.cumsum(onehot, axis=0) - 1) * onehot, axis=1)).astype(jnp.int32)
    position = (flat_routes * CAP + slot_rank).astype(jnp.int32)
    entries = flat_routes.shape[0]
    slot_pick = jnp.full((EXPERTS * CAP,), entries, jnp.int32).at[position].set(jnp.arange(entries, dtype=jnp.int32))
    return (position, slot_pick)

def attend_rows(query_rows, key_rows, value_rows, begin_row):
    scale_factor = (NOPE + RD) ** (-0.5)
    scores = low_back(matmul(query_rows, key_rows.T)) * scale_factor
    row_pos = begin_row + jnp.arange(query_rows.shape[0])
    allowed = jnp.arange(key_rows.shape[0])[None, :] <= row_pos[:, None]
    masked = jnp.where(allowed, scores, -jnp.inf)
    highest = lax.optimization_barrier(jnp.max(masked, axis=1, keepdims=True))
    exponent = jnp.exp(masked - highest)
    probability = exponent / lax.optimization_barrier(jnp.sum(exponent, axis=1, keepdims=True))
    return (matmul(low(probability), value_rows), highest[:, 0])

def attend_sequence(operands):
    query, key_all, value_all = operands
    block_rows = min(512, LEN)
    starts = (jnp.arange(LEN // block_rows) * block_rows).astype(jnp.int32)

    def per_head(head_operands):
        head_query, head_keys, head_values = head_operands

        def per_block(begin_row):
            query_rows = lax.dynamic_slice_in_dim(head_query, begin_row, block_rows, 0)
            return attend_rows(query_rows, head_keys, head_values, begin_row)
        outputs, maxima = lax.map(jax.checkpoint(per_block), starts)
        return (outputs.reshape(LEN, VH), maxima.reshape(LEN))
    outputs, maxima = lax.map(per_head, (jnp.swapaxes(query, 0, 1), jnp.swapaxes(key_all, 0, 1), jnp.swapaxes(value_all, 0, 1)))
    return (jnp.swapaxes(outputs, 0, 1), maxima)

def routed_experts(normed_mid, gate_weights, route_rows, w_gate, w_up, w_down):
    devices = N_BLK * N_ULYSSES
    rows_dev = SEQS * SEQ_DEV

    def by_device(values):
        tail = values.shape[1:]
        return jnp.swapaxes(values.reshape((SEQS, devices, SEQ_DEV) + tail), 0, 1).reshape((devices, rows_dev) + tail)
    inputs_dev = by_device(normed_mid)
    gates_dev = by_device(gate_weights)
    routes_dev = by_device(route_rows)
    positions, slot_pick = jax.vmap(slot_tables)(routes_dev)
    padded_rows = jnp.concatenate([inputs_dev, jnp.zeros((devices, 1, D), jnp.float32)], axis=1).reshape(devices * (rows_dev + 1), D)
    offsets = (jnp.arange(devices) * (rows_dev + 1)).astype(jnp.int32)
    slot_rows = (slot_pick // TOP + offsets[:, None]).astype(jnp.int32)
    padded_gates = jnp.concatenate([gates_dev.reshape(devices, rows_dev * TOP), jnp.zeros((devices, 1), jnp.float32)], axis=1)
    slot_gates = jnp.take_along_axis(padded_gates, slot_pick, axis=1)
    expert_rows = jnp.swapaxes(slot_rows.reshape(devices, EXPERTS, CAP), 0, 1).reshape(EXPERTS, devices * CAP)
    expert_gates = jnp.swapaxes(slot_gates.reshape(devices, EXPERTS, CAP), 0, 1).reshape(EXPERTS, devices * CAP)
    full_gate = w_gate.reshape(EXPERTS, SPLIT, D, FFE // SPLIT).transpose(0, 2, 1, 3).reshape(EXPERTS, D, FFE)
    full_up = w_up.reshape(EXPERTS, SPLIT, D, FFE // SPLIT).transpose(0, 2, 1, 3).reshape(EXPERTS, D, FFE)
    full_down = w_down.reshape(EXPERTS, FFE, D)

    def weighted_expert(rows_index, weights, gate_matrix, up_matrix, down_matrix):
        picked = padded_rows[rows_index]
        gate_value = low_back(matmul(picked, gate_matrix))
        up_value = low_back(matmul(picked, up_matrix))
        produced = low_back(matmul(low(jax.nn.silu(gate_value) * up_value), down_matrix))
        return weights[:, None] * produced
    checked = jax.checkpoint(weighted_expert)

    def expert_step(totals, operands):
        return (totals.at[operands[0]].add(checked(*operands)), None)
    totals, unused = lax.scan(expert_step, jnp.zeros_like(padded_rows), (expert_rows, expert_gates, full_gate, full_up, full_down))
    result = totals.reshape(devices, rows_dev + 1, D)[:, :rows_dev]
    return jnp.swapaxes(result.reshape(devices, SEQS, SEQ_DEV, D), 0, 1).reshape(SEQS * LEN, D)

def block_forward(tokens, attn_gain, w_query, w_latent, latent_gain, w_expand, w_output, ffn_gain, w_router, w_shared_gate, w_shared_up, w_shared_down, w_gate, w_up, w_down, routes):
    qk_width = NOPE + RD
    row_count = SEQS * LEN
    flat_in = tokens.reshape(row_count, D)
    normed_in = low(rms_norm(flat_in, attn_gain))
    query_lin = low_back(matmul(normed_in, w_query)).reshape(SEQS, LEN, H, qk_width)
    latent_all = low_back(matmul(normed_in, w_latent)).reshape(SEQS, LEN, KVR + RD)
    latent = low(rms_norm(latent_all[..., :KVR], latent_gain))
    expanded = matmul(latent.reshape(row_count, KVR), w_expand).reshape(SEQS, LEN, H, NOPE + VH)
    cosine, sine_table = rotary_tables(jnp.arange(LEN))
    query = jnp.concatenate([query_lin[..., :NOPE], rotate(query_lin[..., NOPE:], cosine[:, None, :], sine_table[:, None, :])], axis=-1)
    key_rope = rotate(latent_all[..., KVR:], cosine, sine_table)
    key_all = jnp.concatenate([expanded[..., :NOPE], jnp.broadcast_to(key_rope[:, :, None, :], (SEQS, LEN, H, RD))], axis=-1)
    value_all = expanded[..., NOPE:]
    query = low_back(low(query))
    key_all = low_back(low(key_all))
    value_all = low_back(low(value_all))
    attended, maxima = lax.map(attend_sequence, (query, key_all, value_all))
    attended = low_back(low(attended.reshape(row_count, H * VH)))
    residual = flat_in + low_back(matmul(attended, w_output))
    normed_mid = low(rms_norm(residual, ffn_gain))
    logits = low_back(matmul(normed_mid, w_router))
    route_rows = jnp.swapaxes(routes, 0, 1).reshape(row_count, TOP).astype(jnp.int32)
    gate_weights = jax.nn.softmax(jnp.take_along_axis(logits, route_rows, axis=1), axis=-1)
    shared_gate = low_back(matmul(normed_mid, w_shared_gate))
    shared_up = low_back(matmul(normed_mid, w_shared_up))
    shared = matmul(low(jax.nn.silu(shared_gate) * shared_up), w_shared_down)
    routed = routed_experts(normed_mid, gate_weights, route_rows, w_gate, w_up, w_down)
    return ((residual + shared + routed).reshape(SEQS, LEN, D), maxima)

def reference(tokens, attn_gain, w_query, w_latent, latent_gain, w_expand, w_output, ffn_gain, w_router, w_shared_gate, w_shared_up, w_shared_down, w_gate, w_up, w_down, routes, clip_limit, out_grad):
    floats = tuple((item.astype(jnp.float32) for item in (tokens, attn_gain, w_query, w_latent, latent_gain, w_expand, w_output, ffn_gain, w_router, w_shared_gate, w_shared_up, w_shared_down, w_gate, w_up, w_down)))

    def forward(*values):
        return block_forward(*values, routes)
    output, vjp_function, maxima = jax.vjp(forward, *floats, has_aux=True)
    grads = vjp_function(out_grad.astype(jnp.float32))
    head_top = lax.optimization_barrier(jnp.max(maxima, axis=(0, 2)))
    clip_factor = clip_limit[0] / jnp.maximum(head_top, clip_limit[0])
    return (output.astype(jnp.bfloat16), grads[0].astype(jnp.bfloat16), grads[1], grads[2], grads[3], grads[4], grads[5], grads[6], grads[7], grads[8], grads[9], grads[10], grads[11], grads[12], grads[13], grads[14], clip_factor)
```

```python
import jax
import jax.numpy as jnp
from jax import lax
from jax.sharding import Mesh
from jax.sharding import PartitionSpec as P

H = 16
NOPE = 128
RD = 64
VH = 128
KVR = 512
EXPERTS = 64
TOP = 6
CAP = 14
Z_SIZE = 4
CORES = 2

epsilon = 1e-06
rope_base = 10000.0
wide = jnp.float32
narrow = jnp.bfloat16


def dot(a, b, out=wide):
    return jnp.dot(a, b, preferred_element_type=out)


def dot_tn(a, b, out=wide):
    return lax.dot_general(a, b, (((0,), (0,)), ((), ())), preferred_element_type=out)


def dot_nt(a, b, out=wide):
    return lax.dot_general(a, b, (((1,), (1,)), ((), ())), preferred_element_type=out)


def norm_rows(values, gain):
    inverse = lax.rsqrt(jnp.mean(values * values, axis=-1, keepdims=True) + epsilon)
    normed = values * inverse
    return (normed * gain, normed, inverse)


def norm_input_back(grad_out, normed, inverse, gain):
    scaled = grad_out * gain
    return inverse * (scaled - normed * jnp.mean(scaled * normed, axis=-1, keepdims=True))


def rotary_tables(positions):
    half_width = RD // 2
    frequency = rope_base ** (-2.0 * jnp.arange(half_width).astype(wide) / RD)
    angles = positions.astype(wide)[:, None] * frequency[None, :]
    return (jnp.cos(angles), jnp.sin(angles))


def rotate(values, cosine, sine):
    half = RD // 2
    a, b = values[..., :half], values[..., half:]
    return jnp.concatenate([a * cosine - b * sine, b * cosine + a * sine], axis=-1)


def unrotate(values, cosine, sine):
    half = RD // 2
    a, b = values[..., :half], values[..., half:]
    return jnp.concatenate([a * cosine + b * sine, b * cosine - a * sine], axis=-1)


def silu_slope(values):
    s = jax.nn.sigmoid(values)
    return s * (1.0 + values * (1.0 - s))


def hop(value, axis):
    n = lax.axis_size(axis)
    return lax.ppermute(value, axis, [(i, (i + 1) % n) for i in range(n)])


def ring(value, axis):
    items = [value]
    for _ in range(lax.axis_size(axis) - 1):
        items.append(hop(items[-1], axis))
    return items


def ring_sum(blocks, axis):
    n = lax.axis_size(axis)
    if n == 1:
        return blocks[0].astype(wide)
    running = hop(blocks[1].astype(narrow), axis)
    for s in range(2, n):
        running = hop((running.astype(wide) + blocks[s].astype(wide)).astype(narrow), axis)
    return running.astype(wide) + blocks[0].astype(wide)


def flat_ring(value, axes):
    items = [value]
    for axis in axes:
        items = [piece for item in items for piece in ring(item, axis)]
    return items


def tree_sum(blocks, axes):
    for axis in reversed(axes):
        n = lax.axis_size(axis)
        blocks = [ring_sum(blocks[i : i + n], axis) for i in range(0, len(blocks), n)]
    return blocks[0]


def per_device(
    tokens, attn_gain, w_query, w_latent, latent_gain, w_expand, w_output, ffn_gain, w_router,
    w_shared_gate, w_shared_up, w_shared_down, w_gate, w_up, w_down, routes, clip_limit, out_grad,
):
    seqs, local_len, features = tokens.shape
    rows = seqs * local_len
    qk = NOPE + RD
    nz, nx, ny, nc = (lax.axis_size(a) for a in ("z", "x", "y", "core"))
    zi, xi, yi, ci = (lax.axis_index(a) for a in ("z", "x", "y", "core"))
    nb, nu = nz * nx, ny * nc
    layer = nx * nu
    heads = H // nu
    group = nu * rows
    all_rows = nb * group
    upd = w_gate.shape[0]
    split = upd * nz * layer // EXPERTS
    scale = qk ** (-0.5)
    GROUP = ("y", "core")
    ALL = ("z", "x", "y", "core")
    LAYER = ("x", "y", "core")

    def gather_blk(shard, dim):
        size = shard.shape[dim]
        shape = list(shard.shape)
        shape[dim] = size * nb
        whole = jnp.zeros(tuple(shape), shard.dtype)
        for sz, behind in enumerate(ring(shard, "z")):
            for sx, piece in enumerate(ring(behind, "x")):
                owner = ((zi + nz - sz) % nz) * nx + (xi + nx - sx) % nx
                whole = lax.dynamic_update_slice_in_dim(whole, piece, owner * size, dim)
        return whole

    def scatter_blk(whole, dim):
        size = whole.shape[dim] // nb
        blocks = []
        for sz in range(nz):
            for sx in range(nx):
                owner = ((zi + nz - sz) % nz) * nx + (xi + nx - sx) % nx
                blocks.append(lax.dynamic_slice_in_dim(whole, owner * size, size, dim))
        return tree_sum(blocks, ("z", "x"))

    def group_gather(value):
        return jnp.concatenate(flat_ring(value, GROUP), axis=0)

    def group_scatter(value):
        return tree_sum([value[i * rows : (i + 1) * rows] for i in range(nu)], GROUP)

    def group_sum(value):
        for axis in GROUP:
            items = ring(value, axis)
            value = sum(item.astype(wide) for item in items)
        return value

    def device_positions(blk, u):
        return (blk * nu + u) * local_len + jnp.arange(local_len, dtype=jnp.int32)

    local_pos = device_positions(zi * nx + xi, yi * nc + ci)
    group_pos = jnp.concatenate(
        [
            device_positions(zi * nx + xi, (yi + ny - sy) % ny * nc + (ci + nc - sc) % nc)
            for sy in range(ny)
            for sc in range(nc)
        ]
    )
    key_pos = jnp.concatenate(
        [
            device_positions(
                (zi + nz - sz) % nz * nx + (xi + nx - sx) % nx,
                (yi + ny - sy) % ny * nc + (ci + nc - sc) % nc,
            )
            for sz in range(nz)
            for sx in range(nx)
            for sy in range(ny)
            for sc in range(nc)
        ]
    )

    small = jnp.concatenate(
        [
            w_latent,
            w_router,
            attn_gain[:, None],
            ffn_gain[:, None],
            jnp.pad(latent_gain, (0, attn_gain.shape[0] - latent_gain.shape[0]))[:, None],
        ],
        axis=1,
    )
    small_whole = gather_blk(small, 0)
    tokens_local = tokens.reshape(rows, features)
    grad_narrow = out_grad.reshape(rows, features)
    tokens_group = group_gather(tokens_local)
    latent_w = small_whole[:, : KVR + RD]
    router_w = small_whole[:, KVR + RD : KVR + RD + EXPERTS]
    gain_attn = small_whole[:, KVR + RD + EXPERTS].astype(wide)
    gain_ffn = small_whole[:, KVR + RD + EXPERTS + 1].astype(wide)
    gain_latent = (
        small_whole[:, KVR + RD + EXPERTS + 2]
        .reshape(nb, -1)[:, : latent_gain.shape[0]]
        .reshape(-1)
        .astype(wide)
    )
    query_w = gather_blk(w_query, 0)
    expand_w = gather_blk(w_expand, 0)
    output_w = gather_blk(w_output, 1)

    inputs = tokens_local.astype(wide)
    scaled_in, normed_in, inverse_in = norm_rows(inputs, gain_attn)
    hidden_local = scaled_in.astype(narrow)
    latent_all = dot(hidden_local, latent_w)
    scaled_lat, normed_lat, inverse_lat = norm_rows(latent_all[:, :KVR], gain_latent)
    cos_local, sin_local = rotary_tables(jnp.tile(local_pos, seqs))
    latent_pack = jnp.concatenate(
        [scaled_lat, rotate(latent_all[:, KVR:], cos_local, sin_local)], axis=-1
    ).astype(narrow)
    latent_keys = jnp.concatenate(
        [p.reshape(seqs, local_len, KVR + RD) for p in flat_ring(latent_pack, ALL)], axis=1
    )
    length = latent_keys.shape[1]
    latent_rows = latent_keys[..., :KVR].reshape(all_rows, KVR)
    rope_keys = latent_keys[..., KVR:]

    grad_group = group_gather(grad_narrow)

    route_line = jnp.concatenate(
        ring(jnp.swapaxes(routes, 0, 1).reshape(rows, TOP), "z"), axis=0
    ).reshape(nz, rows, TOP)
    member = jnp.any(
        route_line[..., None] == jnp.arange(EXPERTS, dtype=jnp.int32), axis=2
    )
    earlier = (
        jnp.arange(rows, dtype=jnp.int32)[None, :] < jnp.arange(rows, dtype=jnp.int32)[:, None]
    ).astype(narrow)
    rank = jnp.einsum(
        "tq,zqe->zte", earlier, member.astype(narrow), preferred_element_type=wide
    ).astype(jnp.int32)
    here = EXPERTS // nz
    rank = jnp.where(member, rank, -1)
    rank_layer = lax.dynamic_slice_in_dim(rank, zi * here, here, 2)
    picks = []
    for a in range(upd):
        experts = [(d * upd + a) // split for d in range(layer)]
        chosen = jnp.stack([rank_layer[..., e] for e in experts], axis=-1)
        hit = chosen[..., None] == jnp.arange(CAP, dtype=jnp.int32)
        own = jnp.eye(nz, dtype=jnp.bool_)
        pick = hit[:, :, :, None, :] & own[:, None, None, :, None]
        picks.append(pick.astype(narrow).reshape(nz * rows, layer * nz * CAP))

    def to_experts(line):
        return [
            lax.all_to_all(
                dot_tn(pick, line, narrow).reshape(layer, nz * CAP, -1),
                LAYER, split_axis=0, concat_axis=0, tiled=True,
            ).reshape(layer * nz * CAP, -1)
            for pick in picks
        ]

    def from_experts(parts):
        back = [
            lax.all_to_all(
                part.reshape(layer, nz * CAP, -1), LAYER, split_axis=0, concat_axis=0, tiled=True
            ).reshape(layer * nz * CAP, -1)
            for part in parts
        ]
        line = sum(dot(pick, rows_back) for pick, rows_back in zip(picks, back))
        return ring_sum([line[i * rows : (i + 1) * rows] for i in range(nz)], "z")

    grad_line = jnp.concatenate(ring(grad_narrow, "z"), axis=0)
    expert_grads = to_experts(grad_line)
    down_back = [dot_nt(expert_grads[a], w_down[a]) for a in range(upd)]

    gate_w = gather_blk(w_shared_gate, 0)
    up_w = gather_blk(w_shared_up, 0)
    down_w = gather_blk(w_shared_down, 1)

    hidden_group = norm_rows(tokens_group.astype(wide), gain_attn)[0].astype(narrow)
    cos_group, sin_group = rotary_tables(
        jnp.repeat(group_pos.reshape(nu, 1, local_len), seqs, 1).reshape(-1)
    )
    query_lin = dot(hidden_group, query_w).reshape(group, heads, qk)
    query_rows = jnp.concatenate(
        [
            query_lin[..., :NOPE],
            rotate(query_lin[..., NOPE:], cos_group[:, None, :], sin_group[:, None, :]),
        ],
        axis=-1,
    ).astype(narrow)

    def by_seq(values):
        tail = values.shape[1:]
        return jnp.swapaxes(values.reshape((nu, seqs, local_len) + tail), 0, 1).reshape(
            (seqs, nu * local_len) + tail
        )

    def from_seq(values):
        tail = values.shape[2:]
        return jnp.swapaxes(values.reshape((seqs, nu, local_len) + tail), 0, 1).reshape(
            (group,) + tail
        )

    query_four = by_seq(query_rows)
    expanded = dot(latent_rows, expand_w, narrow).reshape(seqs, length, heads, NOPE + VH)
    rope_wide = jnp.broadcast_to(rope_keys[:, :, None, :], (seqs, length, heads, RD))
    key_four = jnp.concatenate([expanded[..., :NOPE], rope_wide], axis=-1)
    value_four = expanded[..., NOPE:]
    allowed = key_pos[None, :] <= group_pos[:, None]
    scores = (
        jnp.einsum("sqhc,skhc->shqk", query_four, key_four, preferred_element_type=wide) * scale
    )
    masked = jnp.where(allowed, scores, -jnp.inf)
    maxima = jnp.max(masked, axis=-1)
    totals = jnp.sum(jnp.exp(masked - maxima[..., None]), axis=-1)
    log_sum = maxima + jnp.log(totals)
    probability = jnp.exp(masked - log_sum[..., None])
    prob_narrow = probability.astype(narrow)
    attention = jnp.einsum(
        "shqk,skhd->sqhd", prob_narrow, value_four, preferred_element_type=wide
    )
    attended = from_seq(attention).reshape(group, heads * VH).astype(narrow)

    top = jnp.max(maxima, axis=(0, 2))
    for axis in ("z", "x"):
        items = ring(top, axis)
        for item in items[1:]:
            top = jnp.maximum(top, item)
    clip_value = clip_limit[0]
    clip_factor = clip_value / jnp.maximum(top, clip_value)

    residual = inputs + group_scatter(dot(attended, output_w, narrow))
    scaled_mid, normed_mid, inverse_mid = norm_rows(residual, gain_ffn)
    hidden_mid = scaled_mid.astype(narrow)

    logits = dot(hidden_mid, router_w)
    own_member = member[0]
    chosen_logits = jnp.where(own_member, logits, -jnp.inf)
    raised = jnp.exp(chosen_logits - jnp.max(chosen_logits, axis=-1, keepdims=True))
    gates = raised / jnp.sum(raised, axis=-1, keepdims=True)

    def halves(values):
        high = values.astype(narrow)
        return [high, (values - high.astype(wide)).astype(narrow)]

    dispatch_line = jnp.concatenate(
        ring(jnp.concatenate([hidden_mid] + halves(gates), axis=1), "z"), axis=0
    )
    expert_rows = to_experts(dispatch_line)
    hidden_mid_group = group_gather(hidden_mid)

    shared_gate = dot(hidden_mid_group, gate_w)
    shared_up = dot(hidden_mid_group, up_w)
    shared_act = (jax.nn.silu(shared_gate) * shared_up).astype(narrow)
    shared_partial = dot(shared_act, down_w, narrow)
    shared_act_grad = dot_nt(grad_group, down_w)
    shared_gate_grad = (shared_act_grad * shared_up * silu_slope(shared_gate)).astype(narrow)
    shared_up_grad = (shared_act_grad * jax.nn.silu(shared_gate)).astype(narrow)
    mid_shared = dot_nt(shared_gate_grad, gate_w) + dot_nt(shared_up_grad, up_w)
    mid_shared_local = group_scatter(mid_shared.astype(narrow))
    shared_local = group_scatter(shared_partial)

    first_unit = ((zi * nx + xi) * nu + yi * nc + ci) * upd
    returned, outputs, gate_wgrad, up_wgrad, down_wgrad = [], [], [], [], []
    for a in range(upd):
        expert = (first_unit + a) // split
        lane = jnp.arange(EXPERTS, dtype=jnp.int32)[None, :] == expert
        picked = expert_rows[a][:, :features]
        gate_lanes = expert_rows[a][:, features:].astype(wide)
        weight = jnp.sum(
            jnp.where(lane, gate_lanes[:, :EXPERTS] + gate_lanes[:, EXPERTS:], 0.0),
            axis=1, keepdims=True,
        )
        unit_gate = dot(picked, w_gate[a])
        unit_up = dot(picked, w_up[a])
        unit_act = (jax.nn.silu(unit_gate) * unit_up).astype(narrow)
        unit_out = dot(unit_act, w_down[a])
        grad_rows = expert_grads[a].astype(wide)
        gate_grad = jnp.sum(unit_out * grad_rows, axis=1, keepdims=True)
        act_grad = down_back[a] * weight
        lin_gate_grad = (act_grad * unit_up * silu_slope(unit_gate)).astype(narrow)
        lin_up_grad = (act_grad * jax.nn.silu(unit_gate)).astype(narrow)
        unit_in_grad = dot_nt(lin_gate_grad, w_gate[a]) + dot_nt(lin_up_grad, w_up[a])
        returned.append(
            jnp.concatenate(
                [unit_in_grad.astype(narrow)]
                + [jnp.where(lane, half, jnp.zeros((), narrow)) for half in halves(gate_grad)],
                axis=1,
            )
        )
        outputs.append((unit_out * weight).astype(narrow))
        route_grad = (grad_rows * weight).astype(narrow)
        gate_wgrad.append(dot_tn(picked, lin_gate_grad))
        up_wgrad.append(dot_tn(picked, lin_up_grad))
        down_wgrad.append(dot_tn(unit_act, route_grad))
    gate_wgrad, up_wgrad, down_wgrad = (
        jnp.stack(items) for items in (gate_wgrad, up_wgrad, down_wgrad)
    )

    back = from_experts(returned)
    routed = from_experts(outputs)
    block_out = (residual + shared_local + routed).astype(narrow).reshape(tokens.shape)

    shared_gate_wgrad = scatter_blk(dot_tn(hidden_mid_group, shared_gate_grad, narrow), 0)
    shared_up_wgrad = scatter_blk(dot_tn(hidden_mid_group, shared_up_grad, narrow), 0)
    shared_down_wgrad = scatter_blk(dot_tn(shared_act, grad_group, narrow), 1)

    grad_wide = grad_narrow.astype(wide)
    gate_grads = back[:, features : features + EXPERTS] + back[:, features + EXPERTS :]
    logit_grad = (
        gates * (gate_grads - jnp.sum(gates * gate_grads, axis=-1, keepdims=True))
    ).astype(narrow)
    mid_grad = back[:, :features] + mid_shared_local + dot_nt(logit_grad, router_w)
    residual_grad = grad_wide + norm_input_back(mid_grad, normed_mid, inverse_mid, gain_ffn)
    ffn_gain_grad = jnp.sum(mid_grad * normed_mid, axis=0)
    router_wgrad = dot_tn(hidden_mid, logit_grad)
    mid_small = group_sum(
        scatter_blk(
            jnp.concatenate([router_wgrad, ffn_gain_grad[:, None]], axis=1).astype(narrow), 0
        )
    )

    attn_grad = group_gather(residual_grad.astype(narrow))
    attended_grad = dot_nt(attn_grad, output_w, narrow)
    output_wgrad = scatter_blk(dot_tn(attended, attn_grad, narrow), 1)

    grad_four = by_seq(attended_grad.reshape(group, heads, VH))
    prob_grad = jnp.einsum("sqhd,skhd->shqk", grad_four, value_four, preferred_element_type=wide)
    row_delta = jnp.einsum("sqhd,sqhd->shq", grad_four, attention, preferred_element_type=wide)
    score_grad = (probability * (prob_grad - row_delta[..., None]) * scale).astype(narrow)
    query_acc = jnp.einsum("shqk,skhc->sqhc", score_grad, key_four, preferred_element_type=wide)
    key_grad = jnp.einsum("shqk,sqhc->skhc", score_grad, query_four, preferred_element_type=wide)
    value_grad = jnp.einsum("shqk,sqhd->skhd", prob_narrow, grad_four, preferred_element_type=wide)

    query_back = from_seq(query_acc)
    query_lin_grad = (
        jnp.concatenate(
            [
                query_back[..., :NOPE],
                unrotate(query_back[..., NOPE:], cos_group[:, None, :], sin_group[:, None, :]),
            ],
            axis=-1,
        )
        .reshape(group, heads * qk)
        .astype(narrow)
    )
    hidden_sum = group_scatter(dot_nt(query_lin_grad, query_w, narrow))
    expand_grad = (
        jnp.concatenate([key_grad[..., :NOPE], value_grad], axis=-1)
        .astype(narrow)
        .reshape(all_rows, heads * (NOPE + VH))
    )
    rope_partial = jnp.sum(key_grad[..., NOPE:], axis=2)
    latent_partial = jnp.concatenate(
        [dot_nt(expand_grad, expand_w).reshape(seqs, length, KVR), rope_partial], axis=-1
    ).astype(narrow)
    latent_sum = tree_sum(
        [
            latent_partial[:, i * local_len : (i + 1) * local_len].reshape(rows, KVR + RD)
            for i in range(nb * nu)
        ],
        ALL,
    )
    query_wgrad = scatter_blk(dot_tn(hidden_group, query_lin_grad, narrow), 0)
    expand_wgrad = scatter_blk(dot_tn(latent_rows, expand_grad, narrow), 0)

    latent_grad = latent_sum[:, :KVR]
    key_rope_grad = unrotate(latent_sum[:, KVR:], cos_local, sin_local)
    latent_in_grad = norm_input_back(latent_grad, normed_lat, inverse_lat, gain_latent)
    latent_gain_grad = jnp.sum(latent_grad * normed_lat, axis=0)
    latent_all_grad = jnp.concatenate([latent_in_grad, key_rope_grad], axis=-1).astype(narrow)
    hidden_grad = hidden_sum + dot_nt(latent_all_grad, latent_w)
    input_grad = norm_input_back(hidden_grad, normed_in, inverse_in, gain_attn)
    attn_gain_grad = jnp.sum(hidden_grad * normed_in, axis=0)
    tokens_grad = (residual_grad + input_grad).astype(narrow).reshape(tokens.shape)
    latent_wgrad = dot_tn(hidden_local, latent_all_grad)
    lat_len = latent_gain.shape[0]
    latent_gain_column = jnp.pad(
        latent_gain_grad.reshape(nb, lat_len), ((0, 0), (0, attn_gain.shape[0] - lat_len))
    ).reshape(-1)
    in_small = group_sum(
        scatter_blk(
            jnp.concatenate(
                [latent_wgrad, attn_gain_grad[:, None], latent_gain_column[:, None]], axis=1
            ).astype(narrow),
            0,
        )
    )
    width = KVR + RD
    return (
        block_out,
        tokens_grad,
        in_small[:, width],
        query_wgrad,
        in_small[:, :width],
        in_small[:lat_len, width + 1],
        expand_wgrad,
        output_wgrad,
        mid_small[:, EXPERTS],
        mid_small[:, :EXPERTS],
        shared_gate_wgrad,
        shared_up_wgrad,
        shared_down_wgrad,
        gate_wgrad,
        up_wgrad,
        down_wgrad,
        clip_factor,
    )


def solution(mesh):
    blocks, group = mesh.shape["blk"], mesh.shape["ulysses"]
    chips = Mesh(
        mesh.devices.reshape(Z_SIZE, blocks // Z_SIZE, group // CORES, CORES),
        ("z", "x", "y", "core"),
    )
    blk, uly, every = ("z", "x"), ("y", "core"), ("z", "x", "y", "core")
    rows = P(None, every, None)
    unit = P(every, None, None)
    return jax.shard_map(
        per_device,
        mesh=chips,
        in_specs=(
            rows, P(blk), P(blk, uly), P(blk, None), P(blk), P(blk, uly), P(uly, blk), P(blk),
            P(blk, None), P(blk, uly), P(blk, uly), P(uly, blk), unit, unit, unit, unit, P(), rows,
        ),
        out_specs=(
            rows, rows, P(blk), P(blk, uly), P(blk, None), P(blk), P(blk, uly), P(uly, blk), P(blk),
            P(blk, None), P(blk, uly), P(blk, uly), P(uly, blk), unit, unit, unit, P(uly),
        ),
        check_vma=False,
    )
```

```python
import functools

import jax
import jax.numpy as jnp
from jax import lax
from jax.experimental import pallas as pl
from jax.experimental.pallas import tpu as pltpu
from jax.sharding import Mesh
from jax.sharding import PartitionSpec as P

H = 16
NOPE = 128
RD = 64
VH = 128
KVR = 512
EXPERTS = 64
TOP = 6
CAP = 14
SLOTS = 16
Z_SIZE = 4
CORES = 2

epsilon = 1e-06
rope_base = 10000.0
wide = jnp.float32
narrow = jnp.bfloat16


def dot(a, b, out=wide):
    return jnp.dot(a, b, preferred_element_type=out)


def dot_tn(a, b, out=wide):
    return lax.dot_general(a, b, (((0,), (0,)), ((), ())), preferred_element_type=out)


def dot_nt(a, b, out=wide):
    return lax.dot_general(a, b, (((1,), (1,)), ((), ())), preferred_element_type=out)


def norm_rows(values, gain):
    inverse = lax.rsqrt(jnp.mean(values * values, axis=-1, keepdims=True) + epsilon)
    normed = values * inverse
    return (normed * gain, normed, inverse)


def norm_input_back(grad_out, normed, inverse, gain):
    scaled = grad_out * gain
    return inverse * (scaled - normed * jnp.mean(scaled * normed, axis=-1, keepdims=True))


def rotary_tables(positions):
    half_width = RD // 2
    frequency = rope_base ** (-2.0 * jnp.arange(half_width).astype(wide) / RD)
    angles = positions.astype(wide)[:, None] * frequency[None, :]
    return (jnp.cos(angles), jnp.sin(angles))


def rotate(values, cosine, sine):
    half = RD // 2
    a, b = values[..., :half], values[..., half:]
    return jnp.concatenate([a * cosine - b * sine, b * cosine + a * sine], axis=-1)


def unrotate(values, cosine, sine):
    half = RD // 2
    a, b = values[..., :half], values[..., half:]
    return jnp.concatenate([a * cosine + b * sine, b * cosine - a * sine], axis=-1)


def silu_slope(values):
    s = jax.nn.sigmoid(values)
    return s * (1.0 + values * (1.0 - s))


def hop(value, axis):
    n = lax.axis_size(axis)
    return lax.ppermute(value, axis, [(i, (i + 1) % n) for i in range(n)])


def ring(value, axis):
    items = [value]
    for _ in range(lax.axis_size(axis) - 1):
        items.append(hop(items[-1], axis))
    return items


def ring_sum(blocks, axis):
    n = lax.axis_size(axis)
    if n == 1:
        return blocks[0].astype(wide)
    running = hop(blocks[1].astype(narrow), axis)
    for s in range(2, n):
        running = hop((running.astype(wide) + blocks[s].astype(wide)).astype(narrow), axis)
    return running.astype(wide) + blocks[0].astype(wide)


def flat_ring(value, axes):
    items = [value]
    for axis in axes:
        items = [piece for item in items for piece in ring(item, axis)]
    return items


def tree_sum(blocks, axes):
    for axis in reversed(axes):
        n = lax.axis_size(axis)
        blocks = [ring_sum(blocks[i : i + n], axis) for i in range(0, len(blocks), n)]
    return blocks[0]


ANY = pl.BlockSpec(memory_space=pl.ANY)
VMEM = pl.BlockSpec(memory_space=pltpu.VMEM)
MESH = pl.DeviceIdType.MESH
AXES = ("z", "x", "y", "core")


def behind(axis, steps):
    n = lax.axis_size(axis)
    return lax.rem(lax.axis_index(axis) + (n - steps), n)


def ahead(axis):
    n = lax.axis_size(axis)
    return lax.rem(lax.axis_index(axis) + 1, n)


def greet(axes):
    barrier = pltpu.get_barrier_semaphore()
    for axis in axes:
        pl.semaphore_signal(
            barrier, inc=1, device_id={axis: behind(axis, 1)}, device_id_type=MESH
        )
    pl.semaphore_wait(barrier, len(axes))


class Wires:
    def __init__(self, send, recv):
        self.send, self.recv, self.used, self.sent = send, recv, 0, []

    def port(self):
        self.used += 1
        return self.used - 1

    def push(self, src, dst, port, axis):
        copy = pltpu.make_async_remote_copy(
            src_ref=src,
            dst_ref=dst,
            send_sem=self.send.at[port],
            recv_sem=self.recv.at[port],
            device_id={axis: ahead(axis)},
            device_id_type=MESH,
        )
        copy.start()
        self.sent.append(copy)

    def arrived(self, dst, port, axis):
        pltpu.make_async_remote_copy(
            src_ref=dst,
            dst_ref=dst,
            send_sem=self.send.at[port],
            recv_sem=self.recv.at[port],
            device_id={axis: ahead(axis)},
            device_id_type=MESH,
        ).wait_recv()

    def drain(self):
        for copy in self.sent:
            copy.wait_send()


class BlockGather:
    def __init__(self, wires, src, dst, place, x_first):
        self.wires, self.src, self.dst, self.place, self.x_first = wires, src, dst, place, x_first
        self.nz, self.nx = lax.axis_size("z"), lax.axis_size("x")
        self.ports = {
            (sz, sx): wires.port() for sz in range(self.nz) for sx in range(self.nx) if sz or sx
        }

    def at(self, sz, sx):
        return self.place(self.dst, behind("z", sz) * self.nx + behind("x", sx))

    def forward(self, sz, sx):
        src = self.src if sz == 0 and sx == 0 else self.at(sz, sx)
        if self.x_first:
            go_x, go_z = sz == 0, True
        else:
            go_x, go_z = True, sx == 0
        if go_z and sz + 1 < self.nz:
            self.wires.push(src, self.at(sz, sx), self.ports[sz + 1, sx], "z")
        if go_x and sx + 1 < self.nx:
            self.wires.push(src, self.at(sz, sx), self.ports[sz, sx + 1], "x")

    def take(self, sz, sx):
        from_x = sx > 0 and (sz == 0 if self.x_first else True)
        self.wires.arrived(self.at(sz, sx), self.ports[sz, sx], "x" if from_x else "z")
        self.forward(sz, sx)

    def chain(self):
        self.forward(0, 0)
        for slots in self.rounds():
            for slot in slots:
                yield
                self.take(*slot)

    def rounds(self):
        if self.x_first:
            order = [[(0, sx)] for sx in range(1, self.nx)]
            order += [[(sz, sx) for sx in range(self.nx)] for sz in range(1, self.nz)]
            return order
        last = [[(sz, sx) for sz in range(self.nz)] for sx in range(1, self.nx)]
        return [[(sz, 0)] for sz in range(1, self.nz)] + last


def rows_of(size):
    return lambda ref, owner: ref.at[pl.ds(pl.multiple_of(owner * size, size), size)]


def columns_of(size):
    return lambda ref, owner: ref.at[:, pl.ds(pl.multiple_of(owner * size, size), size)]


def start_kernel(
    tokens, grads, cosine, sine, gains, small, routes, w_query, w_expand, w_output,
    gains_out, small_out, query_out, expand_out, output_out,
    tokens_out, grads_out, line_out, routes_out, latents_out, hidden_out, latent_all_out,
    own_latent, send, recv, local,
):
    nz, nx, ny, nc = (lax.axis_size(a) for a in AXES)
    nb, nu = nz * nx, ny * nc
    me = lax.axis_index("z") * nx + lax.axis_index("x")
    uly = lax.axis_index("y") * nc + lax.axis_index("core")
    seqs, local_len, features = tokens.shape
    rows = seqs * local_len
    greet(AXES)
    wires = Wires(send, recv)
    used, waited = [], set()

    def load(src, dst):
        copy = pltpu.make_async_copy(src, dst, local.at[len(used)])
        used.append(copy)
        copy.start()
        return copy

    def member(sy, sc):
        return behind("y", sy) * nc + behind("core", sc)

    def line_chain(src, dst):
        ports = [wires.port() for _ in range(nz)]
        wires.push(src, dst.at[1], ports[1], "z")
        load(src, dst.at[0])
        for sz in range(1, nz):
            yield
            wires.arrived(dst.at[sz], ports[sz], "z")
            if sz + 1 < nz:
                wires.push(dst.at[sz], dst.at[sz + 1], ports[sz + 1], "z")

    def main():
        g_gains = BlockGather(wires, gains, gains_out, lambda ref, owner: ref.at[owner], False)
        g_small = BlockGather(
            wires, small.at[uly], small_out, lambda ref, owner: ref.at[owner, uly], False
        )
        slots = [(0, 0)] + [slot for r in g_small.rounds() for slot in r]
        y_ports = {(slot, sy): wires.port() for slot in slots for sy in range(1, ny)}
        c_ports = {(slot, sy): wires.port() for slot in slots for sy in range(ny)}

        def piece(slot, sy, sc):
            owner = behind("z", slot[0]) * nx + behind("x", slot[1])
            return small_out.at[owner, member(sy, sc)]

        def spread(slot):
            here = piece(slot, 0, 0)
            if ny > 1:
                wires.push(here, here, y_ports[slot, 1], "y")
            wires.push(here, here, c_ports[slot, 0], "core")

        g_small.forward(0, 0)
        g_gains.forward(0, 0)
        mine = [load(small.at[uly], small_out.at[me, uly]), load(gains, gains_out.at[me])]
        yield
        for slots_now in g_small.rounds():
            for slot in slots_now:
                yield
                g_small.take(*slot)
                if mine:
                    for copy in mine:
                        copy.wait()
                    waited.update(id(copy) for copy in mine)
                    mine = []
                    spread((0, 0))
                spread(slot)
                g_gains.take(*slot)
        for sy in range(1, ny):
            for slot in slots:
                yield
                here = piece(slot, sy, 0)
                wires.arrived(here, y_ports[slot, sy], "y")
                if sy + 1 < ny:
                    wires.push(here, here, y_ports[slot, sy + 1], "y")
                wires.push(here, here, c_ports[slot, sy], "core")
        for sy in range(ny):
            for slot in slots:
                wires.arrived(piece(slot, sy, 1), c_ports[slot, sy], "core")
        gain = jnp.concatenate([gains_out[b, 0:1, : features // nb] for b in range(nb)], axis=1)
        latent_gain = sum(gains_out[b, 2:3, :] for b in range(nb))
        x = tokens[...].astype(wide).reshape(rows, features)
        hidden = norm_rows(x, gain)[0].astype(narrow)
        hidden_out[...] = hidden
        width = small_out.shape[-1]
        latent_all = dot(hidden, small_out[...].reshape(features, width))[:, : KVR + RD]
        latent_all_out[...] = latent_all
        latent = norm_rows(latent_all[:, :KVR], latent_gain)[0]
        rope = rotate(latent_all[:, KVR:], cosine[...], sine[...])
        own_latent[:, :, KVR:] = jnp.zeros((seqs, local_len, NOPE), narrow)
        own_latent[:, :, :KVR] = latent.astype(narrow).reshape(seqs, local_len, KVR)
        own_latent[:, :, KVR : KVR + RD] = rope.astype(narrow).reshape(seqs, local_len, RD)
        z_ports = [wires.port() for _ in range(nz)]
        x_ports = [wires.port() for _ in range(nx)]
        yx_ports = [[wires.port() for _ in range(nx)] for _ in range(ny)]
        cx_ports = [[wires.port() for _ in range(nx)] for _ in range(ny)]
        wires.push(own_latent, latents_out.at[:, 0, 0, 0, 1], z_ports[1], "z")
        own_place = load(own_latent, latents_out.at[:, 0, 0, 0, 0])
        for sz in range(1, nz):
            yield
            here = latents_out.at[:, 0, 0, 0, sz]
            wires.arrived(here, z_ports[sz], "z")
            if sz + 1 < nz:
                wires.push(here, latents_out.at[:, 0, 0, 0, sz + 1], z_ports[sz + 1], "z")
        own_place.wait()
        waited.add(id(own_place))
        for sx in range(nx):
            block = latents_out.at[:, 0, 0, sx]
            if sx:
                yield
                wires.arrived(block, x_ports[sx], "x")
            if sx + 1 < nx:
                wires.push(block, latents_out.at[:, 0, 0, sx + 1], x_ports[sx + 1], "x")
            if ny > 1:
                wires.push(block, latents_out.at[:, 0, 1, sx], yx_ports[1][sx], "y")
            wires.push(block, latents_out.at[:, 1, 0, sx], cx_ports[0][sx], "core")
        for sy in range(1, ny):
            for sx in range(nx):
                yield
                block = latents_out.at[:, 0, sy, sx]
                wires.arrived(block, yx_ports[sy][sx], "y")
                if sy + 1 < ny:
                    wires.push(block, latents_out.at[:, 0, sy + 1, sx], yx_ports[sy + 1][sx], "y")
                wires.push(block, latents_out.at[:, 1, sy, sx], cx_ports[sy][sx], "core")
        for sy in range(ny):
            for sx in range(nx):
                yield
                wires.arrived(latents_out.at[:, 1, sy, sx], cx_ports[sy][sx], "core")

    def group_chain(src, dst):
        gather = GroupGather(wires, src, dst)
        gather.start()
        load(src, dst.at[:, 0, 0])
        yield from gather.chain()

    def array_chain(src, dst, place, x_first):
        gather = BlockGather(wires, src, dst, place, x_first)
        load(src, gather.at(0, 0))
        yield from gather.chain()

    first = main()
    next(first)
    others = [
        array_chain(w_query, query_out, rows_of(w_query.shape[0]), False),
        array_chain(w_expand, expand_out, rows_of(w_expand.shape[0]), True),
        array_chain(w_output, output_out, columns_of(w_output.shape[1]), False),
        line_chain(routes, routes_out),
        group_chain(tokens, tokens_out),
        group_chain(grads, grads_out),
        line_chain(grads, line_out),
    ]
    weave(first, others, 1)
    wires.drain()
    for copy in used:
        if id(copy) not in waited:
            copy.wait()


def start(tokens, grads, cosine, sine, gains, small, routes, weights):
    nz, nx, ny, nc = (lax.axis_size(a) for a in AXES)
    nb, nu = nz * nx, ny * nc
    seqs, local_len, features = tokens.shape
    shape = jax.ShapeDtypeStruct

    def whole(w, dim):
        size = list(w.shape)
        size[dim] *= nb
        return shape(tuple(size), w.dtype)

    grouped = (seqs, ny, nc, local_len, features)
    outs = [
        shape((nb,) + gains.shape, wide),
        shape((nb,) + small.shape, narrow),
        *[whole(w, d) for w, d in zip(weights, (0, 0, 1))],
        shape(grouped, narrow),
        shape(grouped, narrow),
        shape((nz,) + grads.shape, narrow),
        shape((nz,) + routes.shape, routes.dtype),
        shape((seqs, nc, ny, nx, nz, local_len, KVR + NOPE), narrow),
        shape((seqs * local_len, features), narrow),
        shape((seqs * local_len, KVR + RD), wide),
    ]
    return pl.pallas_call(
        start_kernel,
        out_shape=outs,
        in_specs=[VMEM, ANY, VMEM, VMEM, VMEM, VMEM, VMEM] + [ANY] * 3,
        out_specs=[VMEM, VMEM] + [ANY] * 6 + [VMEM] + [ANY] + [VMEM, VMEM],
        scratch_shapes=[
            pltpu.VMEM((seqs, local_len, KVR + NOPE), narrow),
            pltpu.SemaphoreType.DMA((384,)),
            pltpu.SemaphoreType.DMA((384,)),
            pltpu.SemaphoreType.DMA((16,)),
        ],
        compiler_params=pltpu.CompilerParams(
            collective_id=0, has_side_effects=True, vmem_limit_bytes=40 * 1024 * 1024
        ),
        cost_estimate=costs(120),
    )(tokens, grads, cosine, sine, gains, small, routes, *weights)


def scores_of(query, keys, rope, scale):
    return (dot_nt(query[:, :NOPE], keys) + dot_nt(query[:, NOPE:], rope)) * scale


def attend_kernel(
    query, cosine, sine, keys, rope, query_pos, key_pos, query_out, attended, stats, head_lin,
    *, scale, sub,
):
    qk = NOPE + RD
    for head in range(query.shape[1] // qk):

        @pl.when(pl.program_id(1) == head)
        def _(head=head):
            head_lin[:, :qk] = query[:, head * qk : (head + 1) * qk]

    keys_ = keys[:, :NOPE]
    values = keys[:, NOPE:]

    @pl.loop(0, query.shape[0], step=sub)
    def _(first):
        span = pl.ds(pl.multiple_of(first, sub), sub)
        lin = head_lin[span, :]
        turned = rotate(lin[:, NOPE : NOPE + RD], cosine[span, :], sine[span, :])
        query_out[span, :NOPE] = lin[:, :NOPE].astype(narrow)
        query_out[span, NOPE:] = jnp.zeros((sub, NOPE), narrow)
        query_out[span, NOPE : NOPE + RD] = turned.astype(narrow)
        scores = scores_of(query_out[span, :], keys_, rope[0], scale)
        scores = jnp.where(key_pos[...] <= query_pos[span, :], scores, -jnp.inf)
        top = jnp.max(scores, axis=1, keepdims=True)
        raised = jnp.exp(scores - top)
        total = jnp.sum(raised, axis=1, keepdims=True)
        probability = (raised * (1.0 / total)).astype(narrow)
        attended[span, :] = dot(probability, values).astype(narrow)
        stats[0, 0, span, 0:1] = top
        stats[0, 0, span, 1:2] = top + jnp.log(total)


def attend_back_kernel(
    query, cosine, sine, keys, rope, query_pos, key_pos, stats, grads,
    query_grad, expand_grad, rope_grad, key_acc, *, scale, sub,
):
    keys_ = keys[:, :NOPE]
    values = keys[:, NOPE:]
    key_acc[...] = jnp.zeros(key_acc.shape, wide)

    @pl.loop(0, query.shape[0], step=sub)
    def _(first):
        span = pl.ds(pl.multiple_of(first, sub), sub)
        rows = query[span, :]
        scores = scores_of(rows, keys_, rope[0], scale)
        scores = jnp.where(key_pos[...] <= query_pos[span, :], scores, -jnp.inf)
        probability = jnp.exp(scores - stats[0, 0, span, 1:2])
        grad = grads[span, :]
        prob_grad = dot_nt(grad, values)
        weighted = probability * prob_grad
        delta = jnp.sum(weighted, axis=1, keepdims=True)
        score_grad = ((weighted - probability * delta) * scale).astype(narrow)
        back_plain = dot(score_grad, keys_).astype(narrow)
        back_turned = dot(score_grad, rope[0])[:, :RD].astype(narrow).astype(wide)
        turned = unrotate(back_turned, cosine[span, :], sine[span, :]).astype(narrow)
        head_grad = jnp.concatenate([back_plain, turned], axis=1)
        qk = NOPE + RD
        for head in range(query_grad.shape[1] // qk):

            @pl.when(pl.program_id(1) == head)
            def _(head=head):
                query_grad[span, head * qk : (head + 1) * qk] = head_grad

        key_acc[:, : 2 * NOPE] += dot_tn(score_grad, rows)
        key_acc[:, 2 * NOPE :] += dot_tn(probability.astype(narrow), grad)

    expand_grad[:, :NOPE] = key_acc[:, :NOPE].astype(narrow)
    expand_grad[:, NOPE:] = key_acc[:, 2 * NOPE :].astype(narrow)

    @pl.when(pl.program_id(1) == 0)
    def _():
        rope_grad[0] = key_acc[:, NOPE : 2 * NOPE]

    @pl.when(pl.program_id(1) > 0)
    def _():
        rope_grad[0] += key_acc[:, NOPE : 2 * NOPE]


def attention_specs(seqs, heads, reach, length):
    both = NOPE + VH
    return dict(
        query=pl.BlockSpec((reach, both), lambda s, h: (s, h)),
        heads=pl.BlockSpec((reach, heads * (NOPE + RD)), lambda s, h: (s, 0)),
        rope_grad=pl.BlockSpec((1, length, NOPE), lambda s, h: (s, 0, 0)),
        table=pl.BlockSpec((reach, RD // 2), lambda s, h: (0, 0)),
        keys=pl.BlockSpec((length, both), lambda s, h: (s, h)),
        rope=pl.BlockSpec((1, length, NOPE), lambda s, h: (s, 0, KVR // NOPE)),
        query_pos=pl.BlockSpec((reach, 1), lambda s, h: (0, 0)),
        key_pos=pl.BlockSpec((1, length), lambda s, h: (0, 0)),
        head=pl.BlockSpec((reach, VH), lambda s, h: (s, h)),
        stats=pl.BlockSpec((1, 1, reach, 2), lambda s, h: (s, h, 0, 0)),
    )


def attend(query_lin, cosine, sine, keys, rope, query_pos, key_pos, seqs, heads):
    reach, length = query_pos.shape[0], key_pos.shape[1]
    sub = min(reach, max(16, 256 * 2048 // length))
    sp = attention_specs(seqs, heads, reach, length)
    shape = jax.ShapeDtypeStruct
    return pl.pallas_call(
        functools.partial(attend_kernel, scale=(NOPE + RD) ** -0.5, sub=sub),
        grid=(seqs, heads),
        in_specs=[sp[k] for k in ("heads", "table", "table", "keys", "rope", "query_pos", "key_pos")],
        out_specs=[sp["query"], sp["head"], sp["stats"]],
        out_shape=[
            shape((seqs * reach, heads * 2 * NOPE), narrow),
            shape((seqs * reach, heads * VH), narrow),
            shape((seqs, heads, reach, 2), wide),
        ],
        scratch_shapes=[pltpu.VMEM((reach, 2 * NOPE), wide)],
        cost_estimate=costs(16),
        compiler_params=pltpu.CompilerParams(vmem_limit_bytes=61 * 1024 * 1024),
    )(query_lin, cosine, sine, keys, rope, query_pos, key_pos)


def attend_back(query, cosine, sine, keys, rope, query_pos, key_pos, stats, grads, seqs, heads):
    reach, length = query_pos.shape[0], key_pos.shape[1]
    sub = min(reach, max(16, 256 * 2048 // length))
    sp = attention_specs(seqs, heads, reach, length)
    shape = jax.ShapeDtypeStruct
    return pl.pallas_call(
        functools.partial(attend_back_kernel, scale=(NOPE + RD) ** -0.5, sub=sub),
        grid=(seqs, heads),
        in_specs=[
            sp[k]
            for k in (
                "query", "table", "table", "keys", "rope", "query_pos", "key_pos", "stats", "head",
            )
        ],
        out_specs=[sp["heads"], sp["keys"], sp["rope_grad"]],
        cost_estimate=costs(25),
        out_shape=[
            shape((seqs * reach, heads * (NOPE + RD)), narrow),
            shape(keys.shape, narrow),
            shape((seqs, length, NOPE), wide),
        ],
        scratch_shapes=[pltpu.VMEM((length, 2 * NOPE + VH), wide)],
        compiler_params=pltpu.CompilerParams(vmem_limit_bytes=61 * 1024 * 1024),
    )(query, cosine, sine, keys, rope, query_pos, key_pos, stats, grads)


def costs(us):
    return pl.CostEstimate(flops=int(us * 1e9), bytes_accessed=int(us * 1e6), transcendentals=0)


def add_into(target, *terms):
    lead, count = target.shape[:-2], target.shape[-2]
    step = 32 if count % 32 == 0 else 16 if count % 16 == 0 else count
    pieces = count // step
    total = pieces
    for size in lead:
        total *= size

    @pl.loop(0, total)
    def _(i):
        at = []
        rest = i // pieces
        for size in reversed(lead):
            at.insert(0, lax.rem(rest, size))
            rest = rest // size
        span = pl.ds(pl.multiple_of(lax.rem(i, pieces) * step, step), step)
        place = (*at, span, slice(None))
        target[place] = sum(term[place].astype(wide) for term in terms).astype(target.dtype)


class Queue:
    def __init__(self):
        self.items = []

    def add(self, place, thunk):
        self.items.append((place, len(self.items), thunk))
        self.items.sort(key=lambda item: item[:2])

    def go(self, count):
        for _, _, thunk in self.items[:count]:
            thunk()
        del self.items[:count]


class BlockScatter:
    def __init__(self, wires, loads, src, place, axes, acc, first, second, out):
        self.wires, self.loads, self.src, self.place, self.axes = wires, loads, src, place, axes
        self.acc, self.first, self.second, self.out = acc, first, second, out
        self.na, self.nb = (lax.axis_size(a) for a in axes)
        self.ports = {
            (a, b): wires.port() for b in range(self.nb) for a in range(self.na) if a or b
        }
        self.order = [*range(1, self.nb), 0]

    def mine(self, a, b):
        steps = dict(zip(self.axes, (a, b)))
        owner = behind("z", steps["z"]) * lax.axis_size("x") + behind("x", steps["x"])
        return self.place(self.src, owner)

    def slot(self, a, b):
        return self.acc.at[b, max(a - 1, 0)]

    def start(self, queue=None):
        self.loading, self.queue = {}, queue or Queue()
        for place, b in enumerate(self.order):
            self.queue.add(
                place,
                lambda b=b: self.wires.push(
                    self.mine(1, b), self.first.at[b, 0], self.ports[1, b], self.axes[0]
                ),
            )
        if queue is None:
            self.queue.go(self.nb)
        for b in self.order:
            for a in [*range(2, self.na), 0]:
                self.loading[a, b] = self.loads(self.mine(a, b), self.slot(a, b))

    def chain(self):
        wires, (axis_a, axis_b) = self.wires, self.axes
        for b in self.order:
            for a in [*range(2, self.na), 0]:
                came = self.first.at[b, (a or self.na) - 2]
                yield
                wires.arrived(came, self.ports[(a or self.na) - 1, b], axis_a)
                if not a:
                    self.queue.go(1)
                self.loading[a, b].wait()
                add_into(self.slot(a, b), self.slot(a, b), came)
                if a:
                    wires.push(self.slot(a, b), self.first.at[b, a - 1], self.ports[a, b], axis_a)
            if b >= 2:
                yield
                wires.arrived(self.second.at[b - 2], self.ports[0, b - 1], axis_b)
                add_into(self.slot(0, b), self.slot(0, b), self.second.at[b - 2])
            if b >= 1:
                wires.push(self.slot(0, b), self.second.at[b - 1], self.ports[0, b], axis_b)
        yield
        wires.arrived(self.second.at[self.nb - 2], self.ports[0, self.nb - 1], axis_b)
        add_into(self.out, self.slot(0, 0), self.second.at[self.nb - 2])


def scatter_scratch(shard, axes, dtype=narrow):
    na, nb = (lax.axis_size(a) for a in axes)
    return [
        pltpu.VMEM((nb, na - 1) + shard, dtype),
        pltpu.VMEM((nb, na - 1) + shard, dtype),
        pltpu.VMEM((nb - 1,) + shard, dtype),
    ]


class GroupGather:
    def __init__(self, wires, src, dst):
        self.wires, self.src, self.dst = wires, src, dst
        self.ny, self.nc = lax.axis_size("y"), lax.axis_size("core")
        self.ports = [wires.port() for _ in range(self.ny * self.nc)]

    def start(self):
        if self.ny > 1:
            self.wires.push(self.src, self.dst.at[:, 1, 0], self.ports[self.nc], "y")
        self.wires.push(self.src, self.dst.at[:, 0, 1], self.ports[1], "core")

    def chain(self):
        wires, dst, nc = self.wires, self.dst, self.nc
        for sy in range(1, self.ny):
            piece = dst.at[:, sy, 0]
            yield
            wires.arrived(piece, self.ports[sy * nc], "y")
            if sy + 1 < self.ny:
                wires.push(piece, dst.at[:, sy + 1, 0], self.ports[(sy + 1) * nc], "y")
            wires.push(piece, dst.at[:, sy, 1], self.ports[sy * nc + 1], "core")
        for sy in range(self.ny):
            yield
            wires.arrived(dst.at[:, sy, 1], self.ports[sy * nc + 1], "core")


def group_sum_chain(wires, src, own, other, came, load):
    ny = lax.axis_size("y")
    core_ports = [wires.port() for _ in range(ny)]
    y_ports = [wires.port() for _ in range(ny)]
    order = [*range(1, ny), 0]
    for sy in order:
        wires.push(src.at[:, sy, 1], other.at[:, sy], core_ports[sy], "core")
    loading = [load(src.at[:, sy, 0], own.at[:, sy]) for sy in range(ny)]
    for sy in order:
        yield
        wires.arrived(other.at[:, sy], core_ports[sy], "core")
        loading[sy].wait()
        add_into(own.at[:, sy], own.at[:, sy], other.at[:, sy])
        if ny > 1:
            last = (sy or ny) - 1
            if last:
                yield
                wires.arrived(came.at[:, last - 1], y_ports[last], "y")
                add_into(own.at[:, sy], own.at[:, sy], came.at[:, last - 1])
            if sy:
                wires.push(own.at[:, sy], came.at[:, sy - 1], y_ports[sy], "y")


def weave(main, others, share):
    others = list(others)
    running = True
    while running or others:
        if running:
            running = next(main, True) is None
        for _ in range(share if running else max(1, len(others))):
            if others:
                chain = others.pop(0)
                if next(chain, True) is None:
                    others.append(chain)


def finish_kernel(
    hidden_partial, latent_partial, tokens, residual_grad, small, hidden_t, mid_t, logit_grad,
    ffn_gain, gain_attn, gain_latent, latent_all, cosine, sine, residual, shared_sum, routed,
    *rest, modes,
):
    count = len(modes)
    partials, rest = rest[:count], rest[count:]
    tokens_grad, block_out, latent_w_out, gains_out, *rest = rest
    outs, rest = rest[:count], rest[count:]
    (
        hid_own, hid_other, hid_came, lat_own, lat_other, lat_came, lat_x, lat_z,
        own_lag, lag_group, wide_acc, lat_wgrad, gain_terms, routed_own, routed_came, *rest,
    ) = rest
    buffers, rest = rest[: 3 * count], rest[3 * count :]
    lw_buffers, g_buffers = rest[:3], rest[3:6]
    send, recv, local = rest[6:]
    nz, nx, ny, nc = (lax.axis_size(a) for a in AXES)
    nb, nu = nz * nx, ny * nc
    uly = lax.axis_index("y") * nc + lax.axis_index("core")
    seqs, local_len, features = tokens.shape
    rows = seqs * local_len
    greet(AXES)
    wires = Wires(send, recv)
    used = []

    def load(src, dst):
        copy = pltpu.make_async_copy(src, dst, local.at[len(used)])
        used.append(copy)
        copy.start()
        return copy

    def blocks_of(size, dim):
        return rows_of(size) if dim == 0 else columns_of(size)

    scatters = [
        BlockScatter(
            wires, load, partials[i], blocks_of(partials[i].shape[dim] // nb, dim), axes,
            *buffers[3 * i : 3 * i + 3], outs[i],
        )
        for i, (dim, axes) in enumerate(modes)
    ]

    def routed_chain():
        ports = [wires.port() for _ in range(nz)]
        loading = {s: load(routed.at[s], routed_own.at[s]) for s in [*range(1, nz), 0]}
        for s in [*range(1, nz), 0]:
            own = routed_own.at[s]
            last = (s or nz) - 1
            yield
            loading[s].wait()
            if last:
                wires.arrived(routed_came.at[last - 1], ports[last], "z")
                add_into(own, own, routed_came.at[last - 1])
            if s:
                wires.push(own, routed_came.at[s - 1], ports[s], "z")

    def output_chain():
        yield from routed_chain()
        total = residual[...] + shared_sum[...].astype(wide).reshape(rows, features)
        total = total + routed_own[0].astype(wide)
        block_out[...] = total.astype(narrow).reshape(tokens.shape)

    def latent_chain():
        c_ports = [[wires.port() for _ in range(nx)] for _ in range(ny)]
        y_ports = [[wires.port() for _ in range(nx)] for _ in range(ny)]
        x_ports = [wires.port() for _ in range(nx)]
        z_ports = [wires.port() for _ in range(nz)]
        order_y, order_x = [*range(1, ny), 0], [*range(1, nx), 0]
        blocks = [(sy, sx) for sy in order_y for sx in order_x]
        loading = []

        def load_block():
            number = len(loading)
            if number < len(blocks):
                sy, sx = blocks[number]
                loading.append(load(latent_partial.at[:, 0, sy, sx], lat_own.at[number % 2]))

        for sy, sx in blocks:
            wires.push(
                latent_partial.at[:, 1, sy, sx], lat_other.at[:, sy, sx], c_ports[sy][sx], "core"
            )
        load_block()
        load_block()
        yield
        for sy in order_y:
            for sx in order_x:
                own = lat_other.at[:, sy, sx]
                number = blocks.index((sy, sx))
                yield
                wires.arrived(own, c_ports[sy][sx], "core")
                loading[number].wait()
                add_into(own, own, lat_own.at[number % 2])
                load_block()
                last = (sy or ny) - 1
                if last:
                    yield
                    wires.arrived(lat_came.at[:, last - 1, sx], y_ports[last][sx], "y")
                    add_into(own, own, lat_came.at[:, last - 1, sx])
                if sy:
                    wires.push(own, lat_came.at[:, sy - 1, sx], y_ports[sy][sx], "y")
                    continue
                last = (sx or nx) - 1
                if last:
                    yield
                    wires.arrived(lat_x.at[:, last - 1], x_ports[last], "x")
                    add_into(own, own, lat_x.at[:, last - 1])
                if sx:
                    wires.push(own, lat_x.at[:, sx - 1], x_ports[sx], "x")
        for sz in [*range(1, nz), 0]:
            own = lat_other.at[:, 0, 0, sz]
            last = (sz or nz) - 1
            if last:
                yield
                wires.arrived(lat_z.at[:, last - 1], z_ports[last], "z")
                add_into(own, own, lat_z.at[:, last - 1])
            if sz:
                wires.push(own, lat_z.at[:, sz - 1], z_ports[sz], "z")

    def main():
        hidden = group_sum_chain(wires, hidden_partial, hid_own, hid_other, hid_came, load)
        latent = latent_chain()
        next(latent)
        next(hidden)
        for s in scatters:
            s.start(queue)
        queue.go(3)
        yield
        for _ in hidden:
            yield
        for _ in latent:
            yield
        width = KVR + RD
        lat = lat_other[:, 0, 0, 0].astype(wide).reshape(rows, KVR + NOPE)[:, :width]
        latent_grad = lat[:, :KVR]
        _, normed, inverse = norm_rows(latent_all[:, :KVR], gain_latent[...])
        lat_in = norm_input_back(latent_grad, normed, inverse, gain_latent[...])
        turned = unrotate(lat[:, KVR:], cosine[...], sine[...])
        own_lag[:, :, KVR:] = jnp.zeros((seqs, local_len, own_lag.shape[-1] - KVR), narrow)
        own_lag[:, :, :KVR] = lat_in.astype(narrow).reshape(seqs, local_len, KVR)
        own_lag[:, :, KVR:width] = turned.astype(narrow).reshape(seqs, local_len, RD)
        wide_acc[...] = dot_nt(own_lag[...].reshape(rows, own_lag.shape[-1]), small[...])
        own_lag[:, :, width:] = logit_grad[...].reshape(seqs, local_len, EXPERTS)
        lag_gather = GroupGather(wires, own_lag, lag_group)
        lag_gather.start()
        own_copy = load(own_lag, lag_group.at[:, 0, 0])
        x = tokens[...].astype(wide).reshape(rows, features)
        _, normed_in, inverse_in = norm_rows(x, gain_attn[...])
        hidden_grad = wide_acc[...] + hid_own[:, 0].astype(wide).reshape(rows, features)
        wide_acc[...] = residual_grad[...] + norm_input_back(
            hidden_grad, normed_in, inverse_in, gain_attn[...]
        )
        attn_gain = jnp.sum(hidden_grad * normed_in, axis=0, keepdims=True)
        latent_gain = jnp.sum(latent_grad * normed, axis=0, keepdims=True)
        tokens_grad[...] = wide_acc[...].astype(narrow).reshape(tokens.shape)
        shard = features // nb
        gain_terms[...] = jnp.zeros(gain_terms.shape, wide)
        for b in range(nb):
            gain_terms[b, 0:1, :shard] = attn_gain[:, b * shard : (b + 1) * shard]
            gain_terms[b, 0:1, shard:] = latent_gain
            gain_terms[b, 1:2, :shard] = ffn_gain[:, b * shard : (b + 1) * shard]
        gain_sum = BlockScatter(
            wires, load, gain_terms, lambda ref, owner: ref.at[owner], ("x", "z"), *g_buffers,
            gains_out.at[uly],
        )
        gain_sum.start()
        for _ in lag_gather.chain():
            yield
        own_copy.wait()
        lags = lag_group[...].reshape(nu * rows, own_lag.shape[-1])
        terms = dot(hidden_t[...], lags).astype(narrow)
        lat_wgrad[...] = terms.reshape(lat_wgrad.shape)
        terms = dot(mid_t[...], lags)[:, width:].astype(narrow)
        lat_wgrad[:, :, width:] = terms.reshape(lat_wgrad.shape[:2] + (EXPERTS,))
        w_sum = BlockScatter(
            wires, load, lat_wgrad, lambda ref, owner: ref.at[owner], ("x", "z"), *lw_buffers,
            latent_w_out.at[uly],
        )
        w_sum.start()
        chains = [gain_sum.chain(), w_sum.chain()]
        while chains:
            chain = chains.pop(0)
            if next(chain, True) is None:
                chains.append(chain)
                yield
        outs_ = (latent_w_out, gains_out)
        y_ports = [[wires.port() for _ in range(ny)] for _ in outs_]
        c_ports = [[wires.port() for _ in range(ny)] for _ in outs_]
        member = lambda sy, sc: behind("y", sy) * nc + behind("core", sc)
        for ref, yp, cp in zip(outs_, y_ports, c_ports):
            here = ref.at[uly]
            if ny > 1:
                wires.push(here, here, yp[1], "y")
            wires.push(here, here, cp[0], "core")
        for sy in range(1, ny):
            for ref, yp, cp in zip(outs_, y_ports, c_ports):
                piece = ref.at[member(sy, 0)]
                yield
                wires.arrived(piece, yp[sy], "y")
                if sy + 1 < ny:
                    wires.push(piece, piece, yp[sy + 1], "y")
                wires.push(piece, piece, cp[sy], "core")
        for sy in range(ny):
            for ref, cp in zip(outs_, c_ports):
                yield
                wires.arrived(ref.at[member(sy, 1)], cp[sy], "core")

    queue = Queue()
    weave(main(), [s.chain() for s in scatters] + [output_chain()], 1)
    wires.drain()


def finish(
    hidden_partial, latent_partial, tokens, residual_grad, small, hidden_t, mid_t, logit_grad,
    ffn_gain, gain_attn, gain_latent, latent_all, cosine, sine, residual, shared_sum, routed,
    partials, modes,
):
    nz, nx, ny, nc = (lax.axis_size(a) for a in AXES)
    nb, nu = nz * nx, ny * nc
    seqs, local_len, features = tokens.shape
    rows = seqs * local_len
    shape = jax.ShapeDtypeStruct
    shards = []
    for p, (dim, _) in zip(partials, modes):
        size = list(p.shape)
        size[dim] //= nb
        shards.append(tuple(size))
    width, shard = KVR + RD, features // nb
    padded = small.shape[-1]
    latents = (seqs, ny, nx, nz, local_len, KVR + NOPE)
    few = lambda n: max(n - 1, 1)
    scratch = [
        pltpu.VMEM((seqs, ny, local_len, features), narrow),
        pltpu.VMEM((seqs, ny, local_len, features), narrow),
        pltpu.VMEM((seqs, few(ny), local_len, features), narrow),
        pltpu.VMEM((2, seqs, nz, local_len, KVR + NOPE), narrow),
        pltpu.VMEM(latents, narrow),
        pltpu.VMEM((seqs, few(ny), nx, nz, local_len, KVR + NOPE), narrow),
        pltpu.VMEM((seqs, few(nx), nz, local_len, KVR + NOPE), narrow),
        pltpu.VMEM((seqs, few(nz), local_len, KVR + NOPE), narrow),
        pltpu.VMEM((seqs, local_len, padded), narrow),
        pltpu.VMEM((seqs, ny, nc, local_len, padded), narrow),
        pltpu.VMEM((rows, features), wide),
        pltpu.VMEM((nb, shard // nu, padded), narrow),
        pltpu.VMEM((nb, 8, shard + KVR), wide),
        pltpu.VMEM((nz, rows, features), narrow),
        pltpu.VMEM((few(nz), rows, features), narrow),
    ]
    for size, (_, axes) in zip(shards, modes):
        scratch += scatter_scratch(size, axes)
    scratch += scatter_scratch((shard // nu, padded), ("x", "z"))
    scratch += scatter_scratch((8, shard + KVR), ("x", "z"), wide)
    scratch += [
        pltpu.SemaphoreType.DMA((256,)),
        pltpu.SemaphoreType.DMA((256,)),
        pltpu.SemaphoreType.DMA((256,)),
    ]
    return pl.pallas_call(
        functools.partial(finish_kernel, modes=modes),
        out_shape=[
            shape(tokens.shape, narrow),
            shape(tokens.shape, narrow),
            shape((nu, shard // nu, padded), wide),
            shape((nu, 8, shard + KVR), wide),
            *[shape(size, wide) for size in shards],
        ],
        in_specs=[ANY, ANY] + [VMEM] * 14 + [ANY] * (1 + len(partials)),
        out_specs=[VMEM] * (4 + len(partials)),
        scratch_shapes=scratch,
        compiler_params=pltpu.CompilerParams(
            collective_id=1, has_side_effects=True, vmem_limit_bytes=62 * 1024 * 1024
        ),
        cost_estimate=costs(190),
    )(
        hidden_partial, latent_partial, tokens, residual_grad, small, hidden_t, mid_t, logit_grad,
        ffn_gain, gain_attn, gain_latent, latent_all, cosine, sine, residual, shared_sum, routed,
        *partials,
    )


class Layer:
    def __init__(self):
        self.sizes = [lax.axis_size(a) for a in AXES[1:]]
        self.count = self.sizes[0] * self.sizes[1] * self.sizes[2]

    def offsets(self, k):
        _, ny, nc = self.sizes
        return k // (ny * nc), k // nc % ny, k % nc

    def device(self, k, sign=1):
        return {
            axis: lax.rem(lax.axis_index(axis) + (sign * d) % n, n)
            for axis, d, n in zip(AXES[1:], self.offsets(k), self.sizes)
        }

    def number(self, k, sign=1):
        where = self.device(k, sign)
        return (where["x"] * self.sizes[1] + where["y"]) * self.sizes[2] + where["core"]

    def greet(self):
        barrier = pltpu.get_barrier_semaphore()
        for k in range(1, self.count):
            pl.semaphore_signal(barrier, inc=1, device_id=self.device(k), device_id_type=MESH)
        pl.semaphore_signal(
            barrier, inc=1, device_id={"z": behind("z", 1)}, device_id_type=MESH
        )
        pl.semaphore_wait(barrier, self.count)

    def push(self, wires, src, dst, port, k):
        copy = pltpu.make_async_remote_copy(
            src_ref=src,
            dst_ref=dst,
            send_sem=wires.send.at[port],
            recv_sem=wires.recv.at[port],
            device_id=self.device(k),
            device_id_type=MESH,
        )
        copy.start()
        wires.sent.append(copy)


def dispatch_kernel(
    partial, tokens, gain, router, member, picks, top, *rest, plan,
):
    count = len(plan)
    shards, rest = rest[:count], rest[count:]
    residual_out, gates_out, hidden_out, group_out, rows_out, tops_out, *rest = rest
    wholes, rest = rest[:count], rest[count:]
    own, other, came, hidden, line, outgoing, send, recv, local = rest
    nz, nx = lax.axis_size("z"), lax.axis_size("x")
    seqs, local_len, features = tokens.shape
    rows = seqs * local_len
    layer = Layer()
    layer.greet()
    wires = Wires(send, recv)
    used, waited = [], set()

    def load(src, dst):
        copy = pltpu.make_async_copy(src, dst, local.at[len(used)])
        used.append(copy)
        copy.start()
        return copy

    def main():
        for _ in group_sum_chain(wires, partial, own, other, came, load):
            yield
        waited.update(id(copy) for copy in used[: own.shape[1]])
        residual = tokens[...].astype(wide).reshape(rows, features)
        residual = residual + own[:, 0].astype(wide).reshape(rows, features)
        residual_out[...] = residual
        normed = norm_rows(residual, gain[...])[0].astype(narrow)
        hidden_out[...] = normed
        hidden[...] = normed.reshape(tokens.shape)
        line[0, :, :features] = normed
        logits = jnp.where(member[...] > 0, dot(normed, router[...]), -jnp.inf)
        raised = jnp.exp(logits - jnp.max(logits, axis=1, keepdims=True))
        gates = raised / jnp.sum(raised, axis=1, keepdims=True)
        gates_out[...] = gates
        high = gates.astype(narrow).astype(wide)
        line[0, :, features:] = jnp.concatenate([high, gates - high], axis=1).astype(narrow)
        z_ports = [wires.port() for _ in range(nz)]
        wires.push(line.at[0], line.at[1], z_ports[1], "z")
        gather = GroupGather(wires, hidden, group_out)
        gather.start()
        load(hidden, group_out.at[:, 0, 0])
        ports = [[wires.port() for _ in range(layer.count)] for _ in range(nz)]
        me = layer.number(0)
        chain = gather.chain()
        for s in range(nz):
            if s:
                yield
                wires.arrived(line.at[s], z_ports[s], "z")
                if s + 1 < nz:
                    wires.push(line.at[s], line.at[s + 1], z_ports[s + 1], "z")
            outgoing[s] = dot_tn(picks[s], line[s]).astype(narrow).reshape(outgoing.shape[1:])
            for k in range(1, layer.count):
                target = layer.number(k)
                layer.push(wires, outgoing.at[s, target], rows_out.at[s, me], ports[s][k], k)
            load(outgoing.at[s, me], rows_out.at[s, me])
            next(chain, None)
        for _ in chain:
            pass
        for s in range(nz):
            yield
            for k in range(1, layer.count):
                wires.arrived(rows_out.at[s, layer.number(k, -1)], ports[s][k], "z")

    def tops():
        z_ports = [wires.port() for _ in range(nz)]
        x_ports = [wires.port() for _ in range(nx)]
        mine = load(top, tops_out.at[0, 0])
        waited.add(id(mine))
        wires.push(top, tops_out.at[0, 1], z_ports[1], "z")
        for s in range(1, nz):
            yield
            wires.arrived(tops_out.at[0, s], z_ports[s], "z")
            if s + 1 < nz:
                wires.push(tops_out.at[0, s], tops_out.at[0, s + 1], z_ports[s + 1], "z")
        mine.wait()
        wires.push(tops_out.at[0], tops_out.at[1], x_ports[1], "x")
        for s in range(1, nx):
            yield
            wires.arrived(tops_out.at[s], x_ports[s], "x")
            if s + 1 < nx:
                wires.push(tops_out.at[s], tops_out.at[s + 1], x_ports[s + 1], "x")

    def array_chain(src, dst, dim, x_first):
        place = (rows_of if dim == 0 else columns_of)(src.shape[dim])
        gather = BlockGather(wires, src, dst, place, x_first)
        load(src, gather.at(0, 0))
        yield from gather.chain()

    first = main()
    next(first)
    others = [array_chain(a, b, *mode) for a, b, mode in zip(shards, wholes, plan)]
    weave(first, others + [tops()], 1)
    for copy in used:
        if id(copy) not in waited:
            copy.wait()
    wires.drain()


def whole_array(w, dim):
    size = list(w.shape)
    size[dim] *= lax.axis_size("z") * lax.axis_size("x")
    return jax.ShapeDtypeStruct(tuple(size), w.dtype)


def dispatch(partial, tokens, gain, router, member, picks, top, units, shards, plan):
    nz, nx, ny, nc = (lax.axis_size(a) for a in AXES)
    seqs, local_len, features = tokens.shape
    rows = seqs * local_len
    layer = nx * ny * nc
    shape = jax.ShapeDtypeStruct
    extended = features + 2 * EXPERTS
    part = pltpu.VMEM((seqs, ny, local_len, features), narrow)
    return pl.pallas_call(
        functools.partial(dispatch_kernel, plan=plan),
        out_shape=[
            shape((rows, features), wide),
            shape((rows, EXPERTS), wide),
            shape((rows, features), narrow),
            shape((seqs, ny, nc, local_len, features), narrow),
            shape((nz, layer, units, SLOTS, extended), narrow),
            shape((nx, nz) + top.shape, wide),
            *[whole_array(w, dim) for w, (dim, _) in zip(shards, plan)],
        ],
        in_specs=[ANY] + [VMEM] * 6 + [ANY] * len(shards),
        out_specs=[VMEM, VMEM, VMEM, ANY, ANY, VMEM] + [ANY] * len(shards),
        scratch_shapes=[
            part, part, part,
            pltpu.VMEM((seqs, local_len, features), narrow),
            pltpu.VMEM((nz, rows, extended), narrow),
            pltpu.VMEM((nz, layer, units, SLOTS, extended), narrow),
            pltpu.SemaphoreType.DMA((256,)),
            pltpu.SemaphoreType.DMA((256,)),
            pltpu.SemaphoreType.DMA((32,)),
        ],
        compiler_params=pltpu.CompilerParams(
            collective_id=2, has_side_effects=True, vmem_limit_bytes=48 * 1024 * 1024
        ),
        cost_estimate=costs(80),
    )(partial, tokens, gain, router, member, picks, top, *shards)


def return_kernel(
    returned, partial, shared_partial, residual, gates, router, gain, grads, picks, *rest, modes,
):
    count = len(modes)
    partials, rest = rest[:count], rest[count:]
    residual_grad_out, group_out, logit_out, gain_out, shared_out, *rest = rest
    outs, rest = rest[:count], rest[count:]
    own, other, came, sh_own, sh_other, sh_came, back, line, own_grad, *rest = rest
    buffers, rest = rest[: 3 * count], rest[3 * count :]
    send, recv, local = rest
    nz, nx = lax.axis_size("z"), lax.axis_size("x")
    seqs, local_len, features = grads.shape
    rows = seqs * local_len
    layer = Layer()
    layer.greet()
    wires = Wires(send, recv)
    used = []

    def load(src, dst):
        copy = pltpu.make_async_copy(src, dst, local.at[len(used)])
        used.append(copy)
        copy.start()
        return copy

    queue = Queue()
    scatters = [
        BlockScatter(
            wires, load, partials[i],
            (rows_of if dim == 0 else columns_of)(partials[i].shape[dim] // (nz * nx)), axes,
            *buffers[3 * i : 3 * i + 3], outs[i],
        )
        for i, (dim, axes) in enumerate(modes)
    ]

    def main():
        me = layer.number(0)
        ports = [[wires.port() for _ in range(layer.count)] for _ in range(nz)]
        z_ports = [wires.port() for _ in range(nz)]
        order = [*range(1, nz), 0]
        own_copies = {}
        for s in order:
            for k in range(1, layer.count):
                layer.push(
                    wires, returned.at[s, layer.number(k)], back.at[s, me], ports[s][k], k
                )
            own_copies[s] = load(returned.at[s, me], back.at[s, me])
        shared = group_sum_chain(wires, partial, own, other, came, load)
        next(shared)
        yield
        extended = back.shape[-1]
        total = None
        for s in order:
            for k in range(1, layer.count):
                wires.arrived(back.at[s, layer.number(k, -1)], ports[s][k], "z")
            own_copies[s].wait()
            term = dot(picks[s], back[s].reshape(picks.shape[2], extended))
            if s != 1:
                last = (s or nz) - 1
                yield
                wires.arrived(line.at[1, last - 1], z_ports[last], "z")
                term = term + line[1, last - 1].astype(wide)
            if s:
                line[0, s - 1] = term.astype(narrow)
                wires.push(line.at[0, s - 1], line.at[1, s - 1], z_ports[s], "z")
            else:
                total = term
            next(shared, None)
        for _ in shared:
            pass
        lanes = total[:, features:]
        gate_grad = lanes[:, :EXPERTS] + lanes[:, EXPERTS:]
        weight = gates[...]
        logit_grad = (
            weight * (gate_grad - jnp.sum(weight * gate_grad, axis=1, keepdims=True))
        ).astype(narrow)
        logit_out[...] = logit_grad
        mid = total[:, :features] + own[:, 0].astype(wide).reshape(rows, features)
        mid = mid + dot_nt(logit_grad, router[...])
        _, normed, inverse = norm_rows(residual[...], gain[...])
        grad = grads[...].astype(wide).reshape(rows, features)
        grad = grad + norm_input_back(mid, normed, inverse, gain[...])
        residual_grad_out[...] = grad
        own_grad[...] = grad.astype(narrow).reshape(grads.shape)
        gather = GroupGather(wires, own_grad, group_out)
        gather.start()
        mine = load(own_grad, group_out.at[:, 0, 0])
        gain_out[...] = jnp.sum(mid * normed, axis=0, keepdims=True)
        yield from gather.chain()
        mine.wait()

    def shared_sum():
        yield from group_sum_chain(wires, shared_partial, sh_own, sh_other, sh_came, load)
        shared_out[...] = sh_own[:, 0]

    first = main()
    next(first)
    for s in scatters:
        s.start(queue)
    queue.go(2)
    weave(first, [s.chain() for s in scatters] + [shared_sum()], 1)
    wires.drain()


def come_back(
    returned, partial, shared_partial, residual, gates, router, gain, grads, picks, partials, modes
):
    nz, nx, ny, nc = (lax.axis_size(a) for a in AXES)
    seqs, local_len, features = grads.shape
    rows = seqs * local_len
    shape = jax.ShapeDtypeStruct
    extended = returned.shape[-1]
    part = pltpu.VMEM((seqs, ny, local_len, features), narrow)
    shards = []
    for p, (dim, _) in zip(partials, modes):
        size = list(p.shape)
        size[dim] //= nz * nx
        shards.append(tuple(size))
    scratch = [
        part, part, part, part, part, part,
        pltpu.VMEM(returned.shape, narrow),
        pltpu.VMEM((2, nz - 1, rows, extended), narrow),
        pltpu.VMEM((seqs, local_len, features), narrow),
    ]
    for size, (_, axes) in zip(shards, modes):
        scratch += scatter_scratch(size, axes)
    scratch += [
        pltpu.SemaphoreType.DMA((256,)),
        pltpu.SemaphoreType.DMA((256,)),
        pltpu.SemaphoreType.DMA((96,)),
    ]
    return pl.pallas_call(
        functools.partial(return_kernel, modes=modes),
        out_shape=[
            shape((rows, features), wide),
            shape((seqs, ny, nc, local_len, features), narrow),
            shape((rows, EXPERTS), narrow),
            shape((1, features), wide),
            shape(grads.shape, narrow),
            *[shape(size, wide) for size in shards],
        ],
        in_specs=[ANY, ANY, ANY] + [VMEM] * 6 + [ANY] * len(partials),
        out_specs=[VMEM, ANY, VMEM, VMEM, VMEM] + [VMEM] * len(partials),
        scratch_shapes=scratch,
        compiler_params=pltpu.CompilerParams(
            collective_id=3, has_side_effects=True, vmem_limit_bytes=56 * 1024 * 1024
        ),
        cost_estimate=costs(100),
    )(returned, partial, shared_partial, residual, gates, router, gain, grads, picks, *partials)


def expert_kernel(
    rows_in, grads_in, wg, wu, wd, *rest, split, plan,
):
    count = len(plan)
    shards, rest = rest[:count], rest[count:]
    returned, outputs, gated, lin_gate, lin_up, *rest = rest
    wholes, rest = rest[:count], rest[count:]
    (
        rows, grads, bg, bu, bd, act, gated_buf, gate_buf, up_buf, dots,
        back_stage, out_stage, send, recv, local, turn,
    ) = rest
    nz, nx, ny, nc = (lax.axis_size(a) for a in AXES)
    nb = nz * nx
    layer = nx * ny * nc
    units, features, hidden = wg.shape
    first_unit = (
        (lax.axis_index("z") * nx + lax.axis_index("x")) * ny + lax.axis_index("y")
    ) * nc + lax.axis_index("core")
    first_unit = first_unit * units
    per = min(nz, max(1, 512 // (layer * SLOTS)))
    block = per * layer * SLOTS
    blocks = nz // per
    wires = Wires(send, recv)
    greet(("z", "x"))
    used = []

    def load(src, dst):
        copy = pltpu.make_async_copy(src, dst, local.at[len(used)])
        used.append(copy)
        copy.start()
        return copy

    gathers = [
        BlockGather(
            wires, src, dst, (rows_of if dim == 0 else columns_of)(src.shape[dim]), x_first
        )
        for src, dst, (dim, x_first) in zip(shards, wholes, plan)
    ]

    def transfers():
        for g in gathers:
            g.forward(0, 0)
        yield
        plans = [g.rounds() for g in gathers]
        for step in range(max(len(p) for p in plans)):
            for g, p in zip(gathers, plans):
                for slot in p[step] if step < len(p) else []:
                    g.take(*slot)
                    yield

    moving = transfers()
    next(moving, None)

    def tick():
        next(moving, None)

    def fetch(a):
        slot = a % rows.shape[0]
        return [
            load(rows_in.at[:, :, a], rows.at[slot]),
            load(wg.at[a], bg),
            load(wu.at[a], bu),
            load(grads_in.at[:, :, a], grads.at[slot]),
            load(wd.at[a], bd),
        ]

    fetched = fetch(0)
    kept = [load(g.src, g.at(0, 0)) for g in gathers]

    def pump(low, high, body, copies):
        @pl.loop(low, high)
        def _(i):
            slot = lax.rem(i, 2)

            @pl.when(i >= 2)
            def _():
                for copy in copies(i - 2, slot):
                    copy.wait()

            body(i, slot)
            for copy in copies(i, slot):
                copy.start()

    def settle(total, copies):
        for i in range(max(0, total - 2), total):
            for copy in copies(i, i % 2):
                copy.wait()

    saved, extra_copy = [], None
    for a in range(units):
        slot_a = a % rows.shape[0]
        expert = (first_unit + a) // split
        for copy in fetched[:3]:
            copy.wait()
        waiting = fetched[3:]

        def weights_of(b):
            extra = rows[slot_a, pl.ds(b * per, per), :, :, features:].astype(wide)
            extra = extra.reshape(block, 2 * EXPERTS)
            lane = lax.broadcasted_iota(jnp.int32, extra.shape, 1)
            mine = (lane == expert) | (lane == expert + EXPERTS)
            return jnp.sum(jnp.where(mine, extra, 0.0), axis=1, keepdims=True)

        def row_block(ref, b, columns):
            return ref[slot_a, pl.ds(b * per, per), :, :, columns].reshape(block, -1)

        for copy in waiting:
            copy.wait()

        def forward(b, cols):
            span = pl.ds(pl.multiple_of(b * block, block), block)
            picked = row_block(rows, b, slice(0, features))
            lin = dot(picked, bg[:, cols])
            up = dot(picked, bu[:, cols])
            grad = dot_nt(row_block(grads, b, slice(None)), bd[cols, :]) * weights_of(b)
            s = jax.nn.sigmoid(lin)
            silu = lin * s
            value = (silu * up).astype(narrow)
            act[span, cols] = value
            gated_buf[span, cols] = (value.astype(wide) * weights_of(b)).astype(narrow)
            gate_buf[span, cols] = (grad * up * (s * (1.0 + lin * (1.0 - s)))).astype(narrow)
            up_buf[span, cols] = (grad * silu).astype(narrow)

        full = hidden // 256
        for copy in saved:
            copy.wait()

        @pl.loop(0, blocks)
        def _(b):
            @pl.loop(0, full)
            def _(i):
                forward(b, pl.ds(pl.multiple_of(i * 256, 256), 256))

            if hidden % 256:
                forward(b, pl.ds(full * 256, hidden % 256))

        saved = [
            load(src, dst.at[a])
            for src, dst in ((gated_buf, gated), (gate_buf, lin_gate), (up_buf, lin_up))
        ]
        tick()
        tick()
        dots[...] = jnp.zeros(dots.shape, wide)

        def spread(i):
            return pl.ds(pl.multiple_of(i * 256, 256), 256)

        def back_copies(i, slot):
            return [
                pltpu.make_async_copy(
                    back_stage.at[slot], returned.at[:, :, a, :, spread(i)], turn.at[0, slot]
                ),
                pltpu.make_async_copy(
                    out_stage.at[slot], outputs.at[:, :, a, :, spread(i)], turn.at[1, slot]
                ),
            ]

        def backward(i, slot):
            @pl.loop(0, blocks)
            def _(b):
                span = pl.ds(pl.multiple_of(b * block, block), block)
                cols = spread(i)
                out = dot(act[span, :], bd[:, cols])
                dots[span, :] += jnp.sum(
                    out * row_block(grads, b, cols).astype(wide), axis=1, keepdims=True
                )
                shaped = (per, layer, SLOTS, 256)
                out_stage[slot, pl.ds(b * per, per)] = (
                    (out * weights_of(b)).astype(narrow).reshape(shaped)
                )
                inward = dot_nt(gate_buf[span, :], bg[cols, :]) + dot_nt(
                    up_buf[span, :], bu[cols, :]
                )
                back_stage[slot, pl.ds(b * per, per)] = inward.astype(narrow).reshape(shaped)

        chunks = features // 256
        for part in range(4):
            pump(part * chunks // 4, (part + 1) * chunks // 4, backward, back_copies)
            tick()
        settle(chunks, back_copies)

        @pl.loop(0, blocks)
        def _(b):
            span = pl.ds(pl.multiple_of(b * block, block), block)
            lane = lax.broadcasted_iota(jnp.int32, (block, 2 * EXPERTS), 1)
            value = dots[span, :]
            high = value.astype(narrow).astype(wide)
            lanes = jnp.where(lane == expert, high, 0.0)
            lanes = jnp.where(lane == expert + EXPERTS, value - high, lanes)
            rest_ = lanes.astype(narrow).reshape(per, layer, SLOTS, 2 * EXPERTS)
            back_stage[0, pl.ds(b * per, per), :, :, : 2 * EXPERTS] = rest_

        extra_copy = load(
            back_stage.at[0, :, :, :, : 2 * EXPERTS], returned.at[:, :, a, :, features:]
        )
        if a + 1 < units:
            fetched = fetch(a + 1)

        extra_copy.wait()
    for copy in saved:
        copy.wait()
    for _ in moving:
        pass
    for copy in kept:
        copy.wait()
    wires.drain()


def run_experts(rows_in, grads_in, wg, wu, wd, shards, plan, split):
    nz, nx, ny, nc = (lax.axis_size(a) for a in AXES)
    nb = nz * nx
    units, features, hidden = wg.shape
    layer = nx * ny * nc
    total = nz * layer * SLOTS
    shape = jax.ShapeDtypeStruct
    extended = rows_in.shape[-1]

    slots = min(units, 2)
    lines = (nz, layer, SLOTS)
    return pl.pallas_call(
        functools.partial(expert_kernel, split=split, plan=plan),
        out_shape=[
            shape(rows_in.shape, narrow),
            shape(grads_in.shape, narrow),
            *[shape((units, total, hidden), narrow)] * 3,
            *[whole_array(w, dim) for w, (dim, _) in zip(shards, plan)],
        ],
        in_specs=[ANY] * (5 + len(shards)),
        out_specs=[ANY] * (5 + len(shards)),
        scratch_shapes=[
            pltpu.VMEM((slots,) + lines + (extended,), narrow),
            pltpu.VMEM((slots,) + lines + (features,), narrow),
            pltpu.VMEM((features, hidden), narrow),
            pltpu.VMEM((features, hidden), narrow),
            pltpu.VMEM((hidden, features), narrow),
            pltpu.VMEM((total, hidden), narrow),
            pltpu.VMEM((total, hidden), narrow),
            pltpu.VMEM((total, hidden), narrow),
            pltpu.VMEM((total, hidden), narrow),
            pltpu.VMEM((total, 1), wide),
            pltpu.VMEM((2,) + lines + (256,), narrow),
            pltpu.VMEM((2,) + lines + (256,), narrow),
            pltpu.SemaphoreType.DMA((64,)),
            pltpu.SemaphoreType.DMA((64,)),
            pltpu.SemaphoreType.DMA((32,)),
            pltpu.SemaphoreType.DMA((4, 2)),
        ],
        compiler_params=pltpu.CompilerParams(
            collective_id=4, has_side_effects=True, vmem_limit_bytes=60 * 1024 * 1024
        ),
        cost_estimate=costs(80),
    )(rows_in, grads_in, wg, wu, wd, *shards)


def unit_grads_kernel(rows, grads, gated, lin_gate, lin_up, gate_out, up_out, down_out):
    picked = rows[...].reshape(gated.shape[1], rows.shape[-1])
    gate_out[0] = dot_tn(picked, lin_gate[0])
    up_out[0] = dot_tn(picked, lin_up[0])
    down_out[0] = dot_tn(gated[0], grads[...].reshape(gated.shape[1], grads.shape[-1]))


def unit_grads(rows, grads, gated, lin_gate, lin_up):
    nz, layer, units, _, features = grads.shape
    _, total, hidden = gated.shape
    step = 512 if total <= 512 else 128
    lines = (nz, layer, 1, SLOTS, step)
    shape = jax.ShapeDtypeStruct
    line_spec = pl.BlockSpec(lines, lambda a, i: (0, 0, a, 0, i))
    unit_spec = pl.BlockSpec((1, total, hidden), lambda a, i: (a, 0, 0))
    wide_spec = pl.BlockSpec((1, step, hidden), lambda a, i: (a, i, 0))
    return pl.pallas_call(
        unit_grads_kernel,
        grid=(units, features // step),
        in_specs=[line_spec, line_spec, unit_spec, unit_spec, unit_spec],
        out_specs=[wide_spec, wide_spec, pl.BlockSpec((1, hidden, step), lambda a, i: (a, 0, i))],
        out_shape=[
            shape((units, features, hidden), wide),
            shape((units, features, hidden), wide),
            shape((units, hidden, features), wide),
        ],
        cost_estimate=costs(35),
        compiler_params=pltpu.CompilerParams(vmem_limit_bytes=61 * 1024 * 1024),
    )(rows, grads, gated, lin_gate, lin_up)


def per_device(
    tokens, attn_gain, w_query, w_latent, latent_gain, w_expand, w_output, ffn_gain, w_router,
    w_shared_gate, w_shared_up, w_shared_down, w_gate, w_up, w_down, routes, clip_limit, out_grad,
):
    seqs, local_len, features = tokens.shape
    rows = seqs * local_len
    qk = NOPE + RD
    nz, nx, ny, nc = (lax.axis_size(a) for a in ("z", "x", "y", "core"))
    zi, xi, yi, ci = (lax.axis_index(a) for a in ("z", "x", "y", "core"))
    nb, nu = nz * nx, ny * nc
    layer = nx * nu
    heads = H // nu
    group = nu * rows
    all_rows = nb * group
    upd = w_gate.shape[0]
    split = upd * nz * layer // EXPERTS
    scale = qk ** (-0.5)
    GROUP = ("y", "core")
    ALL = ("z", "x", "y", "core")
    LAYER = ("x", "y", "core")

    def scatter_blk(whole, dim):
        size = whole.shape[dim] // nb
        blocks = []
        for sz in range(nz):
            for sx in range(nx):
                owner = ((zi + nz - sz) % nz) * nx + (xi + nx - sx) % nx
                blocks.append(lax.dynamic_slice_in_dim(whole, owner * size, size, dim))
        return tree_sum(blocks, ("z", "x"))

    def group_gather(value):
        return jnp.concatenate(
            [p.reshape(seqs, local_len, -1) for p in flat_ring(value, GROUP)], axis=1
        ).reshape(group, -1)

    def group_scatter(value):
        blocks = value.reshape(seqs, nu, local_len, -1)
        return tree_sum([blocks[:, i].reshape(rows, -1) for i in range(nu)], GROUP)

    def group_sum(value):
        for axis in GROUP:
            items = ring(value, axis)
            value = sum(item.astype(wide) for item in items)
        return value

    def device_positions(blk, u):
        return (blk * nu + u) * local_len + jnp.arange(local_len, dtype=jnp.int32)

    local_pos = device_positions(zi * nx + xi, yi * nc + ci)
    group_pos = jnp.concatenate(
        [
            device_positions(zi * nx + xi, (yi + ny - sy) % ny * nc + (ci + nc - sc) % nc)
            for sy in range(ny)
            for sc in range(nc)
        ]
    )
    key_pos = jnp.concatenate(
        [
            device_positions(
                (zi + nz - sz) % nz * nx + (xi + nx - sx) % nx,
                (yi + ny - sy) % ny * nc + (ci + nc - sc) % nc,
            )
            for sc in range(nc)
            for sy in range(ny)
            for sx in range(nx)
            for sz in range(nz)
        ]
    )

    shard = attn_gain.shape[0]
    lat_len = latent_gain.shape[0]
    gains = jnp.concatenate(
        [
            jnp.pad(jnp.stack([attn_gain, ffn_gain]).astype(wide), ((0, 0), (0, KVR - shard))),
            lax.dynamic_update_slice(
                jnp.zeros((1, KVR), wide),
                latent_gain.astype(wide)[None],
                (0, (zi * nx + xi) * lat_len),
            ),
            jnp.zeros((5, KVR), wide),
        ],
        axis=0,
    )
    small = jnp.concatenate([w_latent, w_router], axis=1).reshape(nu, shard // nu, -1)
    route_rows = jnp.swapaxes(routes, 0, 1).reshape(rows, TOP)
    cos_local, sin_local = rotary_tables(jnp.tile(local_pos, seqs))
    (
        gains_all, small_all, query_w, expand_w, output_w,
        tokens_group, grad_group, grad_line, route_line, latents, hidden_local, latent_all,
    ) = start(
        tokens, out_grad, cos_local, sin_local, gains, small,
        jnp.pad(route_rows, ((0, 0), (0, 128 - TOP))),
        (w_query, w_expand, w_output),
    )
    tokens_local = tokens.reshape(rows, features)
    grad_narrow = out_grad.reshape(rows, features)
    small_whole = small_all.reshape(features, -1)
    latent_w = small_whole[:, : KVR + RD]
    router_w = small_whole[:, KVR + RD :]
    gain_attn = gains_all[:, 0, :shard].reshape(-1)
    gain_ffn = gains_all[:, 1, :shard].reshape(-1)
    gain_latent = jnp.sum(gains_all[:, 2], axis=0)
    inputs = tokens_local.astype(wide)
    _, normed_in, inverse_in = norm_rows(inputs, gain_attn)
    _, normed_lat, inverse_lat = norm_rows(latent_all[:, :KVR], gain_latent)
    length = all_rows // seqs
    latent_keys = latents.reshape(seqs, length, KVR + NOPE)
    latent_rows = latents.reshape(all_rows, KVR + NOPE)
    expand_w = jnp.pad(expand_w, ((0, NOPE), (0, 0)))
    tokens_group = tokens_group.reshape(group, features)
    grad_group = grad_group.reshape(group, features)
    route_line = route_line[:, :, :TOP]

    member = jnp.any(
        route_line[..., None] == jnp.arange(EXPERTS, dtype=jnp.int32), axis=2
    )
    earlier = (
        jnp.arange(rows, dtype=jnp.int32)[None, :] < jnp.arange(rows, dtype=jnp.int32)[:, None]
    ).astype(narrow)
    rank = jnp.einsum(
        "tq,zqe->zte", earlier, member.astype(narrow), preferred_element_type=wide
    ).astype(jnp.int32)
    here = EXPERTS // nz
    rank = jnp.where(member, rank, -1)
    rank_layer = lax.dynamic_slice_in_dim(rank, zi * here, here, 2)
    experts = [(d * upd + a) // split for d in range(layer) for a in range(upd)]
    chosen = jnp.stack([rank_layer[..., e] for e in experts], axis=-1)
    picks = (
        (chosen[..., None] == jnp.arange(SLOTS, dtype=jnp.int32))
        .astype(narrow)
        .reshape(nz, rows, layer * upd * SLOTS)
    )

    def swap_layer(values):
        return lax.all_to_all(values, LAYER, split_axis=1, concat_axis=1, tiled=True)

    grad_line = grad_line.reshape(nz, rows, features)
    grad_slots = swap_layer(
        jnp.einsum("ztk,ztf->zkf", picks, grad_line, preferred_element_type=narrow).reshape(
            nz, layer, upd, SLOTS, features
        )
    )

    hidden_group = norm_rows(tokens_group.astype(wide), gain_attn)[0].astype(narrow)
    reach = nu * local_len
    cos_group, sin_group = rotary_tables(group_pos)
    query_lin = dot(hidden_group, query_w)
    expanded = dot(latent_rows, expand_w, narrow)
    query_pos, keys_pos = group_pos[:, None], key_pos[None, :]
    query_rows, attended, stats = attend(
        query_lin, cos_group, sin_group, expanded, latent_keys, query_pos, keys_pos, seqs, heads
    )
    top = jnp.pad(jnp.max(stats[..., 0], axis=(0, 2))[None], ((0, 7), (0, 128 - heads)))
    own_member = member[0]
    split_group = (seqs, ny, nc, local_len, features)
    residual, gates, hidden_mid, hidden_mid_group, expert_slots, tops, gate_w = dispatch(
        dot(attended, output_w, narrow).reshape(split_group),
        tokens, gain_ffn[None], router_w, own_member.astype(wide), picks, top, upd,
        (w_shared_gate,), ((0, False),),
    )
    clip_value = clip_limit[0]
    clip_factor = clip_value / jnp.maximum(jnp.max(tops, axis=(0, 1))[0, :heads], clip_value)
    hidden_mid_group = hidden_mid_group.reshape(group, features)

    returned, outputs, gated, lin_gate, lin_up, up_w, down_w = run_experts(
        expert_slots, grad_slots, w_gate, w_up, w_down,
        (w_shared_up, w_shared_down), ((0, False), (1, False)), split,
    )

    shared_gate = dot(hidden_mid_group, gate_w)
    shared_up = dot(hidden_mid_group, up_w)
    shared_act = (jax.nn.silu(shared_gate) * shared_up).astype(narrow)
    shared_partial = dot(shared_act, down_w, narrow)
    shared_act_grad = dot_nt(grad_group, down_w)
    shared_gate_grad = (shared_act_grad * shared_up * silu_slope(shared_gate)).astype(narrow)
    shared_up_grad = (shared_act_grad * jax.nn.silu(shared_gate)).astype(narrow)
    mid_shared = dot_nt(shared_gate_grad, gate_w) + dot_nt(shared_up_grad, up_w)

    usual = ("x", "z")
    shared_gate_wgrad = dot_tn(hidden_mid_group, shared_gate_grad, narrow)
    shared_up_wgrad = dot_tn(hidden_mid_group, shared_up_grad, narrow)
    (
        residual_grad, attn_grad, logit_grad, ffn_gain_part, shared_sum,
        shared_gate_wgrad, shared_up_wgrad,
    ) = come_back(
        returned, mid_shared.astype(narrow).reshape(split_group),
        shared_partial.reshape(split_group), residual, gates,
        router_w, gain_ffn[None], out_grad, picks,
        (shared_gate_wgrad, shared_up_wgrad), ((0, usual), (0, usual)),
    )
    attn_grad = attn_grad.reshape(group, features)
    outputs, shared_act, attn_grad = lax.optimization_barrier((outputs, shared_act, attn_grad))
    outputs = swap_layer(outputs)
    gate_wgrad, up_wgrad, down_wgrad = unit_grads(expert_slots, grad_slots, gated, lin_gate, lin_up)
    shared_down_wgrad = dot_tn(shared_act, grad_group, narrow)
    attended_grad = dot_nt(attn_grad, output_w, narrow)
    output_wgrad = dot_tn(attended, attn_grad, narrow)

    query_lin_grad, expand_grad, rope_partial = attend_back(
        query_rows, cos_group, sin_group, expanded, latent_keys, query_pos, keys_pos, stats,
        attended_grad, seqs, heads,
    )
    hidden_partial = dot_nt(query_lin_grad, query_w, narrow)
    latent_partial = (
        dot_nt(expand_grad, expand_w).reshape(seqs, length, KVR + NOPE)
        + jnp.pad(rope_partial, ((0, 0), (0, 0), (KVR, 0)))
    ).astype(narrow)
    routed = jnp.einsum(
        "ztk,zkf->ztf", picks, outputs.reshape(nz, layer * upd * SLOTS, features),
        preferred_element_type=narrow,
    )
    query_wgrad = dot_tn(hidden_group, query_lin_grad, narrow)
    expand_wgrad = dot_tn(latent_rows, expand_grad, narrow)
    uly = yi * nc + ci

    def own_columns(values):
        return lax.dynamic_slice_in_dim(
            values.T.reshape(nb, nu, shard // nu, group), uly, 1, 1
        ).reshape(features // nu, group)

    (
        tokens_grad, block_out, latent_wgrad, gain_sums, query_wgrad, expand_wgrad, output_wgrad,
        shared_down_wgrad,
    ) = finish(
        hidden_partial.reshape(seqs, ny, nc, local_len, features),
        latent_partial.reshape(seqs, nc, ny, nx, nz, local_len, KVR + NOPE),
        tokens, residual_grad, small_whole, own_columns(hidden_group), own_columns(hidden_mid_group),
        logit_grad, ffn_gain_part, gain_attn[None], gain_latent[None],
        latent_all, cos_local, sin_local, residual,
        shared_sum, routed,
        (query_wgrad, expand_wgrad[:KVR], output_wgrad, shared_down_wgrad),
        ((0, usual), (0, ("z", "x")), (1, usual), (1, usual)),
    )
    width = KVR + RD
    small_wgrad = latent_wgrad.reshape(shard, -1)
    latent_wgrad, router_wgrad = small_wgrad[:, :width], small_wgrad[:, width:]
    ffn_gain_grad = jnp.sum(gain_sums[:, 1, :shard], axis=0)
    gain_sums = jnp.sum(gain_sums[:, 0], axis=0)
    attn_gain_grad = gain_sums[:shard]
    latent_gain_grad = lax.dynamic_slice_in_dim(
        gain_sums, shard + (zi * nx + xi) * lat_len, lat_len, 0
    )
    return (
        block_out,
        tokens_grad,
        attn_gain_grad,
        query_wgrad,
        latent_wgrad,
        latent_gain_grad,
        expand_wgrad,
        output_wgrad,
        ffn_gain_grad,
        router_wgrad,
        shared_gate_wgrad,
        shared_up_wgrad,
        shared_down_wgrad,
        gate_wgrad,
        up_wgrad,
        down_wgrad,
        clip_factor,
    )


def solution(mesh):
    blocks, group = mesh.shape["blk"], mesh.shape["ulysses"]
    chips = Mesh(
        mesh.devices.reshape(Z_SIZE, blocks // Z_SIZE, group // CORES, CORES),
        ("z", "x", "y", "core"),
    )
    blk, uly, every = ("z", "x"), ("y", "core"), ("z", "x", "y", "core")
    rows = P(None, every, None)
    unit = P(every, None, None)
    return jax.shard_map(
        per_device,
        mesh=chips,
        in_specs=(
            rows, P(blk), P(blk, uly), P(blk, None), P(blk), P(blk, uly), P(uly, blk), P(blk),
            P(blk, None), P(blk, uly), P(blk, uly), P(uly, blk), unit, unit, unit, unit, P(), rows,
        ),
        out_specs=(
            rows, rows, P(blk), P(blk, uly), P(blk, None), P(blk), P(blk, uly), P(uly, blk), P(blk),
            P(blk, None), P(blk, uly), P(blk, uly), P(uly, blk), unit, unit, unit, P(uly),
        ),
        check_vma=False,
    )
```

```python
import functools

import jax
import jax.numpy as jnp
from jax import lax
from jax.experimental import pallas as pl
from jax.experimental.pallas import tpu as pltpu
from jax.sharding import Mesh
from jax.sharding import PartitionSpec as P

H = 16
NOPE = 128
RD = 64
VH = 128
KVR = 512
EXPERTS = 64
TOP = 6
CAP = 14
SLOTS = 16
HEAD_START = 12
Z_SIZE = 4
CORES = 2

epsilon = 1e-06
rope_base = 10000.0
wide = jnp.float32
narrow = jnp.bfloat16


def dot(a, b, out=wide):
    return jnp.dot(a, b, preferred_element_type=out)


def dot_tn(a, b, out=wide):
    return lax.dot_general(a, b, (((0,), (0,)), ((), ())), preferred_element_type=out)


def dot_nt(a, b, out=wide):
    return lax.dot_general(a, b, (((1,), (1,)), ((), ())), preferred_element_type=out)


def norm_rows(values, gain):
    inverse = lax.rsqrt(jnp.mean(values * values, axis=-1, keepdims=True) + epsilon)
    normed = values * inverse
    return (normed * gain, normed, inverse)


def norm_input_back(grad_out, normed, inverse, gain):
    scaled = grad_out * gain
    return inverse * (scaled - normed * jnp.mean(scaled * normed, axis=-1, keepdims=True))


def rotary_tables(positions):
    half_width = RD // 2
    frequency = rope_base ** (-2.0 * jnp.arange(half_width).astype(wide) / RD)
    angles = positions.astype(wide)[:, None] * frequency[None, :]
    return (jnp.cos(angles), jnp.sin(angles))


def rotate(values, cosine, sine):
    half = RD // 2
    a, b = values[..., :half], values[..., half:]
    return jnp.concatenate([a * cosine - b * sine, b * cosine + a * sine], axis=-1)


def unrotate(values, cosine, sine):
    half = RD // 2
    a, b = values[..., :half], values[..., half:]
    return jnp.concatenate([a * cosine + b * sine, b * cosine - a * sine], axis=-1)


def silu_slope(values):
    s = jax.nn.sigmoid(values)
    return s * (1.0 + values * (1.0 - s))


def hop(value, axis):
    n = lax.axis_size(axis)
    return lax.ppermute(value, axis, [(i, (i + 1) % n) for i in range(n)])


def ring(value, axis):
    items = [value]
    for _ in range(lax.axis_size(axis) - 1):
        items.append(hop(items[-1], axis))
    return items


def ring_sum(blocks, axis):
    n = lax.axis_size(axis)
    if n == 1:
        return blocks[0].astype(wide)
    running = hop(blocks[1].astype(narrow), axis)
    for s in range(2, n):
        running = hop((running.astype(wide) + blocks[s].astype(wide)).astype(narrow), axis)
    return running.astype(wide) + blocks[0].astype(wide)


def flat_ring(value, axes):
    items = [value]
    for axis in axes:
        items = [piece for item in items for piece in ring(item, axis)]
    return items


def tree_sum(blocks, axes):
    for axis in reversed(axes):
        n = lax.axis_size(axis)
        blocks = [ring_sum(blocks[i : i + n], axis) for i in range(0, len(blocks), n)]
    return blocks[0]


ANY = pl.BlockSpec(memory_space=pl.ANY)
VMEM = pl.BlockSpec(memory_space=pltpu.VMEM)
MESH = pl.DeviceIdType.MESH
AXES = ("z", "x", "y", "core")


def behind(axis, steps):
    n = lax.axis_size(axis)
    return lax.rem(lax.axis_index(axis) + (n - steps), n)


def ahead(axis):
    n = lax.axis_size(axis)
    return lax.rem(lax.axis_index(axis) + 1, n)


def greet(axes):
    barrier = pltpu.get_barrier_semaphore()
    for axis in axes:
        pl.semaphore_signal(
            barrier, inc=1, device_id={axis: behind(axis, 1)}, device_id_type=MESH
        )
    pl.semaphore_wait(barrier, len(axes))


class Wires:
    def __init__(self, send, recv):
        self.send, self.recv, self.used, self.sent = send, recv, 0, []

    def port(self):
        self.used += 1
        return self.used - 1

    def push(self, src, dst, port, axis):
        copy = pltpu.make_async_remote_copy(
            src_ref=src,
            dst_ref=dst,
            send_sem=self.send.at[port],
            recv_sem=self.recv.at[port],
            device_id={axis: ahead(axis)},
            device_id_type=MESH,
        )
        copy.start()
        self.sent.append(copy)

    def arrived(self, dst, port, axis):
        pltpu.make_async_remote_copy(
            src_ref=dst,
            dst_ref=dst,
            send_sem=self.send.at[port],
            recv_sem=self.recv.at[port],
            device_id={axis: ahead(axis)},
            device_id_type=MESH,
        ).wait_recv()

    def drain(self):
        for copy in self.sent:
            copy.wait_send()


class BlockGather:
    def __init__(self, wires, src, dst, place, x_first):
        self.wires, self.src, self.dst, self.place, self.x_first = wires, src, dst, place, x_first
        self.nz, self.nx = lax.axis_size("z"), lax.axis_size("x")
        self.ports = {
            (sz, sx): wires.port() for sz in range(self.nz) for sx in range(self.nx) if sz or sx
        }

    def at(self, sz, sx):
        return self.place(self.dst, behind("z", sz) * self.nx + behind("x", sx))

    def forward(self, sz, sx):
        src = self.src if sz == 0 and sx == 0 else self.at(sz, sx)
        if self.x_first:
            go_x, go_z = sz == 0, True
        else:
            go_x, go_z = True, sx == 0
        if go_z and sz + 1 < self.nz:
            self.wires.push(src, self.at(sz, sx), self.ports[sz + 1, sx], "z")
        if go_x and sx + 1 < self.nx:
            self.wires.push(src, self.at(sz, sx), self.ports[sz, sx + 1], "x")

    def take(self, sz, sx):
        from_x = sx > 0 and (sz == 0 if self.x_first else True)
        self.wires.arrived(self.at(sz, sx), self.ports[sz, sx], "x" if from_x else "z")
        self.forward(sz, sx)

    def chain(self):
        self.forward(0, 0)
        for slots in self.rounds():
            for slot in slots:
                yield
                self.take(*slot)

    def rounds(self):
        if self.x_first:
            order = [[(0, sx)] for sx in range(1, self.nx)]
            order += [[(sz, sx) for sx in range(self.nx)] for sz in range(1, self.nz)]
            return order
        last = [[(sz, sx) for sz in range(self.nz)] for sx in range(1, self.nx)]
        return [[(sz, 0)] for sz in range(1, self.nz)] + last


def rows_of(size):
    return lambda ref, owner: ref.at[pl.ds(pl.multiple_of(owner * size, size), size)]


def columns_of(size):
    return lambda ref, owner: ref.at[:, pl.ds(pl.multiple_of(owner * size, size), size)]


def start_kernel(
    tokens, grads, cosine, sine, gains, small, routes, w_query, w_expand, w_output,
    gains_out, small_out, query_out, expand_out, output_out,
    group_out, grads_out, picks_out, member_out, slots_out, latents_out, hidden_out, latent_all_out,
    own_latent, own_hidden, routes_line, grads_line, send, recv, local, *, units, split,
):
    nz, nx, ny, nc = (lax.axis_size(a) for a in AXES)
    nb, nu = nz * nx, ny * nc
    me = lax.axis_index("z") * nx + lax.axis_index("x")
    uly = lax.axis_index("y") * nc + lax.axis_index("core")
    seqs, local_len, features = tokens.shape
    rows = seqs * local_len
    greet(AXES)
    wires = Wires(send, recv)
    used, waited = [], set()

    def load(src, dst):
        copy = pltpu.make_async_copy(src, dst, local.at[len(used)])
        used.append(copy)
        copy.start()
        return copy

    def member(sy, sc):
        return behind("y", sy) * nc + behind("core", sc)

    def line_chain(src, dst):
        ports = [wires.port() for _ in range(nz)]
        wires.push(src, dst.at[1], ports[1], "z")
        mine = load(src, dst.at[0])
        for sz in range(1, nz):
            yield
            wires.arrived(dst.at[sz], ports[sz], "z")
            if sz + 1 < nz:
                wires.push(dst.at[sz], dst.at[sz + 1], ports[sz + 1], "z")
        mine.wait()
        waited.add(id(mine))

    def main():
        g_gains = BlockGather(wires, gains, gains_out, lambda ref, owner: ref.at[owner], False)
        g_small = BlockGather(
            wires, small.at[uly], small_out, lambda ref, owner: ref.at[owner, uly], False
        )
        slots = [(0, 0)] + [slot for r in g_small.rounds() for slot in r]
        y_ports = {(slot, sy): wires.port() for slot in slots for sy in range(1, ny)}
        c_ports = {(slot, sy): wires.port() for slot in slots for sy in range(ny)}

        def piece(slot, sy, sc):
            owner = behind("z", slot[0]) * nx + behind("x", slot[1])
            return small_out.at[owner, member(sy, sc)]

        def spread(slot):
            here = piece(slot, 0, 0)
            if ny > 1:
                wires.push(here, here, y_ports[slot, 1], "y")
            wires.push(here, here, c_ports[slot, 0], "core")

        g_small.forward(0, 0)
        g_gains.forward(0, 0)
        mine = [load(small.at[uly], small_out.at[me, uly]), load(gains, gains_out.at[me])]
        yield
        for slots_now in g_small.rounds():
            for slot in slots_now:
                yield
                g_small.take(*slot)
                if mine:
                    for copy in mine:
                        copy.wait()
                    waited.update(id(copy) for copy in mine)
                    mine = []
                    spread((0, 0))
                spread(slot)
                g_gains.take(*slot)
        for sy in range(1, ny):
            for slot in slots:
                yield
                here = piece(slot, sy, 0)
                wires.arrived(here, y_ports[slot, sy], "y")
                if sy + 1 < ny:
                    wires.push(here, here, y_ports[slot, sy + 1], "y")
                wires.push(here, here, c_ports[slot, sy], "core")
        for sy in range(ny):
            for slot in slots:
                wires.arrived(piece(slot, sy, 1), c_ports[slot, sy], "core")
        gain = jnp.concatenate([gains_out[b, 0:1, : features // nb] for b in range(nb)], axis=1)
        latent_gain = sum(gains_out[b, 2:3, :] for b in range(nb))
        x = tokens[...].astype(wide).reshape(rows, features)
        hidden = norm_rows(x, gain)[0].astype(narrow)
        hidden_out[...] = hidden
        own_hidden[...] = hidden.reshape(tokens.shape)
        spread_hidden = GroupGather(wires, own_hidden, group_out)
        spread_hidden.start()
        load(own_hidden, group_out.at[:, 0, 0])
        width = small_out.shape[-1]
        latent_all = dot(hidden, small_out[...].reshape(features, width))[:, : KVR + RD]
        latent_all_out[...] = latent_all
        latent = norm_rows(latent_all[:, :KVR], latent_gain)[0]
        rope = rotate(latent_all[:, KVR:], cosine[...], sine[...])
        own_latent[:, :, KVR:] = jnp.zeros((seqs, local_len, NOPE), narrow)
        own_latent[:, :, :KVR] = latent.astype(narrow).reshape(seqs, local_len, KVR)
        own_latent[:, :, KVR : KVR + RD] = rope.astype(narrow).reshape(seqs, local_len, RD)
        z_ports = [wires.port() for _ in range(nz)]
        x_ports = [wires.port() for _ in range(nx)]
        yx_ports = [[wires.port() for _ in range(nx)] for _ in range(ny)]
        cx_ports = [[wires.port() for _ in range(nx)] for _ in range(ny)]
        wires.push(own_latent, latents_out.at[:, 0, 0, 0, 1], z_ports[1], "z")
        own_place = load(own_latent, latents_out.at[:, 0, 0, 0, 0])
        for sz in range(1, nz):
            yield
            here = latents_out.at[:, 0, 0, 0, sz]
            wires.arrived(here, z_ports[sz], "z")
            if sz + 1 < nz:
                wires.push(here, latents_out.at[:, 0, 0, 0, sz + 1], z_ports[sz + 1], "z")
        own_place.wait()
        waited.add(id(own_place))
        for sx in range(nx):
            block = latents_out.at[:, 0, 0, sx]
            if sx:
                yield
                wires.arrived(block, x_ports[sx], "x")
            if sx + 1 < nx:
                wires.push(block, latents_out.at[:, 0, 0, sx + 1], x_ports[sx + 1], "x")
            if ny > 1:
                wires.push(block, latents_out.at[:, 0, 1, sx], yx_ports[1][sx], "y")
            wires.push(block, latents_out.at[:, 1, 0, sx], cx_ports[0][sx], "core")
        for sy in range(1, ny):
            for sx in range(nx):
                yield
                block = latents_out.at[:, 0, sy, sx]
                wires.arrived(block, yx_ports[sy][sx], "y")
                if sy + 1 < ny:
                    wires.push(block, latents_out.at[:, 0, sy + 1, sx], yx_ports[sy + 1][sx], "y")
                wires.push(block, latents_out.at[:, 1, sy, sx], cx_ports[sy][sx], "core")
        for sy in range(ny):
            for sx in range(nx):
                yield
                wires.arrived(latents_out.at[:, 1, sy, sx], cx_ports[sy][sx], "core")
        yield from spread_hidden.chain()

    def slots_chain():
        yield from line_chain(routes, routes_line)
        yield from line_chain(grads, grads_line)
        count = rows
        earlier = (
            lax.broadcasted_iota(jnp.int32, (count, count), 1)
            < lax.broadcasted_iota(jnp.int32, (count, count), 0)
        ).astype(narrow)
        columns = picks_out.shape[-1]
        expert = lax.broadcasted_iota(jnp.int32, (EXPERTS, columns), 0)
        column = lax.broadcasted_iota(jnp.int32, (EXPERTS, columns), 1)
        unit = column // SLOTS
        if split > 1:
            unit = unit // split
        chosen = (expert == unit + lax.axis_index("z") * (EXPERTS // nz)).astype(narrow)
        slot = lax.rem(lax.broadcasted_iota(jnp.int32, (count, columns), 1), SLOTS)
        names = lax.broadcasted_iota(jnp.int32, (count, EXPERTS), 1)
        for s in range(nz):
            member = sum(
                (routes_line[s, :, j : j + 1] == names).astype(wide) for j in range(TOP)
            )
            if s == 0:
                member_out[...] = member
            rank = dot(earlier, member.astype(narrow))
            code = jnp.where(member > 0, rank, -1.0).astype(narrow)
            pick = (dot(code, chosen) == slot.astype(wide)).astype(narrow)
            picks_out[s] = pick
            row_grads = grads_line[s].reshape(rows, features)
            shaped = (slots_out.shape[0],) + slots_out.shape[2:]
            slots_out[:, s] = dot_tn(pick, row_grads).astype(narrow).reshape(shaped)

    def group_chain(src, dst):
        gather = GroupGather(wires, src, dst)
        gather.start()
        load(src, dst.at[:, 0, 0])
        yield from gather.chain()

    def array_chain(src, dst, place, x_first):
        gather = BlockGather(wires, src, dst, place, x_first)
        load(src, gather.at(0, 0))
        yield from gather.chain()

    first = main()
    next(first)
    others = [
        array_chain(w_query, query_out, rows_of(w_query.shape[0]), False),
        array_chain(w_expand, expand_out, rows_of(w_expand.shape[0]), True),
        array_chain(w_output, output_out, columns_of(w_output.shape[1]), False),
        slots_chain(),
        group_chain(grads, grads_out),
    ]
    for _ in range(HEAD_START):
        next(first)
    weave(first, others, 2)
    wires.drain()
    for copy in used:
        if id(copy) not in waited:
            copy.wait()


def start(tokens, grads, cosine, sine, gains, small, routes, weights, units, split):
    nz, nx, ny, nc = (lax.axis_size(a) for a in AXES)
    nb, nu = nz * nx, ny * nc
    seqs, local_len, features = tokens.shape
    shape = jax.ShapeDtypeStruct

    def whole(w, dim):
        size = list(w.shape)
        size[dim] *= nb
        return shape(tuple(size), w.dtype)

    rows = seqs * local_len
    grouped = (seqs, ny, nc, local_len, features)
    outs = [
        shape((nb,) + gains.shape, wide),
        shape((nb,) + small.shape, narrow),
        *[whole(w, d) for w, d in zip(weights, (0, 0, 1))],
        shape(grouped, narrow),
        shape(grouped, narrow),
        shape((nz, rows, nx * nu * units * SLOTS), narrow),
        shape((rows, EXPERTS), wide),
        shape((nx * nu, nz, units, SLOTS, features), narrow),
        shape((seqs, nc, ny, nx, nz, local_len, KVR + NOPE), narrow),
        shape((seqs * local_len, features), narrow),
        shape((seqs * local_len, KVR + RD), wide),
    ]
    return pl.pallas_call(
        functools.partial(start_kernel, units=units, split=split),
        out_shape=outs,
        in_specs=[VMEM, ANY, VMEM, VMEM, VMEM, VMEM, VMEM] + [ANY] * 3,
        out_specs=[VMEM, VMEM] + [ANY] * 5 + [VMEM] * 3 + [ANY] + [VMEM, VMEM],
        scratch_shapes=[
            pltpu.VMEM((seqs, local_len, KVR + NOPE), narrow),
            pltpu.VMEM(tokens.shape, narrow),
            pltpu.VMEM((nz,) + routes.shape, routes.dtype),
            pltpu.VMEM((nz,) + grads.shape, narrow),
            pltpu.SemaphoreType.DMA((384,)),
            pltpu.SemaphoreType.DMA((384,)),
            pltpu.SemaphoreType.DMA((16,)),
        ],
        compiler_params=pltpu.CompilerParams(
            collective_id=0, has_side_effects=True, vmem_limit_bytes=40 * 1024 * 1024
        ),
        cost_estimate=costs(120),
    )(tokens, grads, cosine, sine, gains, small, routes, *weights)


def scores_of(query, keys, rope, scale):
    return (dot_nt(query[:, :NOPE], keys) + dot_nt(query[:, NOPE:], rope)) * scale


def attend_kernel(
    query, cosine, sine, keys, rope, query_pos, key_pos, query_out, attended, stats, head_lin,
    *, scale, sub,
):
    qk = NOPE + RD
    for head in range(query.shape[1] // qk):

        @pl.when(pl.program_id(1) == head)
        def _(head=head):
            head_lin[:, :qk] = query[:, head * qk : (head + 1) * qk]

    keys_ = keys[:, :NOPE]
    values = keys[:, NOPE:]

    @pl.loop(0, query.shape[0], step=sub)
    def _(first):
        span = pl.ds(pl.multiple_of(first, sub), sub)
        lin = head_lin[span, :]
        turned = rotate(lin[:, NOPE : NOPE + RD], cosine[span, :], sine[span, :])
        query_out[span, :NOPE] = lin[:, :NOPE].astype(narrow)
        query_out[span, NOPE:] = jnp.zeros((sub, NOPE), narrow)
        query_out[span, NOPE : NOPE + RD] = turned.astype(narrow)
        scores = scores_of(query_out[span, :], keys_, rope[0], scale)
        scores = jnp.where(key_pos[...] <= query_pos[span, :], scores, -jnp.inf)
        top = jnp.max(scores, axis=1, keepdims=True)
        raised = jnp.exp(scores - top)
        total = jnp.sum(raised, axis=1, keepdims=True)
        probability = (raised * (1.0 / total)).astype(narrow)
        attended[span, :] = dot(probability, values).astype(narrow)
        stats[0, 0, span, 0:1] = top
        stats[0, 0, span, 1:2] = top + jnp.log(total)


def attend_back_kernel(
    query, cosine, sine, keys, rope, query_pos, key_pos, stats, grads,
    query_grad, expand_grad, rope_grad, key_acc, *, scale, sub,
):
    keys_ = keys[:, :NOPE]
    values = keys[:, NOPE:]
    key_acc[...] = jnp.zeros(key_acc.shape, wide)

    @pl.loop(0, query.shape[0], step=sub)
    def _(first):
        span = pl.ds(pl.multiple_of(first, sub), sub)
        rows = query[span, :]
        scores = scores_of(rows, keys_, rope[0], scale)
        scores = jnp.where(key_pos[...] <= query_pos[span, :], scores, -jnp.inf)
        probability = jnp.exp(scores - stats[0, 0, span, 1:2])
        grad = grads[span, :]
        prob_grad = dot_nt(grad, values)
        weighted = probability * prob_grad
        delta = jnp.sum(weighted, axis=1, keepdims=True)
        score_grad = ((weighted - probability * delta) * scale).astype(narrow)
        back_plain = dot(score_grad, keys_).astype(narrow)
        back_turned = dot(score_grad, rope[0])[:, :RD].astype(narrow).astype(wide)
        turned = unrotate(back_turned, cosine[span, :], sine[span, :]).astype(narrow)
        head_grad = jnp.concatenate([back_plain, turned], axis=1)
        qk = NOPE + RD
        for head in range(query_grad.shape[1] // qk):

            @pl.when(pl.program_id(1) == head)
            def _(head=head):
                query_grad[span, head * qk : (head + 1) * qk] = head_grad

        key_acc[:, : 2 * NOPE] += dot_tn(score_grad, rows)
        key_acc[:, 2 * NOPE :] += dot_tn(probability.astype(narrow), grad)

    expand_grad[:, :NOPE] = key_acc[:, :NOPE].astype(narrow)
    expand_grad[:, NOPE:] = key_acc[:, 2 * NOPE :].astype(narrow)

    @pl.when(pl.program_id(1) == 0)
    def _():
        rope_grad[0] = key_acc[:, NOPE : 2 * NOPE]

    @pl.when(pl.program_id(1) > 0)
    def _():
        rope_grad[0] += key_acc[:, NOPE : 2 * NOPE]


def attention_specs(seqs, heads, reach, length):
    both = NOPE + VH
    return dict(
        query=pl.BlockSpec((reach, both), lambda s, h: (s, h)),
        heads=pl.BlockSpec((reach, heads * (NOPE + RD)), lambda s, h: (s, 0)),
        rope_grad=pl.BlockSpec((1, length, NOPE), lambda s, h: (s, 0, 0)),
        table=pl.BlockSpec((reach, RD // 2), lambda s, h: (0, 0)),
        keys=pl.BlockSpec((length, both), lambda s, h: (s, h)),
        rope=pl.BlockSpec((1, length, NOPE), lambda s, h: (s, 0, KVR // NOPE)),
        query_pos=pl.BlockSpec((reach, 1), lambda s, h: (0, 0)),
        key_pos=pl.BlockSpec((1, length), lambda s, h: (0, 0)),
        head=pl.BlockSpec((reach, VH), lambda s, h: (s, h)),
        stats=pl.BlockSpec((1, 1, reach, 2), lambda s, h: (s, h, 0, 0)),
    )


def attend(query_lin, cosine, sine, keys, rope, query_pos, key_pos, seqs, heads):
    reach, length = query_pos.shape[0], key_pos.shape[1]
    sub = min(reach, max(16, 256 * 2048 // length))
    sp = attention_specs(seqs, heads, reach, length)
    shape = jax.ShapeDtypeStruct
    return pl.pallas_call(
        functools.partial(attend_kernel, scale=(NOPE + RD) ** -0.5, sub=sub),
        grid=(seqs, heads),
        in_specs=[sp[k] for k in ("heads", "table", "table", "keys", "rope", "query_pos", "key_pos")],
        out_specs=[sp["query"], sp["head"], sp["stats"]],
        out_shape=[
            shape((seqs * reach, heads * 2 * NOPE), narrow),
            shape((seqs * reach, heads * VH), narrow),
            shape((seqs, heads, reach, 2), wide),
        ],
        scratch_shapes=[pltpu.VMEM((reach, 2 * NOPE), wide)],
        cost_estimate=costs(16),
        compiler_params=pltpu.CompilerParams(vmem_limit_bytes=61 * 1024 * 1024),
    )(query_lin, cosine, sine, keys, rope, query_pos, key_pos)


def attend_back(query, cosine, sine, keys, rope, query_pos, key_pos, stats, grads, seqs, heads):
    reach, length = query_pos.shape[0], key_pos.shape[1]
    sub = min(reach, max(16, 256 * 2048 // length))
    sp = attention_specs(seqs, heads, reach, length)
    shape = jax.ShapeDtypeStruct
    return pl.pallas_call(
        functools.partial(attend_back_kernel, scale=(NOPE + RD) ** -0.5, sub=sub),
        grid=(seqs, heads),
        in_specs=[
            sp[k]
            for k in (
                "query", "table", "table", "keys", "rope", "query_pos", "key_pos", "stats", "head",
            )
        ],
        out_specs=[sp["heads"], sp["keys"], sp["rope_grad"]],
        cost_estimate=costs(25),
        out_shape=[
            shape((seqs * reach, heads * (NOPE + RD)), narrow),
            shape(keys.shape, narrow),
            shape((seqs, length, NOPE), wide),
        ],
        scratch_shapes=[pltpu.VMEM((length, 2 * NOPE + VH), wide)],
        compiler_params=pltpu.CompilerParams(vmem_limit_bytes=61 * 1024 * 1024),
    )(query, cosine, sine, keys, rope, query_pos, key_pos, stats, grads)


def costs(us):
    return pl.CostEstimate(flops=int(us * 1e9), bytes_accessed=int(us * 1e6), transcendentals=0)


def add_into(target, *terms):
    lead, count = target.shape[:-2], target.shape[-2]
    step = 32 if count % 32 == 0 else 16 if count % 16 == 0 else count
    pieces = count // step
    total = pieces
    for size in lead:
        total *= size

    @pl.loop(0, total)
    def _(i):
        at = []
        rest = i // pieces
        for size in reversed(lead):
            at.insert(0, lax.rem(rest, size))
            rest = rest // size
        span = pl.ds(pl.multiple_of(lax.rem(i, pieces) * step, step), step)
        place = (*at, span, slice(None))
        target[place] = sum(term[place].astype(wide) for term in terms).astype(target.dtype)


class Queue:
    def __init__(self):
        self.items = []

    def add(self, place, thunk):
        self.items.append((place, len(self.items), thunk))
        self.items.sort(key=lambda item: item[:2])

    def go(self, count):
        for _, _, thunk in self.items[:count]:
            thunk()
        del self.items[:count]


class BlockScatter:
    def __init__(self, wires, loads, src, place, axes, acc, first, second, out):
        self.wires, self.loads, self.src, self.place, self.axes = wires, loads, src, place, axes
        self.acc, self.first, self.second, self.out = acc, first, second, out
        self.na, self.nb = (lax.axis_size(a) for a in axes)
        self.ports = {
            (a, b): wires.port() for b in range(self.nb) for a in range(self.na) if a or b
        }
        self.order = [*range(1, self.nb), 0]

    def mine(self, a, b):
        steps = dict(zip(self.axes, (a, b)))
        owner = behind("z", steps["z"]) * lax.axis_size("x") + behind("x", steps["x"])
        return self.place(self.src, owner)

    def slot(self, a, b):
        return self.acc.at[b, max(a - 1, 0)]

    def start(self, queue=None):
        self.loading, self.queue = {}, queue or Queue()
        for place, b in enumerate(self.order):
            self.queue.add(
                place,
                lambda b=b: self.wires.push(
                    self.mine(1, b), self.first.at[b, 0], self.ports[1, b], self.axes[0]
                ),
            )
        if queue is None:
            self.queue.go(self.nb)
        for b in self.order:
            for a in [*range(2, self.na), 0]:
                self.loading[a, b] = self.loads(self.mine(a, b), self.slot(a, b))

    def chain(self):
        wires, (axis_a, axis_b) = self.wires, self.axes
        for b in self.order:
            for a in [*range(2, self.na), 0]:
                came = self.first.at[b, (a or self.na) - 2]
                yield
                wires.arrived(came, self.ports[(a or self.na) - 1, b], axis_a)
                if not a:
                    self.queue.go(1)
                self.loading[a, b].wait()
                add_into(self.slot(a, b), self.slot(a, b), came)
                if a:
                    wires.push(self.slot(a, b), self.first.at[b, a - 1], self.ports[a, b], axis_a)
            if b >= 2:
                yield
                wires.arrived(self.second.at[b - 2], self.ports[0, b - 1], axis_b)
                add_into(self.slot(0, b), self.slot(0, b), self.second.at[b - 2])
            if b >= 1:
                wires.push(self.slot(0, b), self.second.at[b - 1], self.ports[0, b], axis_b)
        yield
        wires.arrived(self.second.at[self.nb - 2], self.ports[0, self.nb - 1], axis_b)
        add_into(self.out, self.slot(0, 0), self.second.at[self.nb - 2])


def scatter_scratch(shard, axes, dtype=narrow):
    na, nb = (lax.axis_size(a) for a in axes)
    return [
        pltpu.VMEM((nb, na - 1) + shard, dtype),
        pltpu.VMEM((nb, na - 1) + shard, dtype),
        pltpu.VMEM((nb - 1,) + shard, dtype),
    ]


class GroupGather:
    def __init__(self, wires, src, dst):
        self.wires, self.src, self.dst = wires, src, dst
        self.ny, self.nc = lax.axis_size("y"), lax.axis_size("core")
        self.ports = [wires.port() for _ in range(self.ny * self.nc)]

    def start(self):
        if self.ny > 1:
            self.wires.push(self.src, self.dst.at[:, 1, 0], self.ports[self.nc], "y")
        self.wires.push(self.src, self.dst.at[:, 0, 1], self.ports[1], "core")

    def chain(self):
        wires, dst, nc = self.wires, self.dst, self.nc
        for sy in range(1, self.ny):
            piece = dst.at[:, sy, 0]
            yield
            wires.arrived(piece, self.ports[sy * nc], "y")
            if sy + 1 < self.ny:
                wires.push(piece, dst.at[:, sy + 1, 0], self.ports[(sy + 1) * nc], "y")
            wires.push(piece, dst.at[:, sy, 1], self.ports[sy * nc + 1], "core")
        for sy in range(self.ny):
            yield
            wires.arrived(dst.at[:, sy, 1], self.ports[sy * nc + 1], "core")


def group_sum_chain(wires, src, own, other, came, load):
    ny = lax.axis_size("y")
    core_ports = [wires.port() for _ in range(ny)]
    y_ports = [wires.port() for _ in range(ny)]
    order = [*range(1, ny), 0]
    for sy in order:
        wires.push(src.at[:, sy, 1], other.at[:, sy], core_ports[sy], "core")
    loading = [load(src.at[:, sy, 0], own.at[:, sy]) for sy in range(ny)]
    for sy in order:
        yield
        wires.arrived(other.at[:, sy], core_ports[sy], "core")
        loading[sy].wait()
        add_into(own.at[:, sy], own.at[:, sy], other.at[:, sy])
        if ny > 1:
            last = (sy or ny) - 1
            if last:
                yield
                wires.arrived(came.at[:, last - 1], y_ports[last], "y")
                add_into(own.at[:, sy], own.at[:, sy], came.at[:, last - 1])
            if sy:
                wires.push(own.at[:, sy], came.at[:, sy - 1], y_ports[sy], "y")


def weave(main, others, share):
    others = list(others)
    running = True
    while running or others:
        if running:
            running = next(main, True) is None
        for _ in range(share if running else max(1, len(others))):
            if others:
                chain = others.pop(0)
                if next(chain, True) is None:
                    others.append(chain)


def finish_kernel(
    hidden_sum, latent_partial, tokens, residual_grad, small, hidden_t, mid_t, logit_grad,
    ffn_gain, gain_attn, gain_latent, latent_all, cosine, sine, residual, shared_sum, picks, slots,
    *rest, modes,
):
    count = len(modes)
    partials, rest = rest[:count], rest[count:]
    tokens_grad, block_out, latent_w_out, gains_out, *rest = rest
    outs, rest = rest[:count], rest[count:]
    (
        lat_own, lat_x, lat_z,
        own_lag, lag_group, wide_acc, lat_wgrad, gain_terms, routed_slots, routed_own, routed_came, *rest,
    ) = rest
    buffers, rest = rest[: 3 * count], rest[3 * count :]
    lw_buffers, g_buffers = rest[:3], rest[3:6]
    send, recv, local = rest[6:]
    nz, nx, ny, nc = (lax.axis_size(a) for a in AXES)
    nb, nu = nz * nx, ny * nc
    uly = lax.axis_index("y") * nc + lax.axis_index("core")
    seqs, local_len, features = tokens.shape
    rows = seqs * local_len
    greet(AXES)
    wires = Wires(send, recv)
    used = []

    def load(src, dst):
        copy = pltpu.make_async_copy(src, dst, local.at[len(used)])
        used.append(copy)
        copy.start()
        return copy

    def blocks_of(size, dim):
        return rows_of(size) if dim == 0 else columns_of(size)

    scatters = [
        BlockScatter(
            wires, load, partials[i], blocks_of(partials[i].shape[dim] // nb, dim), axes,
            *buffers[3 * i : 3 * i + 3], outs[i],
        )
        for i, (dim, axes) in enumerate(modes)
    ]

    def routed_chain():
        ports = [wires.port() for _ in range(nz)]
        loading = {s: load(slots.at[:, s], routed_slots.at[s]) for s in [*range(1, nz), 0]}
        for s in [*range(1, nz), 0]:
            own = routed_own.at[s]
            last = (s or nz) - 1
            yield
            loading[s].wait()
            term = dot(picks[s], routed_slots[s].reshape(picks.shape[2], features))
            routed_own[s] = term.astype(narrow)
            if last:
                wires.arrived(routed_came.at[last - 1], ports[last], "z")
                add_into(own, own, routed_came.at[last - 1])
            if s:
                wires.push(own, routed_came.at[s - 1], ports[s], "z")

    def output_chain():
        yield from routed_chain()
        total = residual[...] + shared_sum[...].astype(wide).reshape(rows, features)
        total = total + routed_own[0].astype(wide)
        block_out[...] = total.astype(narrow).reshape(tokens.shape)

    def latent_chain():
        x_ports = [wires.port() for _ in range(nx)]
        z_ports = [wires.port() for _ in range(nz)]
        wires.push(latent_partial.at[:, 1], lat_x.at[:, 0], x_ports[1], "x")
        order_x = [*range(2, nx), 0]
        loading = {sx: load(latent_partial.at[:, sx], lat_own.at[:, sx]) for sx in order_x}
        yield
        for sx in order_x:
            own, last = lat_own.at[:, sx], (sx or nx) - 1
            yield
            wires.arrived(lat_x.at[:, last - 1], x_ports[last], "x")
            loading[sx].wait()
            add_into(own, own, lat_x.at[:, last - 1])
            if sx:
                wires.push(own, lat_x.at[:, sx - 1], x_ports[sx], "x")
        for sz in [*range(1, nz), 0]:
            own = lat_own.at[:, 0, sz]
            last = (sz or nz) - 1
            if last:
                yield
                wires.arrived(lat_z.at[:, last - 1], z_ports[last], "z")
                add_into(own, own, lat_z.at[:, last - 1])
            if sz:
                wires.push(own, lat_z.at[:, sz - 1], z_ports[sz], "z")

    def main():
        latent = latent_chain()
        next(latent)
        for s in scatters:
            s.start(queue)
        queue.go(3)
        yield
        for _ in latent:
            yield
        width = KVR + RD
        lat = lat_own[:, 0, 0].astype(wide).reshape(rows, KVR + NOPE)[:, :width]
        latent_grad = lat[:, :KVR]
        _, normed, inverse = norm_rows(latent_all[:, :KVR], gain_latent[...])
        lat_in = norm_input_back(latent_grad, normed, inverse, gain_latent[...])
        turned = unrotate(lat[:, KVR:], cosine[...], sine[...])
        own_lag[:, :, KVR:] = jnp.zeros((seqs, local_len, own_lag.shape[-1] - KVR), narrow)
        own_lag[:, :, :KVR] = lat_in.astype(narrow).reshape(seqs, local_len, KVR)
        own_lag[:, :, KVR:width] = turned.astype(narrow).reshape(seqs, local_len, RD)
        wide_acc[...] = dot_nt(own_lag[...].reshape(rows, own_lag.shape[-1]), small[...])
        own_lag[:, :, width:] = logit_grad[...].reshape(seqs, local_len, EXPERTS)
        lag_gather = GroupGather(wires, own_lag, lag_group)
        lag_gather.start()
        own_copy = load(own_lag, lag_group.at[:, 0, 0])
        x = tokens[...].astype(wide).reshape(rows, features)
        _, normed_in, inverse_in = norm_rows(x, gain_attn[...])
        hidden_grad = wide_acc[...] + hidden_sum[...].astype(wide).reshape(rows, features)
        wide_acc[...] = residual_grad[...] + norm_input_back(
            hidden_grad, normed_in, inverse_in, gain_attn[...]
        )
        attn_gain = jnp.sum(hidden_grad * normed_in, axis=0, keepdims=True)
        latent_gain = jnp.sum(latent_grad * normed, axis=0, keepdims=True)
        tokens_grad[...] = wide_acc[...].astype(narrow).reshape(tokens.shape)
        shard = features // nb
        gain_terms[...] = jnp.zeros(gain_terms.shape, wide)
        for b in range(nb):
            gain_terms[b, 0:1, :shard] = attn_gain[:, b * shard : (b + 1) * shard]
            gain_terms[b, 0:1, shard:] = latent_gain
            gain_terms[b, 1:2, :shard] = ffn_gain[:, b * shard : (b + 1) * shard]
        gain_sum = BlockScatter(
            wires, load, gain_terms, lambda ref, owner: ref.at[owner], ("x", "z"), *g_buffers,
            gains_out.at[uly],
        )
        gain_sum.start()
        for _ in lag_gather.chain():
            yield
        own_copy.wait()
        lags = lag_group[...].reshape(nu * rows, own_lag.shape[-1])
        terms = dot(hidden_t[...], lags).astype(narrow)
        lat_wgrad[...] = terms.reshape(lat_wgrad.shape)
        terms = dot(mid_t[...], lags)[:, width:].astype(narrow)
        lat_wgrad[:, :, width:] = terms.reshape(lat_wgrad.shape[:2] + (EXPERTS,))
        w_sum = BlockScatter(
            wires, load, lat_wgrad, lambda ref, owner: ref.at[owner], ("x", "z"), *lw_buffers,
            latent_w_out.at[uly],
        )
        w_sum.start()
        chains = [gain_sum.chain(), w_sum.chain()]
        while chains:
            chain = chains.pop(0)
            if next(chain, True) is None:
                chains.append(chain)
                yield
        outs_ = (latent_w_out, gains_out)
        y_ports = [[wires.port() for _ in range(ny)] for _ in outs_]
        c_ports = [[wires.port() for _ in range(ny)] for _ in outs_]
        member = lambda sy, sc: behind("y", sy) * nc + behind("core", sc)
        for ref, yp, cp in zip(outs_, y_ports, c_ports):
            here = ref.at[uly]
            if ny > 1:
                wires.push(here, here, yp[1], "y")
            wires.push(here, here, cp[0], "core")
        for sy in range(1, ny):
            for ref, yp, cp in zip(outs_, y_ports, c_ports):
                piece = ref.at[member(sy, 0)]
                yield
                wires.arrived(piece, yp[sy], "y")
                if sy + 1 < ny:
                    wires.push(piece, piece, yp[sy + 1], "y")
                wires.push(piece, piece, cp[sy], "core")
        for sy in range(ny):
            for ref, cp in zip(outs_, c_ports):
                yield
                wires.arrived(ref.at[member(sy, 1)], cp[sy], "core")

    queue = Queue()
    weave(main(), [s.chain() for s in scatters] + [output_chain()], 1)
    wires.drain()


def finish(
    hidden_sum, latent_partial, tokens, residual_grad, small, hidden_t, mid_t, logit_grad,
    ffn_gain, gain_attn, gain_latent, latent_all, cosine, sine, residual, shared_sum, picks, slots,
    partials, modes,
):
    nz, nx, ny, nc = (lax.axis_size(a) for a in AXES)
    nb, nu = nz * nx, ny * nc
    seqs, local_len, features = tokens.shape
    rows = seqs * local_len
    shape = jax.ShapeDtypeStruct
    shards = []
    for p, (dim, _) in zip(partials, modes):
        size = list(p.shape)
        size[dim] //= nb
        shards.append(tuple(size))
    width, shard = KVR + RD, features // nb
    padded = small.shape[-1]
    few = lambda n: max(n - 1, 1)
    scratch = [
        pltpu.VMEM((seqs, nx, nz, local_len, KVR + NOPE), narrow),
        pltpu.VMEM((seqs, few(nx), nz, local_len, KVR + NOPE), narrow),
        pltpu.VMEM((seqs, few(nz), local_len, KVR + NOPE), narrow),
        pltpu.VMEM((seqs, local_len, padded), narrow),
        pltpu.VMEM((seqs, ny, nc, local_len, padded), narrow),
        pltpu.VMEM((rows, features), wide),
        pltpu.VMEM((nb, shard // nu, padded), narrow),
        pltpu.VMEM((nb, 8, shard + KVR), wide),
        pltpu.VMEM((nz, nx * nu, *slots.shape[2:]), narrow),
        pltpu.VMEM((nz, rows, features), narrow),
        pltpu.VMEM((few(nz), rows, features), narrow),
    ]
    for size, (_, axes) in zip(shards, modes):
        scratch += scatter_scratch(size, axes)
    scratch += scatter_scratch((shard // nu, padded), ("x", "z"))
    scratch += scatter_scratch((8, shard + KVR), ("x", "z"), wide)
    scratch += [
        pltpu.SemaphoreType.DMA((256,)),
        pltpu.SemaphoreType.DMA((256,)),
        pltpu.SemaphoreType.DMA((256,)),
    ]
    return pl.pallas_call(
        functools.partial(finish_kernel, modes=modes),
        out_shape=[
            shape(tokens.shape, narrow),
            shape(tokens.shape, narrow),
            shape((nu, shard // nu, padded), wide),
            shape((nu, 8, shard + KVR), wide),
            *[shape(size, wide) for size in shards],
        ],
        in_specs=[VMEM, ANY] + [VMEM] * 15 + [ANY] * (1 + len(partials)),
        out_specs=[VMEM] * (4 + len(partials)),
        scratch_shapes=scratch,
        compiler_params=pltpu.CompilerParams(
            collective_id=1, has_side_effects=True, vmem_limit_bytes=62 * 1024 * 1024
        ),
        cost_estimate=costs(190),
    )(
        hidden_sum, latent_partial, tokens, residual_grad, small, hidden_t, mid_t, logit_grad,
        ffn_gain, gain_attn, gain_latent, latent_all, cosine, sine, residual, shared_sum, picks, slots,
        *partials,
    )


class Layer:
    def __init__(self):
        self.sizes = [lax.axis_size(a) for a in AXES[1:]]
        self.count = self.sizes[0] * self.sizes[1] * self.sizes[2]

    def offsets(self, k):
        _, ny, nc = self.sizes
        return k // (ny * nc), k // nc % ny, k % nc

    def device(self, k, sign=1):
        return {
            axis: lax.rem(lax.axis_index(axis) + (sign * d) % n, n)
            for axis, d, n in zip(AXES[1:], self.offsets(k), self.sizes)
        }

    def number(self, k, sign=1):
        where = self.device(k, sign)
        return (where["x"] * self.sizes[1] + where["y"]) * self.sizes[2] + where["core"]

    def greet(self):
        barrier = pltpu.get_barrier_semaphore()
        for k in range(1, self.count):
            pl.semaphore_signal(barrier, inc=1, device_id=self.device(k), device_id_type=MESH)
        pl.semaphore_signal(
            barrier, inc=1, device_id={"z": behind("z", 1)}, device_id_type=MESH
        )
        pl.semaphore_wait(barrier, self.count)

    def push(self, wires, src, dst, port, k):
        copy = pltpu.make_async_remote_copy(
            src_ref=src,
            dst_ref=dst,
            send_sem=wires.send.at[port],
            recv_sem=wires.recv.at[port],
            device_id=self.device(k),
            device_id_type=MESH,
        )
        copy.start()
        wires.sent.append(copy)


def dispatch_kernel(
    partial, tokens, gain, router, member, picks, top, *rest, plan,
):
    count = len(plan)
    shards, rest = rest[:count], rest[count:]
    residual_out, gates_out, hidden_out, group_out, rows_out, tops_out, *rest = rest
    wholes, rest = rest[:count], rest[count:]
    own, other, came, hidden, line, outgoing, send, recv, local = rest
    nz, nx = lax.axis_size("z"), lax.axis_size("x")
    seqs, local_len, features = tokens.shape
    rows = seqs * local_len
    layer = Layer()
    layer.greet()
    wires = Wires(send, recv)
    used, waited = [], set()

    def load(src, dst):
        copy = pltpu.make_async_copy(src, dst, local.at[len(used)])
        used.append(copy)
        copy.start()
        return copy

    def main():
        for _ in group_sum_chain(wires, partial, own, other, came, load):
            yield
        waited.update(id(copy) for copy in used[: own.shape[1]])
        residual = tokens[...].astype(wide).reshape(rows, features)
        residual = residual + own[:, 0].astype(wide).reshape(rows, features)
        residual_out[...] = residual
        normed = norm_rows(residual, gain[...])[0].astype(narrow)
        hidden_out[...] = normed
        hidden[...] = normed.reshape(tokens.shape)
        line[0, :, :features] = normed
        logits = jnp.where(member[...] > 0, dot(normed, router[...]), -jnp.inf)
        raised = jnp.exp(logits - jnp.max(logits, axis=1, keepdims=True))
        gates = raised / jnp.sum(raised, axis=1, keepdims=True)
        gates_out[...] = gates
        high = gates.astype(narrow).astype(wide)
        line[0, :, features:] = jnp.concatenate([high, gates - high], axis=1).astype(narrow)
        z_ports = [wires.port() for _ in range(nz)]
        wires.push(line.at[0], line.at[1], z_ports[1], "z")
        gather = GroupGather(wires, hidden, group_out)
        gather.start()
        load(hidden, group_out.at[:, 0, 0])
        ports = [[wires.port() for _ in range(layer.count)] for _ in range(nz)]
        me = layer.number(0)
        chain = gather.chain()
        for s in range(nz):
            if s:
                yield
                wires.arrived(line.at[s], z_ports[s], "z")
                if s + 1 < nz:
                    wires.push(line.at[s], line.at[s + 1], z_ports[s + 1], "z")
            outgoing[s] = dot_tn(picks[s], line[s]).astype(narrow).reshape(outgoing.shape[1:])
            for k in range(1, layer.count):
                target = layer.number(k)
                layer.push(wires, outgoing.at[s, target], rows_out.at[me, s], ports[s][k], k)
            load(outgoing.at[s, me], rows_out.at[me, s])
            next(chain, None)
        for _ in chain:
            pass
        for s in range(nz):
            yield
            for k in range(1, layer.count):
                wires.arrived(rows_out.at[layer.number(k, -1), s], ports[s][k], "z")

    def tops():
        z_ports = [wires.port() for _ in range(nz)]
        x_ports = [wires.port() for _ in range(nx)]
        mine = load(top, tops_out.at[0, 0])
        waited.add(id(mine))
        wires.push(top, tops_out.at[0, 1], z_ports[1], "z")
        for s in range(1, nz):
            yield
            wires.arrived(tops_out.at[0, s], z_ports[s], "z")
            if s + 1 < nz:
                wires.push(tops_out.at[0, s], tops_out.at[0, s + 1], z_ports[s + 1], "z")
        mine.wait()
        wires.push(tops_out.at[0], tops_out.at[1], x_ports[1], "x")
        for s in range(1, nx):
            yield
            wires.arrived(tops_out.at[s], x_ports[s], "x")
            if s + 1 < nx:
                wires.push(tops_out.at[s], tops_out.at[s + 1], x_ports[s + 1], "x")

    def array_chain(src, dst, dim, x_first):
        place = (rows_of if dim == 0 else columns_of)(src.shape[dim])
        gather = BlockGather(wires, src, dst, place, x_first)
        load(src, gather.at(0, 0))
        yield from gather.chain()

    first = main()
    next(first)
    others = [array_chain(a, b, *mode) for a, b, mode in zip(shards, wholes, plan)]
    weave(first, others + [tops()], 1)
    for copy in used:
        if id(copy) not in waited:
            copy.wait()
    wires.drain()


def whole_array(w, dim):
    size = list(w.shape)
    size[dim] *= lax.axis_size("z") * lax.axis_size("x")
    return jax.ShapeDtypeStruct(tuple(size), w.dtype)


def dispatch(partial, tokens, gain, router, member, picks, top, units, shards, plan):
    nz, nx, ny, nc = (lax.axis_size(a) for a in AXES)
    seqs, local_len, features = tokens.shape
    rows = seqs * local_len
    layer = nx * ny * nc
    shape = jax.ShapeDtypeStruct
    extended = features + 2 * EXPERTS
    part = pltpu.VMEM((seqs, ny, local_len, features), narrow)
    return pl.pallas_call(
        functools.partial(dispatch_kernel, plan=plan),
        out_shape=[
            shape((rows, features), wide),
            shape((rows, EXPERTS), wide),
            shape((rows, features), narrow),
            shape((seqs, ny, nc, local_len, features), narrow),
            shape((layer, nz, units, SLOTS, extended), narrow),
            shape((nx, nz) + top.shape, wide),
            *[whole_array(w, dim) for w, (dim, _) in zip(shards, plan)],
        ],
        in_specs=[ANY] + [VMEM] * 6 + [ANY] * len(shards),
        out_specs=[VMEM, VMEM, VMEM, ANY, ANY, VMEM] + [ANY] * len(shards),
        scratch_shapes=[
            part, part, part,
            pltpu.VMEM((seqs, local_len, features), narrow),
            pltpu.VMEM((nz, rows, extended), narrow),
            pltpu.VMEM((nz, layer, units, SLOTS, extended), narrow),
            pltpu.SemaphoreType.DMA((256,)),
            pltpu.SemaphoreType.DMA((256,)),
            pltpu.SemaphoreType.DMA((32,)),
        ],
        compiler_params=pltpu.CompilerParams(
            collective_id=2, has_side_effects=True, vmem_limit_bytes=48 * 1024 * 1024
        ),
        cost_estimate=costs(80),
    )(partial, tokens, gain, router, member, picks, top, *shards)


def return_kernel(
    returned, partial, shared_partial, residual, gates, router, gain, grads, picks, *rest, modes,
):
    count = len(modes)
    partials, rest = rest[:count], rest[count:]
    residual_grad_out, group_out, logit_out, gain_out, shared_out, *rest = rest
    outs, rest = rest[:count], rest[count:]
    own, other, came, sh_own, sh_other, sh_came, back, line, own_grad, *rest = rest
    buffers, rest = rest[: 3 * count], rest[3 * count :]
    send, recv, local = rest
    nz, nx = lax.axis_size("z"), lax.axis_size("x")
    seqs, local_len, features = grads.shape
    rows = seqs * local_len
    layer = Layer()
    layer.greet()
    wires = Wires(send, recv)
    used = []

    def load(src, dst):
        copy = pltpu.make_async_copy(src, dst, local.at[len(used)])
        used.append(copy)
        copy.start()
        return copy

    queue = Queue()
    scatters = [
        BlockScatter(
            wires, load, partials[i],
            (rows_of if dim == 0 else columns_of)(partials[i].shape[dim] // (nz * nx)), axes,
            *buffers[3 * i : 3 * i + 3], outs[i],
        )
        for i, (dim, axes) in enumerate(modes)
    ]

    def main():
        me = layer.number(0)
        ports = [[wires.port() for _ in range(layer.count)] for _ in range(nz)]
        z_ports = [wires.port() for _ in range(nz)]
        order = [*range(1, nz), 0]
        own_copies = {}
        for s in order:
            for k in range(1, layer.count):
                layer.push(
                    wires, returned.at[layer.number(k), s], back.at[s, me], ports[s][k], k
                )
            own_copies[s] = load(returned.at[me, s], back.at[s, me])
        shared = group_sum_chain(wires, partial, own, other, came, load)
        next(shared)
        yield
        extended = back.shape[-1]
        total = None
        for s in order:
            for k in range(1, layer.count):
                wires.arrived(back.at[s, layer.number(k, -1)], ports[s][k], "z")
            own_copies[s].wait()
            term = dot(picks[s], back[s].reshape(picks.shape[2], extended))
            if s != 1:
                last = (s or nz) - 1
                yield
                wires.arrived(line.at[1, last - 1], z_ports[last], "z")
                term = term + line[1, last - 1].astype(wide)
            if s:
                line[0, s - 1] = term.astype(narrow)
                wires.push(line.at[0, s - 1], line.at[1, s - 1], z_ports[s], "z")
            else:
                total = term
            next(shared, None)
        for _ in shared:
            pass
        lanes = total[:, features:]
        gate_grad = lanes[:, :EXPERTS] + lanes[:, EXPERTS:]
        weight = gates[...]
        logit_grad = (
            weight * (gate_grad - jnp.sum(weight * gate_grad, axis=1, keepdims=True))
        ).astype(narrow)
        logit_out[...] = logit_grad
        mid = total[:, :features] + own[:, 0].astype(wide).reshape(rows, features)
        mid = mid + dot_nt(logit_grad, router[...])
        _, normed, inverse = norm_rows(residual[...], gain[...])
        grad = grads[...].astype(wide).reshape(rows, features)
        grad = grad + norm_input_back(mid, normed, inverse, gain[...])
        residual_grad_out[...] = grad
        own_grad[...] = grad.astype(narrow).reshape(grads.shape)
        gather = GroupGather(wires, own_grad, group_out)
        gather.start()
        mine = load(own_grad, group_out.at[:, 0, 0])
        gain_out[...] = jnp.sum(mid * normed, axis=0, keepdims=True)
        yield from gather.chain()
        mine.wait()

    def shared_sum():
        yield from group_sum_chain(wires, shared_partial, sh_own, sh_other, sh_came, load)
        shared_out[...] = sh_own[:, 0]

    first = main()
    next(first)
    for s in scatters:
        s.start(queue)
    queue.go(2)
    weave(first, [s.chain() for s in scatters] + [shared_sum()], 1)
    wires.drain()


def come_back(
    returned, partial, shared_partial, residual, gates, router, gain, grads, picks, partials, modes
):
    nz, nx, ny, nc = (lax.axis_size(a) for a in AXES)
    seqs, local_len, features = grads.shape
    rows = seqs * local_len
    shape = jax.ShapeDtypeStruct
    extended = returned.shape[-1]
    part = pltpu.VMEM((seqs, ny, local_len, features), narrow)
    shards = []
    for p, (dim, _) in zip(partials, modes):
        size = list(p.shape)
        size[dim] //= nz * nx
        shards.append(tuple(size))
    scratch = [
        part, part, part, part, part, part,
        pltpu.VMEM((nz, nx * ny * nc) + returned.shape[2:], narrow),
        pltpu.VMEM((2, nz - 1, rows, extended), narrow),
        pltpu.VMEM((seqs, local_len, features), narrow),
    ]
    for size, (_, axes) in zip(shards, modes):
        scratch += scatter_scratch(size, axes)
    scratch += [
        pltpu.SemaphoreType.DMA((256,)),
        pltpu.SemaphoreType.DMA((256,)),
        pltpu.SemaphoreType.DMA((96,)),
    ]
    return pl.pallas_call(
        functools.partial(return_kernel, modes=modes),
        out_shape=[
            shape((rows, features), wide),
            shape((seqs, ny, nc, local_len, features), narrow),
            shape((rows, EXPERTS), narrow),
            shape((1, features), wide),
            shape(grads.shape, narrow),
            *[shape(size, wide) for size in shards],
        ],
        in_specs=[ANY, ANY, ANY] + [VMEM] * 6 + [ANY] * len(partials),
        out_specs=[VMEM, ANY, VMEM, VMEM, VMEM] + [VMEM] * len(partials),
        scratch_shapes=scratch,
        compiler_params=pltpu.CompilerParams(
            collective_id=3, has_side_effects=True, vmem_limit_bytes=56 * 1024 * 1024
        ),
        cost_estimate=costs(100),
    )(returned, partial, shared_partial, residual, gates, router, gain, grads, picks, *partials)


def expert_kernel(
    rows_in, grads_in, wg, wu, wd, *rest, split, plan,
):
    count = len(plan)
    shards, rest = rest[:count], rest[count:]
    returned, outputs, gated, lin_gate, lin_up, *rest = rest
    wholes, rest = rest[:count], rest[count:]
    (
        rows, grads, bg, bu, bd, act, gated_buf, gate_buf, up_buf, dots,
        back_stage, out_stage, send, recv, local, turn,
    ) = rest
    nz, nx, ny, nc = (lax.axis_size(a) for a in AXES)
    nb = nz * nx
    layer = nx * ny * nc
    units, features, hidden = wg.shape
    first_unit = (
        (lax.axis_index("z") * nx + lax.axis_index("x")) * ny + lax.axis_index("y")
    ) * nc + lax.axis_index("core")
    first_unit = first_unit * units
    per = min(layer, max(1, 512 // (nz * SLOTS)))
    block = per * nz * SLOTS
    blocks = layer // per
    wires = Wires(send, recv)
    if count:
        greet(("z", "x"))
    used = []

    def load(src, dst):
        copy = pltpu.make_async_copy(src, dst, local.at[len(used)])
        used.append(copy)
        copy.start()
        return copy

    gathers = [
        BlockGather(
            wires, src, dst, (rows_of if dim == 0 else columns_of)(src.shape[dim]), x_first
        )
        for src, dst, (dim, x_first) in zip(shards, wholes, plan)
    ]

    def transfers():
        for g in gathers:
            g.forward(0, 0)
        yield
        plans = [g.rounds() for g in gathers]
        for step in range(max([len(p) for p in plans] + [0])):
            for g, p in zip(gathers, plans):
                for slot in p[step] if step < len(p) else []:
                    g.take(*slot)
                    yield

    moving = transfers()
    next(moving, None)

    def tick():
        next(moving, None)

    def fetch(a):
        slot = a % rows.shape[0]
        return [
            load(rows_in.at[:, :, a], rows.at[slot]),
            load(wg.at[a], bg.at[slot]),
            load(wu.at[a], bu.at[slot]),
            load(grads_in.at[:, :, a], grads.at[slot]),
            load(wd.at[a], bd.at[slot]),
        ]

    fetched = fetch(0)
    kept = [load(g.src, g.at(0, 0)) for g in gathers]

    def pump(low, high, body, copies):
        @pl.loop(low, high)
        def _(i):
            slot = lax.rem(i, 2)

            @pl.when(i >= 2)
            def _():
                for copy in copies(i - 2, slot):
                    copy.wait()

            body(i, slot)
            for copy in copies(i, slot):
                copy.start()

    def settle(total, copies):
        for i in range(max(0, total - 2), total):
            for copy in copies(i, i % 2):
                copy.wait()

    saved, extra_copy = [], None
    for a in range(units):
        slot_a = a % rows.shape[0]
        expert = (first_unit + a) // split
        for copy in fetched[:3]:
            copy.wait()
        waiting = fetched[3:]

        def weights_of(b):
            extra = rows[slot_a, pl.ds(b * per, per), :, :, features:].astype(wide)
            extra = extra.reshape(block, 2 * EXPERTS)
            lane = lax.broadcasted_iota(jnp.int32, extra.shape, 1)
            mine = (lane == expert) | (lane == expert + EXPERTS)
            return jnp.sum(jnp.where(mine, extra, 0.0), axis=1, keepdims=True)

        def row_block(ref, b, columns):
            return ref[slot_a, pl.ds(b * per, per), :, :, columns].reshape(block, -1)

        for copy in waiting:
            copy.wait()
        if a + 1 < units:
            fetched = fetch(a + 1)

        def forward(b, cols):
            span = pl.ds(pl.multiple_of(b * block, block), block)
            picked = row_block(rows, b, slice(0, features))
            lin = dot(picked, bg[slot_a, :, cols])
            up = dot(picked, bu[slot_a, :, cols])
            grad = dot_nt(row_block(grads, b, slice(None)), bd[slot_a, cols, :]) * weights_of(b)
            s = jax.nn.sigmoid(lin)
            silu = lin * s
            value = (silu * up).astype(narrow)
            act[span, cols] = value
            gated_buf[span, cols] = (value.astype(wide) * weights_of(b)).astype(narrow)
            gate_buf[span, cols] = (grad * up * (s * (1.0 + lin * (1.0 - s)))).astype(narrow)
            up_buf[span, cols] = (grad * silu).astype(narrow)

        full = hidden // 256
        for copy in saved:
            copy.wait()

        @pl.loop(0, blocks)
        def _(b):
            @pl.loop(0, full)
            def _(i):
                forward(b, pl.ds(pl.multiple_of(i * 256, 256), 256))

            if hidden % 256:
                forward(b, pl.ds(full * 256, hidden % 256))

        saved = [
            load(src, dst.at[a])
            for src, dst in ((gated_buf, gated), (gate_buf, lin_gate), (up_buf, lin_up))
        ]
        tick()
        tick()
        dots[...] = jnp.zeros(dots.shape, wide)

        def spread(i):
            return pl.ds(pl.multiple_of(i * 256, 256), 256)

        def back_copies(i, slot):
            return [
                pltpu.make_async_copy(
                    back_stage.at[slot], returned.at[:, :, a, :, spread(i)], turn.at[0, slot]
                ),
                pltpu.make_async_copy(
                    out_stage.at[slot], outputs.at[:, :, a, :, spread(i)], turn.at[1, slot]
                ),
            ]

        def backward(i, slot):
            @pl.loop(0, blocks)
            def _(b):
                span = pl.ds(pl.multiple_of(b * block, block), block)
                cols = spread(i)
                out = dot(act[span, :], bd[slot_a, :, cols])
                dots[span, :] += jnp.sum(
                    out * row_block(grads, b, cols).astype(wide), axis=1, keepdims=True
                )
                shaped = (per, nz, SLOTS, 256)
                out_stage[slot, pl.ds(b * per, per)] = (
                    (out * weights_of(b)).astype(narrow).reshape(shaped)
                )
                inward = dot_nt(gate_buf[span, :], bg[slot_a, cols, :]) + dot_nt(
                    up_buf[span, :], bu[slot_a, cols, :]
                )
                back_stage[slot, pl.ds(b * per, per)] = inward.astype(narrow).reshape(shaped)

        chunks = features // 256
        for part in range(4):
            pump(part * chunks // 4, (part + 1) * chunks // 4, backward, back_copies)
            tick()
        settle(chunks, back_copies)

        @pl.loop(0, blocks)
        def _(b):
            span = pl.ds(pl.multiple_of(b * block, block), block)
            lane = lax.broadcasted_iota(jnp.int32, (block, 2 * EXPERTS), 1)
            value = dots[span, :]
            high = value.astype(narrow).astype(wide)
            lanes = jnp.where(lane == expert, high, 0.0)
            lanes = jnp.where(lane == expert + EXPERTS, value - high, lanes)
            rest_ = lanes.astype(narrow).reshape(per, nz, SLOTS, 2 * EXPERTS)
            back_stage[0, pl.ds(b * per, per), :, :, : 2 * EXPERTS] = rest_

        extra_copy = load(
            back_stage.at[0, :, :, :, : 2 * EXPERTS], returned.at[:, :, a, :, features:]
        )
        extra_copy.wait()
    for copy in saved:
        copy.wait()
    for _ in moving:
        pass
    for copy in kept:
        copy.wait()
    wires.drain()


def run_experts(rows_in, grads_in, wg, wu, wd, shards, plan, split):
    nz, nx, ny, nc = (lax.axis_size(a) for a in AXES)
    nb = nz * nx
    units, features, hidden = wg.shape
    layer = nx * ny * nc
    total = nz * layer * SLOTS
    shape = jax.ShapeDtypeStruct
    extended = rows_in.shape[-1]

    slots = min(units, 2)
    lines = (layer, nz, SLOTS)
    return pl.pallas_call(
        functools.partial(expert_kernel, split=split, plan=plan),
        out_shape=[
            shape(rows_in.shape, narrow),
            shape(grads_in.shape, narrow),
            *[shape((units, total, hidden), narrow)] * 3,
            *[whole_array(w, dim) for w, (dim, _) in zip(shards, plan)],
        ],
        in_specs=[ANY] * (5 + len(shards)),
        out_specs=[ANY] * (5 + len(shards)),
        scratch_shapes=[
            pltpu.VMEM((slots,) + lines + (extended,), narrow),
            pltpu.VMEM((slots,) + lines + (features,), narrow),
            pltpu.VMEM((slots, features, hidden), narrow),
            pltpu.VMEM((slots, features, hidden), narrow),
            pltpu.VMEM((slots, hidden, features), narrow),
            pltpu.VMEM((total, hidden), narrow),
            pltpu.VMEM((total, hidden), narrow),
            pltpu.VMEM((total, hidden), narrow),
            pltpu.VMEM((total, hidden), narrow),
            pltpu.VMEM((total, 1), wide),
            pltpu.VMEM((2,) + lines + (256,), narrow),
            pltpu.VMEM((2,) + lines + (256,), narrow),
            pltpu.SemaphoreType.DMA((64,)),
            pltpu.SemaphoreType.DMA((64,)),
            pltpu.SemaphoreType.DMA((32,)),
            pltpu.SemaphoreType.DMA((4, 2)),
        ],
        compiler_params=pltpu.CompilerParams(
            collective_id=4 if shards else None, has_side_effects=bool(shards),
            vmem_limit_bytes=60 * 1024 * 1024,
        ),
        cost_estimate=costs(80),
    )(rows_in, grads_in, wg, wu, wd, *shards)


def unit_grads_kernel(rows, grads, gated, lin_gate, lin_up, gate_out, up_out, down_out):
    picked = rows[...].reshape(gated.shape[1], rows.shape[-1])
    gate_out[0] = dot_tn(picked, lin_gate[0])
    up_out[0] = dot_tn(picked, lin_up[0])
    down_out[0] = dot_tn(gated[0], grads[...].reshape(gated.shape[1], grads.shape[-1]))


def unit_grads(rows, grads, gated, lin_gate, lin_up):
    layer, nz, units, _, features = grads.shape
    _, total, hidden = gated.shape
    step = 512 if total <= 512 else 128
    lines = (layer, nz, 1, SLOTS, step)
    shape = jax.ShapeDtypeStruct
    line_spec = pl.BlockSpec(lines, lambda a, i: (0, 0, a, 0, i))
    unit_spec = pl.BlockSpec((1, total, hidden), lambda a, i: (a, 0, 0))
    wide_spec = pl.BlockSpec((1, step, hidden), lambda a, i: (a, i, 0))
    return pl.pallas_call(
        unit_grads_kernel,
        grid=(units, features // step),
        in_specs=[line_spec, line_spec, unit_spec, unit_spec, unit_spec],
        out_specs=[wide_spec, wide_spec, pl.BlockSpec((1, hidden, step), lambda a, i: (a, 0, i))],
        out_shape=[
            shape((units, features, hidden), wide),
            shape((units, features, hidden), wide),
            shape((units, hidden, features), wide),
        ],
        cost_estimate=costs(35),
        compiler_params=pltpu.CompilerParams(vmem_limit_bytes=61 * 1024 * 1024),
    )(rows, grads, gated, lin_gate, lin_up)


def per_device(
    tokens, attn_gain, w_query, w_latent, latent_gain, w_expand, w_output, ffn_gain, w_router,
    w_shared_gate, w_shared_up, w_shared_down, w_gate, w_up, w_down, routes, clip_limit, out_grad,
):
    seqs, local_len, features = tokens.shape
    rows = seqs * local_len
    qk = NOPE + RD
    nz, nx, ny, nc = (lax.axis_size(a) for a in ("z", "x", "y", "core"))
    zi, xi, yi, ci = (lax.axis_index(a) for a in ("z", "x", "y", "core"))
    nb, nu = nz * nx, ny * nc
    layer = nx * nu
    heads = H // nu
    group = nu * rows
    all_rows = nb * group
    upd = w_gate.shape[0]
    split = upd * nz * layer // EXPERTS
    scale = qk ** (-0.5)
    GROUP = ("y", "core")
    ALL = ("z", "x", "y", "core")
    LAYER = ("x", "y", "core")

    def scatter_blk(whole, dim):
        size = whole.shape[dim] // nb
        blocks = []
        for sz in range(nz):
            for sx in range(nx):
                owner = ((zi + nz - sz) % nz) * nx + (xi + nx - sx) % nx
                blocks.append(lax.dynamic_slice_in_dim(whole, owner * size, size, dim))
        return tree_sum(blocks, ("z", "x"))

    def group_gather(value):
        return jnp.concatenate(
            [p.reshape(seqs, local_len, -1) for p in flat_ring(value, GROUP)], axis=1
        ).reshape(group, -1)

    def group_scatter(value):
        blocks = value.reshape(seqs, nu, local_len, -1)
        return tree_sum([blocks[:, i].reshape(rows, -1) for i in range(nu)], GROUP)

    def group_sum(value):
        for axis in GROUP:
            items = ring(value, axis)
            value = sum(item.astype(wide) for item in items)
        return value

    def device_positions(blk, u):
        return (blk * nu + u) * local_len + jnp.arange(local_len, dtype=jnp.int32)

    local_pos = device_positions(zi * nx + xi, yi * nc + ci)
    group_pos = jnp.concatenate(
        [
            device_positions(zi * nx + xi, (yi + ny - sy) % ny * nc + (ci + nc - sc) % nc)
            for sy in range(ny)
            for sc in range(nc)
        ]
    )
    key_pos = jnp.concatenate(
        [
            device_positions(
                (zi + nz - sz) % nz * nx + (xi + nx - sx) % nx,
                (yi + ny - sy) % ny * nc + (ci + nc - sc) % nc,
            )
            for sc in range(nc)
            for sy in range(ny)
            for sx in range(nx)
            for sz in range(nz)
        ]
    )

    shard = attn_gain.shape[0]
    lat_len = latent_gain.shape[0]
    gains = jnp.concatenate(
        [
            jnp.pad(jnp.stack([attn_gain, ffn_gain]).astype(wide), ((0, 0), (0, KVR - shard))),
            lax.dynamic_update_slice(
                jnp.zeros((1, KVR), wide),
                latent_gain.astype(wide)[None],
                (0, (zi * nx + xi) * lat_len),
            ),
            jnp.zeros((5, KVR), wide),
        ],
        axis=0,
    )
    small = jnp.concatenate([w_latent, w_router], axis=1).reshape(nu, shard // nu, -1)
    route_rows = jnp.swapaxes(routes, 0, 1).reshape(rows, TOP)
    cos_local, sin_local = rotary_tables(jnp.tile(local_pos, seqs))
    (
        gains_all, small_all, query_w, expand_w, output_w,
        hidden_group, grad_group, picks, own_member, grad_slots, latents, _, latent_all,
    ) = start(
        tokens, out_grad, cos_local, sin_local, gains, small,
        jnp.pad(route_rows, ((0, 0), (0, 128 - TOP)), constant_values=-1),
        (w_query, w_expand, w_output), upd, split,
    )
    blk = ("z", "x")
    grad_slots, later_gate, later_up, later_down = lax.optimization_barrier(
        (grad_slots, w_shared_gate, w_shared_up, w_shared_down)
    )
    gate_w = lax.all_gather(later_gate, blk, axis=0, tiled=True)
    up_w = lax.all_gather(later_up, blk, axis=0, tiled=True)
    down_w = lax.all_gather(later_down, blk, axis=1, tiled=True)
    tokens_local = tokens.reshape(rows, features)
    grad_narrow = out_grad.reshape(rows, features)
    small_whole = small_all.reshape(features, -1)
    latent_w = small_whole[:, : KVR + RD]
    router_w = small_whole[:, KVR + RD :]
    gain_attn = gains_all[:, 0, :shard].reshape(-1)
    gain_ffn = gains_all[:, 1, :shard].reshape(-1)
    gain_latent = jnp.sum(gains_all[:, 2], axis=0)
    inputs = tokens_local.astype(wide)
    _, normed_in, inverse_in = norm_rows(inputs, gain_attn)
    _, normed_lat, inverse_lat = norm_rows(latent_all[:, :KVR], gain_latent)
    length = all_rows // seqs
    latent_keys = latents.reshape(seqs, length, KVR + NOPE)
    latent_rows = latents.reshape(all_rows, KVR + NOPE)
    expand_w = jnp.pad(expand_w, ((0, NOPE), (0, 0)))
    hidden_group = hidden_group.reshape(group, features)
    grad_group = grad_group.reshape(group, features)

    def swap_layer(values):
        return lax.all_to_all(values, LAYER, split_axis=0, concat_axis=0, tiled=True)

    grad_slots = swap_layer(grad_slots)

    reach = nu * local_len
    cos_group, sin_group = rotary_tables(group_pos)
    query_lin = dot(hidden_group, query_w)
    expanded = dot(latent_rows, expand_w, narrow)
    query_pos, keys_pos = group_pos[:, None], key_pos[None, :]
    query_rows, attended, stats = attend(
        query_lin, cos_group, sin_group, expanded, latent_keys, query_pos, keys_pos, seqs, heads
    )
    top = jnp.pad(jnp.max(stats[..., 0], axis=(0, 2))[None], ((0, 7), (0, 128 - heads)))
    split_group = (seqs, ny, nc, local_len, features)
    residual, gates, hidden_mid, hidden_mid_group, expert_slots, tops = dispatch(
        dot(attended, output_w, narrow).reshape(split_group),
        tokens, gain_ffn[None], router_w, own_member, picks, top, upd,
        (), (),
    )
    clip_value = clip_limit[0]
    clip_factor = clip_value / jnp.maximum(jnp.max(tops, axis=(0, 1))[0, :heads], clip_value)
    hidden_mid_group = hidden_mid_group.reshape(group, features)

    returned, outputs, gated, lin_gate, lin_up = run_experts(
        expert_slots, grad_slots, w_gate, w_up, w_down, (), (), split
    )

    shared_gate = dot(hidden_mid_group, gate_w)
    shared_up = dot(hidden_mid_group, up_w)
    shared_act = (jax.nn.silu(shared_gate) * shared_up).astype(narrow)
    shared_partial = dot(shared_act, down_w, narrow)
    shared_act_grad = dot_nt(grad_group, down_w)
    shared_gate_grad = (shared_act_grad * shared_up * silu_slope(shared_gate)).astype(narrow)
    shared_up_grad = (shared_act_grad * jax.nn.silu(shared_gate)).astype(narrow)
    mid_shared = dot_nt(shared_gate_grad, gate_w) + dot_nt(shared_up_grad, up_w)

    usual = ("x", "z")
    def spread_sum(value, dim):
        return lax.psum_scatter(value, blk, scatter_dimension=dim, tiled=True).astype(wide)

    shared_gate_wgrad, shared_up_wgrad, shared_down_wgrad, returned = lax.optimization_barrier(
        (
            dot_tn(hidden_mid_group, shared_gate_grad, narrow),
            dot_tn(hidden_mid_group, shared_up_grad, narrow),
            dot_tn(shared_act, grad_group, narrow),
            returned,
        )
    )
    shared_up_wgrad = spread_sum(shared_up_wgrad, 0)
    shared_down_wgrad = spread_sum(shared_down_wgrad, 1)
    (
        residual_grad, attn_grad, logit_grad, ffn_gain_part, shared_sum, shared_gate_wgrad,
    ) = come_back(
        returned, mid_shared.astype(narrow).reshape(split_group),
        shared_partial.reshape(split_group), residual, gates,
        router_w, gain_ffn[None], out_grad, picks,
        (shared_gate_wgrad,), ((0, usual),),
    )
    attn_grad = attn_grad.reshape(group, features)
    outputs, attn_grad = lax.optimization_barrier((outputs, attn_grad))
    outputs = swap_layer(outputs)
    attended_grad = dot_nt(attn_grad, output_w, narrow)
    attended_grad, shared_up_wgrad = lax.optimization_barrier((attended_grad, shared_up_wgrad))
    output_wgrad = dot_tn(attended, attn_grad, narrow)

    query_lin_grad, expand_grad, rope_partial = attend_back(
        query_rows, cos_group, sin_group, expanded, latent_keys, query_pos, keys_pos, stats,
        attended_grad, seqs, heads,
    )
    hidden_partial = dot_nt(query_lin_grad, query_w, narrow)
    latent_partial = (
        dot_nt(expand_grad, expand_w).reshape(seqs, length, KVR + NOPE)
        + jnp.pad(rope_partial, ((0, 0), (0, 0), (KVR, 0)))
    ).astype(narrow)
    latent_blocks = latent_partial.reshape(seqs, nc, ny, nx, nz, local_len, KVR + NOPE)
    latent_blocks = ring_sum([latent_blocks[:, i] for i in range(nc)], "core").astype(narrow)
    latent_blocks, gated, outputs = lax.optimization_barrier((latent_blocks, gated, outputs))
    gated, shared_down_wgrad = lax.optimization_barrier((gated, shared_down_wgrad))
    gate_wgrad, up_wgrad, down_wgrad = unit_grads(expert_slots, grad_slots, gated, lin_gate, lin_up)
    latent_blocks = ring_sum([latent_blocks[:, i] for i in range(ny)], "y").astype(narrow)
    hidden_blocks = hidden_partial.reshape(split_group)
    hidden_blocks = ring_sum([hidden_blocks[:, :, i] for i in range(nc)], "core").astype(narrow)
    hidden_sum = ring_sum([hidden_blocks[:, i] for i in range(ny)], "y").astype(narrow)
    query_wgrad = dot_tn(hidden_group, query_lin_grad, narrow)
    expand_wgrad = dot_tn(latent_rows, expand_grad, narrow)
    uly = yi * nc + ci
    hidden_sum, gate_wgrad, up_wgrad, down_wgrad = lax.optimization_barrier(
        (hidden_sum, gate_wgrad, up_wgrad, down_wgrad)
    )

    def own_columns(values):
        return lax.dynamic_slice_in_dim(
            values.T.reshape(nb, nu, shard // nu, group), uly, 1, 1
        ).reshape(features // nu, group)

    (
        tokens_grad, block_out, latent_wgrad, gain_sums, query_wgrad, expand_wgrad, output_wgrad,
    ) = finish(
        hidden_sum, latent_blocks,
        tokens, residual_grad, small_whole, own_columns(hidden_group), own_columns(hidden_mid_group),
        logit_grad, ffn_gain_part, gain_attn[None], gain_latent[None],
        latent_all, cos_local, sin_local, residual,
        shared_sum, picks, outputs,
        (query_wgrad, expand_wgrad[:KVR], output_wgrad),
        ((0, usual), (0, usual), (1, usual)),
    )
    width = KVR + RD
    small_wgrad = latent_wgrad.reshape(shard, -1)
    latent_wgrad, router_wgrad = small_wgrad[:, :width], small_wgrad[:, width:]
    ffn_gain_grad = jnp.sum(gain_sums[:, 1, :shard], axis=0)
    gain_sums = jnp.sum(gain_sums[:, 0], axis=0)
    attn_gain_grad = gain_sums[:shard]
    latent_gain_grad = lax.dynamic_slice_in_dim(
        gain_sums, shard + (zi * nx + xi) * lat_len, lat_len, 0
    )
    return (
        block_out,
        tokens_grad,
        attn_gain_grad,
        query_wgrad,
        latent_wgrad,
        latent_gain_grad,
        expand_wgrad,
        output_wgrad,
        ffn_gain_grad,
        router_wgrad,
        shared_gate_wgrad,
        shared_up_wgrad,
        shared_down_wgrad,
        gate_wgrad,
        up_wgrad,
        down_wgrad,
        clip_factor,
    )


def solution(mesh):
    blocks, group = mesh.shape["blk"], mesh.shape["ulysses"]
    chips = Mesh(
        mesh.devices.reshape(Z_SIZE, blocks // Z_SIZE, group // CORES, CORES),
        ("z", "x", "y", "core"),
    )
    blk, uly, every = ("z", "x"), ("y", "core"), ("z", "x", "y", "core")
    rows = P(None, every, None)
    unit = P(every, None, None)
    return jax.shard_map(
        per_device,
        mesh=chips,
        in_specs=(
            rows, P(blk), P(blk, uly), P(blk, None), P(blk), P(blk, uly), P(uly, blk), P(blk),
            P(blk, None), P(blk, uly), P(blk, uly), P(uly, blk), unit, unit, unit, unit, P(), rows,
        ),
        out_specs=(
            rows, rows, P(blk), P(blk, uly), P(blk, None), P(blk), P(blk, uly), P(uly, blk), P(blk),
            P(blk, None), P(blk, uly), P(blk, uly), P(uly, blk), unit, unit, unit, P(uly),
        ),
        check_vma=False,
    )
```

```python
import functools

import jax
import jax.numpy as jnp
from jax import lax
from jax.experimental import pallas as pl
from jax.experimental.pallas import tpu as pltpu
from jax.sharding import Mesh
from jax.sharding import PartitionSpec as P

H = 16
NOPE = 128
RD = 64
VH = 128
KVR = 512
EXPERTS = 64
TOP = 6
CAP = 14
SLOTS = 16
HEAD_START = 12
Z_SIZE = 4
CORES = 2

epsilon = 1e-06
rope_base = 10000.0
wide = jnp.float32
narrow = jnp.bfloat16


def dot(a, b, out=wide):
    return jnp.dot(a, b, preferred_element_type=out)


def dot_tn(a, b, out=wide):
    return lax.dot_general(a, b, (((0,), (0,)), ((), ())), preferred_element_type=out)


def dot_nt(a, b, out=wide):
    return lax.dot_general(a, b, (((1,), (1,)), ((), ())), preferred_element_type=out)


def norm_rows(values, gain):
    inverse = lax.rsqrt(jnp.mean(values * values, axis=-1, keepdims=True) + epsilon)
    normed = values * inverse
    return (normed * gain, normed, inverse)


def norm_input_back(grad_out, normed, inverse, gain):
    scaled = grad_out * gain
    return inverse * (scaled - normed * jnp.mean(scaled * normed, axis=-1, keepdims=True))


def rotary_tables(positions):
    half_width = RD // 2
    frequency = rope_base ** (-2.0 * jnp.arange(half_width).astype(wide) / RD)
    angles = positions.astype(wide)[:, None] * frequency[None, :]
    return (jnp.cos(angles), jnp.sin(angles))


def rotate(values, cosine, sine):
    half = RD // 2
    a, b = values[..., :half], values[..., half:]
    return jnp.concatenate([a * cosine - b * sine, b * cosine + a * sine], axis=-1)


def unrotate(values, cosine, sine):
    half = RD // 2
    a, b = values[..., :half], values[..., half:]
    return jnp.concatenate([a * cosine + b * sine, b * cosine - a * sine], axis=-1)


def silu_slope(values):
    s = jax.nn.sigmoid(values)
    return s * (1.0 + values * (1.0 - s))


def hop(value, axis):
    n = lax.axis_size(axis)
    return lax.ppermute(value, axis, [(i, (i + 1) % n) for i in range(n)])


def ring(value, axis):
    items = [value]
    for _ in range(lax.axis_size(axis) - 1):
        items.append(hop(items[-1], axis))
    return items


def ring_sum(blocks, axis):
    n = lax.axis_size(axis)
    if n == 1:
        return blocks[0].astype(wide)
    running = hop(blocks[1].astype(narrow), axis)
    for s in range(2, n):
        running = hop((running.astype(wide) + blocks[s].astype(wide)).astype(narrow), axis)
    return running.astype(wide) + blocks[0].astype(wide)


def flat_ring(value, axes):
    items = [value]
    for axis in axes:
        items = [piece for item in items for piece in ring(item, axis)]
    return items


def tree_sum(blocks, axes):
    for axis in reversed(axes):
        n = lax.axis_size(axis)
        blocks = [ring_sum(blocks[i : i + n], axis) for i in range(0, len(blocks), n)]
    return blocks[0]


ANY = pl.BlockSpec(memory_space=pl.ANY)
VMEM = pl.BlockSpec(memory_space=pltpu.VMEM)
MESH = pl.DeviceIdType.MESH
AXES = ("z", "x", "y", "core")


def behind(axis, steps):
    n = lax.axis_size(axis)
    return lax.rem(lax.axis_index(axis) + (n - steps), n)


def ahead(axis):
    n = lax.axis_size(axis)
    return lax.rem(lax.axis_index(axis) + 1, n)


def greet(axes):
    barrier = pltpu.get_barrier_semaphore()
    for axis in axes:
        pl.semaphore_signal(
            barrier, inc=1, device_id={axis: behind(axis, 1)}, device_id_type=MESH
        )
    pl.semaphore_wait(barrier, len(axes))


class Wires:
    def __init__(self, send, recv):
        self.send, self.recv, self.used, self.sent = send, recv, 0, []

    def port(self):
        self.used += 1
        return self.used - 1

    def push(self, src, dst, port, axis):
        copy = pltpu.make_async_remote_copy(
            src_ref=src,
            dst_ref=dst,
            send_sem=self.send.at[port],
            recv_sem=self.recv.at[port],
            device_id={axis: ahead(axis)},
            device_id_type=MESH,
        )
        copy.start()
        self.sent.append(copy)

    def arrived(self, dst, port, axis):
        pltpu.make_async_remote_copy(
            src_ref=dst,
            dst_ref=dst,
            send_sem=self.send.at[port],
            recv_sem=self.recv.at[port],
            device_id={axis: ahead(axis)},
            device_id_type=MESH,
        ).wait_recv()

    def drain(self):
        for copy in self.sent:
            copy.wait_send()


class BlockGather:
    def __init__(self, wires, src, dst, place, x_first):
        self.wires, self.src, self.dst, self.place, self.x_first = wires, src, dst, place, x_first
        self.nz, self.nx = lax.axis_size("z"), lax.axis_size("x")
        self.ports = {
            (sz, sx): wires.port() for sz in range(self.nz) for sx in range(self.nx) if sz or sx
        }

    def at(self, sz, sx):
        return self.place(self.dst, behind("z", sz) * self.nx + behind("x", sx))

    def forward(self, sz, sx):
        src = self.src if sz == 0 and sx == 0 else self.at(sz, sx)
        if self.x_first:
            go_x, go_z = sz == 0, True
        else:
            go_x, go_z = True, sx == 0
        if go_z and sz + 1 < self.nz:
            self.wires.push(src, self.at(sz, sx), self.ports[sz + 1, sx], "z")
        if go_x and sx + 1 < self.nx:
            self.wires.push(src, self.at(sz, sx), self.ports[sz, sx + 1], "x")

    def take(self, sz, sx):
        from_x = sx > 0 and (sz == 0 if self.x_first else True)
        self.wires.arrived(self.at(sz, sx), self.ports[sz, sx], "x" if from_x else "z")
        self.forward(sz, sx)

    def chain(self):
        self.forward(0, 0)
        for slots in self.rounds():
            for slot in slots:
                yield
                self.take(*slot)

    def rounds(self):
        if self.x_first:
            order = [[(0, sx)] for sx in range(1, self.nx)]
            order += [[(sz, sx) for sx in range(self.nx)] for sz in range(1, self.nz)]
            return order
        last = [[(sz, sx) for sz in range(self.nz)] for sx in range(1, self.nx)]
        return [[(sz, 0)] for sz in range(1, self.nz)] + last


def rows_of(size):
    return lambda ref, owner: ref.at[pl.ds(pl.multiple_of(owner * size, size), size)]


def columns_of(size):
    return lambda ref, owner: ref.at[:, pl.ds(pl.multiple_of(owner * size, size), size)]


def start_kernel(
    tokens, grads, cosine, sine, gains, small, routes, w_query, w_expand, w_output,
    gains_out, small_out, query_out, expand_out, output_out,
    group_out, grads_out, picks_out, member_out, slots_out, latents_out, hidden_out, latent_all_out,
    own_latent, own_hidden, routes_line, grads_line, send, recv, local, *, units, split,
):
    nz, nx, ny, nc = (lax.axis_size(a) for a in AXES)
    nb, nu = nz * nx, ny * nc
    me = lax.axis_index("z") * nx + lax.axis_index("x")
    uly = lax.axis_index("y") * nc + lax.axis_index("core")
    seqs, local_len, features = tokens.shape
    rows = seqs * local_len
    greet(AXES)
    wires = Wires(send, recv)
    used, waited = [], set()

    def load(src, dst):
        copy = pltpu.make_async_copy(src, dst, local.at[len(used)])
        used.append(copy)
        copy.start()
        return copy

    def member(sy, sc):
        return behind("y", sy) * nc + behind("core", sc)

    def line_chain(src, dst):
        ports = [wires.port() for _ in range(nz)]
        wires.push(src, dst.at[1], ports[1], "z")
        mine = load(src, dst.at[0])
        for sz in range(1, nz):
            yield
            wires.arrived(dst.at[sz], ports[sz], "z")
            if sz + 1 < nz:
                wires.push(dst.at[sz], dst.at[sz + 1], ports[sz + 1], "z")
        mine.wait()
        waited.add(id(mine))

    def main():
        g_gains = BlockGather(wires, gains, gains_out, lambda ref, owner: ref.at[owner], False)
        g_small = BlockGather(
            wires, small.at[uly], small_out, lambda ref, owner: ref.at[owner, uly], False
        )
        slots = [(0, 0)] + [slot for r in g_small.rounds() for slot in r]
        y_ports = {(slot, sy): wires.port() for slot in slots for sy in range(1, ny)}
        c_ports = {(slot, sy): wires.port() for slot in slots for sy in range(ny)}

        def piece(slot, sy, sc):
            owner = behind("z", slot[0]) * nx + behind("x", slot[1])
            return small_out.at[owner, member(sy, sc)]

        def spread(slot):
            here = piece(slot, 0, 0)
            if ny > 1:
                wires.push(here, here, y_ports[slot, 1], "y")
            wires.push(here, here, c_ports[slot, 0], "core")

        g_small.forward(0, 0)
        g_gains.forward(0, 0)
        mine = [load(small.at[uly], small_out.at[me, uly]), load(gains, gains_out.at[me])]
        yield
        for slots_now in g_small.rounds():
            for slot in slots_now:
                yield
                g_small.take(*slot)
                if mine:
                    for copy in mine:
                        copy.wait()
                    waited.update(id(copy) for copy in mine)
                    mine = []
                    spread((0, 0))
                spread(slot)
                g_gains.take(*slot)
        for sy in range(1, ny):
            for slot in slots:
                yield
                here = piece(slot, sy, 0)
                wires.arrived(here, y_ports[slot, sy], "y")
                if sy + 1 < ny:
                    wires.push(here, here, y_ports[slot, sy + 1], "y")
                wires.push(here, here, c_ports[slot, sy], "core")
        for sy in range(ny):
            for slot in slots:
                wires.arrived(piece(slot, sy, 1), c_ports[slot, sy], "core")
        gain = jnp.concatenate([gains_out[b, 0:1, : features // nb] for b in range(nb)], axis=1)
        latent_gain = sum(gains_out[b, 2:3, :] for b in range(nb))
        x = tokens[...].astype(wide).reshape(rows, features)
        hidden = norm_rows(x, gain)[0].astype(narrow)
        hidden_out[...] = hidden
        own_hidden[...] = hidden.reshape(tokens.shape)
        spread_hidden = GroupGather(wires, own_hidden, group_out)
        spread_hidden.start()
        load(own_hidden, group_out.at[:, 0, 0])
        width = small_out.shape[-1]
        latent_all = dot(hidden, small_out[...].reshape(features, width))[:, : KVR + RD]
        latent_all_out[...] = latent_all
        latent = norm_rows(latent_all[:, :KVR], latent_gain)[0]
        rope = rotate(latent_all[:, KVR:], cosine[...], sine[...])
        own_latent[:, :, KVR:] = jnp.zeros((seqs, local_len, NOPE), narrow)
        own_latent[:, :, :KVR] = latent.astype(narrow).reshape(seqs, local_len, KVR)
        own_latent[:, :, KVR : KVR + RD] = rope.astype(narrow).reshape(seqs, local_len, RD)
        z_ports = [wires.port() for _ in range(nz)]
        x_ports = [wires.port() for _ in range(nx)]
        yx_ports = [[wires.port() for _ in range(nx)] for _ in range(ny)]
        cx_ports = [[wires.port() for _ in range(nx)] for _ in range(ny)]
        wires.push(own_latent, latents_out.at[:, 0, 0, 0, 1], z_ports[1], "z")
        own_place = load(own_latent, latents_out.at[:, 0, 0, 0, 0])
        for sz in range(1, nz):
            yield
            here = latents_out.at[:, 0, 0, 0, sz]
            wires.arrived(here, z_ports[sz], "z")
            if sz + 1 < nz:
                wires.push(here, latents_out.at[:, 0, 0, 0, sz + 1], z_ports[sz + 1], "z")
        own_place.wait()
        waited.add(id(own_place))
        for sx in range(nx):
            block = latents_out.at[:, 0, 0, sx]
            if sx:
                yield
                wires.arrived(block, x_ports[sx], "x")
            if sx + 1 < nx:
                wires.push(block, latents_out.at[:, 0, 0, sx + 1], x_ports[sx + 1], "x")
            if ny > 1:
                wires.push(block, latents_out.at[:, 0, 1, sx], yx_ports[1][sx], "y")
            wires.push(block, latents_out.at[:, 1, 0, sx], cx_ports[0][sx], "core")
        for sy in range(1, ny):
            for sx in range(nx):
                yield
                block = latents_out.at[:, 0, sy, sx]
                wires.arrived(block, yx_ports[sy][sx], "y")
                if sy + 1 < ny:
                    wires.push(block, latents_out.at[:, 0, sy + 1, sx], yx_ports[sy + 1][sx], "y")
                wires.push(block, latents_out.at[:, 1, sy, sx], cx_ports[sy][sx], "core")
        for sy in range(ny):
            for sx in range(nx):
                yield
                wires.arrived(latents_out.at[:, 1, sy, sx], cx_ports[sy][sx], "core")
        yield from spread_hidden.chain()

    def slots_chain():
        yield from line_chain(routes, routes_line)
        yield from line_chain(grads, grads_line)
        count = rows
        earlier = (
            lax.broadcasted_iota(jnp.int32, (count, count), 1)
            < lax.broadcasted_iota(jnp.int32, (count, count), 0)
        ).astype(narrow)
        columns = picks_out.shape[-1]
        expert = lax.broadcasted_iota(jnp.int32, (EXPERTS, columns), 0)
        column = lax.broadcasted_iota(jnp.int32, (EXPERTS, columns), 1)
        unit = column // SLOTS
        if split > 1:
            unit = unit // split
        chosen = (expert == unit + lax.axis_index("z") * (EXPERTS // nz)).astype(narrow)
        slot = lax.rem(lax.broadcasted_iota(jnp.int32, (count, columns), 1), SLOTS)
        names = lax.broadcasted_iota(jnp.int32, (count, EXPERTS), 1)
        for s in range(nz):
            member = sum(
                (routes_line[s, :, j : j + 1] == names).astype(wide) for j in range(TOP)
            )
            if s == 0:
                member_out[...] = member
            rank = dot(earlier, member.astype(narrow))
            code = jnp.where(member > 0, rank, -1.0).astype(narrow)
            pick = (dot(code, chosen) == slot.astype(wide)).astype(narrow)
            picks_out[s] = pick
            row_grads = grads_line[s].reshape(rows, features)
            shaped = (slots_out.shape[0],) + slots_out.shape[2:]
            slots_out[:, s] = dot_tn(pick, row_grads).astype(narrow).reshape(shaped)

    def group_chain(src, dst):
        gather = GroupGather(wires, src, dst)
        gather.start()
        load(src, dst.at[:, 0, 0])
        yield from gather.chain()

    def array_chain(src, dst, place, x_first):
        gather = BlockGather(wires, src, dst, place, x_first)
        load(src, gather.at(0, 0))
        yield from gather.chain()

    first = main()
    next(first)
    others = [
        slots_chain(),
        array_chain(w_query, query_out, rows_of(w_query.shape[0]), False),
        array_chain(w_expand, expand_out, rows_of(w_expand.shape[0]), False),
        array_chain(w_output, output_out, columns_of(w_output.shape[1]), False),
        group_chain(grads, grads_out),
    ]
    for _ in range(HEAD_START):
        next(first)
    weave(first, others, 3)
    wires.drain()
    for copy in used:
        if id(copy) not in waited:
            copy.wait()


def start(tokens, grads, cosine, sine, gains, small, routes, weights, units, split):
    nz, nx, ny, nc = (lax.axis_size(a) for a in AXES)
    nb, nu = nz * nx, ny * nc
    seqs, local_len, features = tokens.shape
    shape = jax.ShapeDtypeStruct

    def whole(w, dim):
        size = list(w.shape)
        size[dim] *= nb
        return shape(tuple(size), w.dtype)

    rows = seqs * local_len
    grouped = (seqs, ny, nc, local_len, features)
    outs = [
        shape((nb,) + gains.shape, wide),
        shape((nb,) + small.shape, narrow),
        *[whole(w, d) for w, d in zip(weights, (0, 0, 1))],
        shape(grouped, narrow),
        shape(grouped, narrow),
        shape((nz, rows, nx * nu * units * SLOTS), narrow),
        shape((rows, EXPERTS), wide),
        shape((nx * nu, nz, units, SLOTS, features), narrow),
        shape((seqs, nc, ny, nx, nz, local_len, KVR + NOPE), narrow),
        shape((seqs * local_len, features), narrow),
        shape((seqs * local_len, KVR + RD), wide),
    ]
    return pl.pallas_call(
        functools.partial(start_kernel, units=units, split=split),
        out_shape=outs,
        in_specs=[VMEM, ANY, VMEM, VMEM, VMEM, VMEM, VMEM] + [ANY] * 3,
        out_specs=[VMEM, VMEM] + [ANY] * 5 + [VMEM] * 3 + [ANY] + [VMEM, VMEM],
        scratch_shapes=[
            pltpu.VMEM((seqs, local_len, KVR + NOPE), narrow),
            pltpu.VMEM(tokens.shape, narrow),
            pltpu.VMEM((nz,) + routes.shape, routes.dtype),
            pltpu.VMEM((nz,) + grads.shape, narrow),
            pltpu.SemaphoreType.DMA((384,)),
            pltpu.SemaphoreType.DMA((384,)),
            pltpu.SemaphoreType.DMA((16,)),
        ],
        compiler_params=pltpu.CompilerParams(
            collective_id=0, has_side_effects=True, vmem_limit_bytes=40 * 1024 * 1024
        ),
        cost_estimate=costs(120),
    )(tokens, grads, cosine, sine, gains, small, routes, *weights)


def scores_of(query, keys, rope, scale):
    return (dot_nt(query[:, :NOPE], keys) + dot_nt(query[:, NOPE:], rope)) * scale


def attend_kernel(
    query, cosine, sine, keys, rope, query_pos, key_pos, query_out, attended, stats, head_lin,
    *, scale, sub,
):
    qk = NOPE + RD
    for head in range(query.shape[1] // qk):

        @pl.when(pl.program_id(1) == head)
        def _(head=head):
            head_lin[:, :qk] = query[:, head * qk : (head + 1) * qk]

    keys_ = keys[:, :NOPE]
    values = keys[:, NOPE:]

    @pl.loop(0, query.shape[0], step=sub)
    def _(first):
        span = pl.ds(pl.multiple_of(first, sub), sub)
        lin = head_lin[span, :]
        turned = rotate(lin[:, NOPE : NOPE + RD], cosine[span, :], sine[span, :])
        query_out[span, :NOPE] = lin[:, :NOPE].astype(narrow)
        query_out[span, NOPE:] = jnp.zeros((sub, NOPE), narrow)
        query_out[span, NOPE : NOPE + RD] = turned.astype(narrow)
        scores = scores_of(query_out[span, :], keys_, rope[0], scale)
        scores = jnp.where(key_pos[...] <= query_pos[span, :], scores, -jnp.inf)
        top = jnp.max(scores, axis=1, keepdims=True)
        raised = jnp.exp(scores - top)
        total = jnp.sum(raised, axis=1, keepdims=True)
        probability = (raised * (1.0 / total)).astype(narrow)
        attended[span, :] = dot(probability, values).astype(narrow)
        stats[0, 0, span, 0:1] = top
        stats[0, 0, span, 1:2] = top + jnp.log(total)


def attend_back_kernel(
    query, cosine, sine, keys, rope, query_pos, key_pos, stats, grads,
    query_grad, expand_grad, rope_grad, key_acc, *, scale, sub,
):
    keys_ = keys[:, :NOPE]
    values = keys[:, NOPE:]
    key_acc[...] = jnp.zeros(key_acc.shape, wide)

    @pl.loop(0, query.shape[0], step=sub)
    def _(first):
        span = pl.ds(pl.multiple_of(first, sub), sub)
        rows = query[span, :]
        scores = scores_of(rows, keys_, rope[0], scale)
        scores = jnp.where(key_pos[...] <= query_pos[span, :], scores, -jnp.inf)
        probability = jnp.exp(scores - stats[0, 0, span, 1:2])
        grad = grads[span, :]
        prob_grad = dot_nt(grad, values)
        weighted = probability * prob_grad
        delta = jnp.sum(weighted, axis=1, keepdims=True)
        score_grad = ((weighted - probability * delta) * scale).astype(narrow)
        back_plain = dot(score_grad, keys_).astype(narrow)
        back_turned = dot(score_grad, rope[0])[:, :RD].astype(narrow).astype(wide)
        turned = unrotate(back_turned, cosine[span, :], sine[span, :]).astype(narrow)
        head_grad = jnp.concatenate([back_plain, turned], axis=1)
        qk = NOPE + RD
        for head in range(query_grad.shape[1] // qk):

            @pl.when(pl.program_id(1) == head)
            def _(head=head):
                query_grad[span, head * qk : (head + 1) * qk] = head_grad

        key_acc[:, : 2 * NOPE] += dot_tn(score_grad, rows)
        key_acc[:, 2 * NOPE :] += dot_tn(probability.astype(narrow), grad)

    expand_grad[:, :NOPE] = key_acc[:, :NOPE].astype(narrow)
    expand_grad[:, NOPE:] = key_acc[:, 2 * NOPE :].astype(narrow)

    @pl.when(pl.program_id(1) == 0)
    def _():
        rope_grad[0] = key_acc[:, NOPE : 2 * NOPE]

    @pl.when(pl.program_id(1) > 0)
    def _():
        rope_grad[0] += key_acc[:, NOPE : 2 * NOPE]


def attention_specs(seqs, heads, reach, length):
    both = NOPE + VH
    return dict(
        query=pl.BlockSpec((reach, both), lambda s, h: (s, h)),
        heads=pl.BlockSpec((reach, heads * (NOPE + RD)), lambda s, h: (s, 0)),
        rope_grad=pl.BlockSpec((1, length, NOPE), lambda s, h: (s, 0, 0)),
        table=pl.BlockSpec((reach, RD // 2), lambda s, h: (0, 0)),
        keys=pl.BlockSpec((length, both), lambda s, h: (s, h)),
        rope=pl.BlockSpec((1, length, NOPE), lambda s, h: (s, 0, KVR // NOPE)),
        query_pos=pl.BlockSpec((reach, 1), lambda s, h: (0, 0)),
        key_pos=pl.BlockSpec((1, length), lambda s, h: (0, 0)),
        head=pl.BlockSpec((reach, VH), lambda s, h: (s, h)),
        stats=pl.BlockSpec((1, 1, reach, 2), lambda s, h: (s, h, 0, 0)),
    )


def attend(query_lin, cosine, sine, keys, rope, query_pos, key_pos, seqs, heads):
    reach, length = query_pos.shape[0], key_pos.shape[1]
    sub = min(reach, max(16, 256 * 2048 // length))
    sp = attention_specs(seqs, heads, reach, length)
    shape = jax.ShapeDtypeStruct
    return pl.pallas_call(
        functools.partial(attend_kernel, scale=(NOPE + RD) ** -0.5, sub=sub),
        grid=(seqs, heads),
        in_specs=[sp[k] for k in ("heads", "table", "table", "keys", "rope", "query_pos", "key_pos")],
        out_specs=[sp["query"], sp["head"], sp["stats"]],
        out_shape=[
            shape((seqs * reach, heads * 2 * NOPE), narrow),
            shape((seqs * reach, heads * VH), narrow),
            shape((seqs, heads, reach, 2), wide),
        ],
        scratch_shapes=[pltpu.VMEM((reach, 2 * NOPE), wide)],
        cost_estimate=costs(16),
        compiler_params=pltpu.CompilerParams(vmem_limit_bytes=61 * 1024 * 1024),
    )(query_lin, cosine, sine, keys, rope, query_pos, key_pos)


def attend_back(query, cosine, sine, keys, rope, query_pos, key_pos, stats, grads, seqs, heads):
    reach, length = query_pos.shape[0], key_pos.shape[1]
    sub = min(reach, max(16, 256 * 2048 // length))
    sp = attention_specs(seqs, heads, reach, length)
    shape = jax.ShapeDtypeStruct
    return pl.pallas_call(
        functools.partial(attend_back_kernel, scale=(NOPE + RD) ** -0.5, sub=sub),
        grid=(seqs, heads),
        in_specs=[
            sp[k]
            for k in (
                "query", "table", "table", "keys", "rope", "query_pos", "key_pos", "stats", "head",
            )
        ],
        out_specs=[sp["heads"], sp["keys"], sp["rope_grad"]],
        cost_estimate=costs(25),
        out_shape=[
            shape((seqs * reach, heads * (NOPE + RD)), narrow),
            shape(keys.shape, narrow),
            shape((seqs, length, NOPE), wide),
        ],
        scratch_shapes=[pltpu.VMEM((length, 2 * NOPE + VH), wide)],
        compiler_params=pltpu.CompilerParams(vmem_limit_bytes=61 * 1024 * 1024),
    )(query, cosine, sine, keys, rope, query_pos, key_pos, stats, grads)


def costs(us):
    return pl.CostEstimate(flops=int(us * 1e9), bytes_accessed=int(us * 1e6), transcendentals=0)


def add_into(target, *terms):
    lead, count = target.shape[:-2], target.shape[-2]
    step = 32 if count % 32 == 0 else 16 if count % 16 == 0 else count
    pieces = count // step
    total = pieces
    for size in lead:
        total *= size

    @pl.loop(0, total)
    def _(i):
        at = []
        rest = i // pieces
        for size in reversed(lead):
            at.insert(0, lax.rem(rest, size))
            rest = rest // size
        span = pl.ds(pl.multiple_of(lax.rem(i, pieces) * step, step), step)
        place = (*at, span, slice(None))
        target[place] = sum(term[place].astype(wide) for term in terms).astype(target.dtype)


class Queue:
    def __init__(self):
        self.items = []

    def add(self, place, thunk):
        self.items.append((place, len(self.items), thunk))
        self.items.sort(key=lambda item: item[:2])

    def go(self, count):
        for _, _, thunk in self.items[:count]:
            thunk()
        del self.items[:count]


class BlockScatter:
    def __init__(self, wires, loads, src, place, axes, acc, first, second, out):
        self.wires, self.loads, self.src, self.place, self.axes = wires, loads, src, place, axes
        self.acc, self.first, self.second, self.out = acc, first, second, out
        self.na, self.nb = (lax.axis_size(a) for a in axes)
        self.ports = {
            (a, b): wires.port() for b in range(self.nb) for a in range(self.na) if a or b
        }
        self.order = [*range(1, self.nb), 0]

    def mine(self, a, b):
        steps = dict(zip(self.axes, (a, b)))
        owner = behind("z", steps["z"]) * lax.axis_size("x") + behind("x", steps["x"])
        return self.place(self.src, owner)

    def slot(self, a, b):
        return self.acc.at[b, max(a - 1, 0)]

    def start(self, queue=None):
        self.loading, self.queue = {}, queue or Queue()
        for place, b in enumerate(self.order):
            self.queue.add(
                place,
                lambda b=b: self.wires.push(
                    self.mine(1, b), self.first.at[b, 0], self.ports[1, b], self.axes[0]
                ),
            )
        if queue is None:
            self.queue.go(self.nb)
        for b in self.order:
            for a in [*range(2, self.na), 0]:
                self.loading[a, b] = self.loads(self.mine(a, b), self.slot(a, b))

    def chain(self):
        wires, (axis_a, axis_b) = self.wires, self.axes
        for b in self.order:
            for a in [*range(2, self.na), 0]:
                came = self.first.at[b, (a or self.na) - 2]
                yield
                wires.arrived(came, self.ports[(a or self.na) - 1, b], axis_a)
                if not a:
                    self.queue.go(1)
                self.loading[a, b].wait()
                add_into(self.slot(a, b), self.slot(a, b), came)
                if a:
                    wires.push(self.slot(a, b), self.first.at[b, a - 1], self.ports[a, b], axis_a)
            if b >= 2:
                yield
                wires.arrived(self.second.at[b - 2], self.ports[0, b - 1], axis_b)
                add_into(self.slot(0, b), self.slot(0, b), self.second.at[b - 2])
            if b >= 1:
                wires.push(self.slot(0, b), self.second.at[b - 1], self.ports[0, b], axis_b)
        yield
        wires.arrived(self.second.at[self.nb - 2], self.ports[0, self.nb - 1], axis_b)
        add_into(self.out, self.slot(0, 0), self.second.at[self.nb - 2])


def scatter_scratch(shard, axes, dtype=narrow):
    na, nb = (lax.axis_size(a) for a in axes)
    return [
        pltpu.VMEM((nb, na - 1) + shard, dtype),
        pltpu.VMEM((nb, na - 1) + shard, dtype),
        pltpu.VMEM((nb - 1,) + shard, dtype),
    ]


class GroupGather:
    def __init__(self, wires, src, dst):
        self.wires, self.src, self.dst = wires, src, dst
        self.ny, self.nc = lax.axis_size("y"), lax.axis_size("core")
        self.ports = [wires.port() for _ in range(self.ny * self.nc)]

    def start(self):
        if self.ny > 1:
            self.wires.push(self.src, self.dst.at[:, 1, 0], self.ports[self.nc], "y")
        self.wires.push(self.src, self.dst.at[:, 0, 1], self.ports[1], "core")

    def chain(self):
        wires, dst, nc = self.wires, self.dst, self.nc
        for sy in range(1, self.ny):
            piece = dst.at[:, sy, 0]
            yield
            wires.arrived(piece, self.ports[sy * nc], "y")
            if sy + 1 < self.ny:
                wires.push(piece, dst.at[:, sy + 1, 0], self.ports[(sy + 1) * nc], "y")
            wires.push(piece, dst.at[:, sy, 1], self.ports[sy * nc + 1], "core")
        for sy in range(self.ny):
            yield
            wires.arrived(dst.at[:, sy, 1], self.ports[sy * nc + 1], "core")


def group_sum_chain(wires, src, own, other, came, load):
    ny = lax.axis_size("y")
    core_ports = [wires.port() for _ in range(ny)]
    y_ports = [wires.port() for _ in range(ny)]
    order = [*range(1, ny), 0]
    for sy in order:
        wires.push(src.at[:, sy, 1], other.at[:, sy], core_ports[sy], "core")
    loading = [load(src.at[:, sy, 0], own.at[:, sy]) for sy in range(ny)]
    for sy in order:
        yield
        wires.arrived(other.at[:, sy], core_ports[sy], "core")
        loading[sy].wait()
        add_into(own.at[:, sy], own.at[:, sy], other.at[:, sy])
        if ny > 1:
            last = (sy or ny) - 1
            if last:
                yield
                wires.arrived(came.at[:, last - 1], y_ports[last], "y")
                add_into(own.at[:, sy], own.at[:, sy], came.at[:, last - 1])
            if sy:
                wires.push(own.at[:, sy], came.at[:, sy - 1], y_ports[sy], "y")


def weave(main, others, share):
    others = list(others)
    running = True
    while running or others:
        if running:
            running = next(main, True) is None
        for _ in range(share if running else max(1, len(others))):
            if others:
                chain = others.pop(0)
                if next(chain, True) is None:
                    others.append(chain)


def finish_kernel(
    hidden_sum, latent_partial, tokens, residual_grad, small, hidden_t, mid_t, logit_grad,
    ffn_gain, gain_attn, gain_latent, latent_all, cosine, sine, residual, shared_sum, picks, slots,
    *rest, modes,
):
    count = len(modes)
    partials, rest = rest[:count], rest[count:]
    tokens_grad, block_out, latent_w_out, gains_out, *rest = rest
    outs, rest = rest[:count], rest[count:]
    (
        lat_own, lat_x, lat_z,
        own_lag, lag_group, wide_acc, lat_wgrad, gain_terms, routed_slots, routed_own, routed_came, *rest,
    ) = rest
    buffers, rest = rest[: 3 * count], rest[3 * count :]
    lw_buffers, g_buffers = rest[:3], rest[3:6]
    send, recv, local = rest[6:]
    nz, nx, ny, nc = (lax.axis_size(a) for a in AXES)
    nb, nu = nz * nx, ny * nc
    uly = lax.axis_index("y") * nc + lax.axis_index("core")
    seqs, local_len, features = tokens.shape
    rows = seqs * local_len
    greet(AXES)
    wires = Wires(send, recv)
    used = []

    def load(src, dst):
        copy = pltpu.make_async_copy(src, dst, local.at[len(used)])
        used.append(copy)
        copy.start()
        return copy

    def blocks_of(size, dim):
        return rows_of(size) if dim == 0 else columns_of(size)

    scatters = [
        BlockScatter(
            wires, load, partials[i], blocks_of(partials[i].shape[dim] // nb, dim), axes,
            *buffers[3 * i : 3 * i + 3], outs[i],
        )
        for i, (dim, axes) in enumerate(modes)
    ]

    def routed_chain():
        ports = [wires.port() for _ in range(nz)]
        loading = {s: load(slots.at[:, s], routed_slots.at[s]) for s in [*range(1, nz), 0]}
        for s in [*range(1, nz), 0]:
            own = routed_own.at[s]
            last = (s or nz) - 1
            yield
            loading[s].wait()
            term = dot(picks[s], routed_slots[s].reshape(picks.shape[2], features))
            routed_own[s] = term.astype(narrow)
            if last:
                wires.arrived(routed_came.at[last - 1], ports[last], "z")
                add_into(own, own, routed_came.at[last - 1])
            if s:
                wires.push(own, routed_came.at[s - 1], ports[s], "z")

    def output_chain():
        yield from routed_chain()
        total = residual[...] + shared_sum[...].astype(wide).reshape(rows, features)
        total = total + routed_own[0].astype(wide)
        block_out[...] = total.astype(narrow).reshape(tokens.shape)

    def latent_chain():
        x_ports = [wires.port() for _ in range(nx)]
        z_ports = [wires.port() for _ in range(nz)]
        wires.push(latent_partial.at[:, 1], lat_x.at[:, 0], x_ports[1], "x")
        order_x = [*range(2, nx), 0]
        loading = {sx: load(latent_partial.at[:, sx], lat_own.at[:, sx]) for sx in order_x}
        yield
        for sx in order_x:
            own, last = lat_own.at[:, sx], (sx or nx) - 1
            yield
            wires.arrived(lat_x.at[:, last - 1], x_ports[last], "x")
            loading[sx].wait()
            add_into(own, own, lat_x.at[:, last - 1])
            if sx:
                wires.push(own, lat_x.at[:, sx - 1], x_ports[sx], "x")
        for sz in [*range(1, nz), 0]:
            own = lat_own.at[:, 0, sz]
            last = (sz or nz) - 1
            if last:
                yield
                wires.arrived(lat_z.at[:, last - 1], z_ports[last], "z")
                add_into(own, own, lat_z.at[:, last - 1])
            if sz:
                wires.push(own, lat_z.at[:, sz - 1], z_ports[sz], "z")

    def main():
        latent = latent_chain()
        next(latent)
        for s in scatters:
            s.start(queue)
        queue.go(3)
        yield
        for _ in latent:
            yield
        width = KVR + RD
        lat = lat_own[:, 0, 0].astype(wide).reshape(rows, KVR + NOPE)[:, :width]
        latent_grad = lat[:, :KVR]
        _, normed, inverse = norm_rows(latent_all[:, :KVR], gain_latent[...])
        lat_in = norm_input_back(latent_grad, normed, inverse, gain_latent[...])
        turned = unrotate(lat[:, KVR:], cosine[...], sine[...])
        own_lag[:, :, KVR:] = jnp.zeros((seqs, local_len, own_lag.shape[-1] - KVR), narrow)
        own_lag[:, :, :KVR] = lat_in.astype(narrow).reshape(seqs, local_len, KVR)
        own_lag[:, :, KVR:width] = turned.astype(narrow).reshape(seqs, local_len, RD)
        wide_acc[...] = dot_nt(own_lag[...].reshape(rows, own_lag.shape[-1]), small[...])
        own_lag[:, :, width:] = logit_grad[...].reshape(seqs, local_len, EXPERTS)
        lag_gather = GroupGather(wires, own_lag, lag_group)
        lag_gather.start()
        own_copy = load(own_lag, lag_group.at[:, 0, 0])
        x = tokens[...].astype(wide).reshape(rows, features)
        _, normed_in, inverse_in = norm_rows(x, gain_attn[...])
        hidden_grad = wide_acc[...] + hidden_sum[...].astype(wide).reshape(rows, features)
        wide_acc[...] = residual_grad[...] + norm_input_back(
            hidden_grad, normed_in, inverse_in, gain_attn[...]
        )
        attn_gain = jnp.sum(hidden_grad * normed_in, axis=0, keepdims=True)
        latent_gain = jnp.sum(latent_grad * normed, axis=0, keepdims=True)
        tokens_grad[...] = wide_acc[...].astype(narrow).reshape(tokens.shape)
        shard = features // nb
        gain_terms[...] = jnp.zeros(gain_terms.shape, wide)
        for b in range(nb):
            gain_terms[b, 0:1, :shard] = attn_gain[:, b * shard : (b + 1) * shard]
            gain_terms[b, 0:1, shard:] = latent_gain
            gain_terms[b, 1:2, :shard] = ffn_gain[:, b * shard : (b + 1) * shard]
        gain_sum = BlockScatter(
            wires, load, gain_terms, lambda ref, owner: ref.at[owner], ("x", "z"), *g_buffers,
            gains_out.at[uly],
        )
        gain_sum.start()
        for _ in lag_gather.chain():
            yield
        own_copy.wait()
        lags = lag_group[...].reshape(nu * rows, own_lag.shape[-1])
        terms = dot(hidden_t[...], lags).astype(narrow)
        lat_wgrad[...] = terms.reshape(lat_wgrad.shape)
        terms = dot(mid_t[...], lags)[:, width:].astype(narrow)
        lat_wgrad[:, :, width:] = terms.reshape(lat_wgrad.shape[:2] + (EXPERTS,))
        w_sum = BlockScatter(
            wires, load, lat_wgrad, lambda ref, owner: ref.at[owner], ("x", "z"), *lw_buffers,
            latent_w_out.at[uly],
        )
        w_sum.start()
        chains = [gain_sum.chain(), w_sum.chain()]
        while chains:
            chain = chains.pop(0)
            if next(chain, True) is None:
                chains.append(chain)
                yield
        outs_ = (latent_w_out, gains_out)
        y_ports = [[wires.port() for _ in range(ny)] for _ in outs_]
        c_ports = [[wires.port() for _ in range(ny)] for _ in outs_]
        member = lambda sy, sc: behind("y", sy) * nc + behind("core", sc)
        for ref, yp, cp in zip(outs_, y_ports, c_ports):
            here = ref.at[uly]
            if ny > 1:
                wires.push(here, here, yp[1], "y")
            wires.push(here, here, cp[0], "core")
        for sy in range(1, ny):
            for ref, yp, cp in zip(outs_, y_ports, c_ports):
                piece = ref.at[member(sy, 0)]
                yield
                wires.arrived(piece, yp[sy], "y")
                if sy + 1 < ny:
                    wires.push(piece, piece, yp[sy + 1], "y")
                wires.push(piece, piece, cp[sy], "core")
        for sy in range(ny):
            for ref, cp in zip(outs_, c_ports):
                yield
                wires.arrived(ref.at[member(sy, 1)], cp[sy], "core")

    queue = Queue()
    weave(main(), [s.chain() for s in scatters] + [output_chain()], 1)
    wires.drain()


def finish(
    hidden_sum, latent_partial, tokens, residual_grad, small, hidden_t, mid_t, logit_grad,
    ffn_gain, gain_attn, gain_latent, latent_all, cosine, sine, residual, shared_sum, picks, slots,
    partials, modes,
):
    nz, nx, ny, nc = (lax.axis_size(a) for a in AXES)
    nb, nu = nz * nx, ny * nc
    seqs, local_len, features = tokens.shape
    rows = seqs * local_len
    shape = jax.ShapeDtypeStruct
    shards = []
    for p, (dim, _) in zip(partials, modes):
        size = list(p.shape)
        size[dim] //= nb
        shards.append(tuple(size))
    width, shard = KVR + RD, features // nb
    padded = small.shape[-1]
    few = lambda n: max(n - 1, 1)
    scratch = [
        pltpu.VMEM((seqs, nx, nz, local_len, KVR + NOPE), narrow),
        pltpu.VMEM((seqs, few(nx), nz, local_len, KVR + NOPE), narrow),
        pltpu.VMEM((seqs, few(nz), local_len, KVR + NOPE), narrow),
        pltpu.VMEM((seqs, local_len, padded), narrow),
        pltpu.VMEM((seqs, ny, nc, local_len, padded), narrow),
        pltpu.VMEM((rows, features), wide),
        pltpu.VMEM((nb, shard // nu, padded), narrow),
        pltpu.VMEM((nb, 8, shard + KVR), wide),
        pltpu.VMEM((nz, nx * nu, *slots.shape[2:]), narrow),
        pltpu.VMEM((nz, rows, features), narrow),
        pltpu.VMEM((few(nz), rows, features), narrow),
    ]
    for size, (_, axes) in zip(shards, modes):
        scratch += scatter_scratch(size, axes)
    scratch += scatter_scratch((shard // nu, padded), ("x", "z"))
    scratch += scatter_scratch((8, shard + KVR), ("x", "z"), wide)
    scratch += [
        pltpu.SemaphoreType.DMA((256,)),
        pltpu.SemaphoreType.DMA((256,)),
        pltpu.SemaphoreType.DMA((256,)),
    ]
    return pl.pallas_call(
        functools.partial(finish_kernel, modes=modes),
        out_shape=[
            shape(tokens.shape, narrow),
            shape(tokens.shape, narrow),
            shape((nu, shard // nu, padded), wide),
            shape((nu, 8, shard + KVR), wide),
            *[shape(size, wide) for size in shards],
        ],
        in_specs=[VMEM, ANY] + [VMEM] * 15 + [ANY] * (1 + len(partials)),
        out_specs=[VMEM] * (4 + len(partials)),
        scratch_shapes=scratch,
        compiler_params=pltpu.CompilerParams(
            collective_id=1, has_side_effects=True, vmem_limit_bytes=62 * 1024 * 1024
        ),
        cost_estimate=costs(190),
    )(
        hidden_sum, latent_partial, tokens, residual_grad, small, hidden_t, mid_t, logit_grad,
        ffn_gain, gain_attn, gain_latent, latent_all, cosine, sine, residual, shared_sum, picks, slots,
        *partials,
    )


class Layer:
    def __init__(self):
        self.sizes = [lax.axis_size(a) for a in AXES[1:]]
        self.count = self.sizes[0] * self.sizes[1] * self.sizes[2]

    def offsets(self, k):
        _, ny, nc = self.sizes
        return k // (ny * nc), k // nc % ny, k % nc

    def device(self, k, sign=1):
        return {
            axis: lax.rem(lax.axis_index(axis) + (sign * d) % n, n)
            for axis, d, n in zip(AXES[1:], self.offsets(k), self.sizes)
        }

    def number(self, k, sign=1):
        where = self.device(k, sign)
        return (where["x"] * self.sizes[1] + where["y"]) * self.sizes[2] + where["core"]

    def greet(self):
        barrier = pltpu.get_barrier_semaphore()
        for k in range(1, self.count):
            pl.semaphore_signal(barrier, inc=1, device_id=self.device(k), device_id_type=MESH)
        pl.semaphore_signal(
            barrier, inc=1, device_id={"z": behind("z", 1)}, device_id_type=MESH
        )
        pl.semaphore_wait(barrier, self.count)

    def push(self, wires, src, dst, port, k):
        copy = pltpu.make_async_remote_copy(
            src_ref=src,
            dst_ref=dst,
            send_sem=wires.send.at[port],
            recv_sem=wires.recv.at[port],
            device_id=self.device(k),
            device_id_type=MESH,
        )
        copy.start()
        wires.sent.append(copy)


def dispatch_kernel(
    partial, tokens, gain, router, member, picks, top, *rest, plan,
):
    count = len(plan)
    shards, rest = rest[:count], rest[count:]
    residual_out, gates_out, hidden_out, group_out, rows_out, tops_out, *rest = rest
    wholes, rest = rest[:count], rest[count:]
    own, other, came, hidden, line, outgoing, send, recv, local = rest
    nz, nx = lax.axis_size("z"), lax.axis_size("x")
    seqs, local_len, features = tokens.shape
    rows = seqs * local_len
    layer = Layer()
    layer.greet()
    wires = Wires(send, recv)
    used, waited = [], set()

    def load(src, dst):
        copy = pltpu.make_async_copy(src, dst, local.at[len(used)])
        used.append(copy)
        copy.start()
        return copy

    def main():
        for _ in group_sum_chain(wires, partial, own, other, came, load):
            yield
        waited.update(id(copy) for copy in used[: own.shape[1]])
        residual = tokens[...].astype(wide).reshape(rows, features)
        residual = residual + own[:, 0].astype(wide).reshape(rows, features)
        residual_out[...] = residual
        normed = norm_rows(residual, gain[...])[0].astype(narrow)
        hidden_out[...] = normed
        hidden[...] = normed.reshape(tokens.shape)
        line[0, :, :features] = normed
        logits = jnp.where(member[...] > 0, dot(normed, router[...]), -jnp.inf)
        raised = jnp.exp(logits - jnp.max(logits, axis=1, keepdims=True))
        gates = raised / jnp.sum(raised, axis=1, keepdims=True)
        gates_out[...] = gates
        high = gates.astype(narrow).astype(wide)
        line[0, :, features:] = jnp.concatenate([high, gates - high], axis=1).astype(narrow)
        z_ports = [wires.port() for _ in range(nz)]
        wires.push(line.at[0], line.at[1], z_ports[1], "z")
        gather = GroupGather(wires, hidden, group_out)
        gather.start()
        load(hidden, group_out.at[:, 0, 0])
        ports = [[wires.port() for _ in range(layer.count)] for _ in range(nz)]
        me = layer.number(0)
        chain = gather.chain()
        for s in range(nz):
            if s:
                yield
                wires.arrived(line.at[s], z_ports[s], "z")
                if s + 1 < nz:
                    wires.push(line.at[s], line.at[s + 1], z_ports[s + 1], "z")
            outgoing[s] = dot_tn(picks[s], line[s]).astype(narrow).reshape(outgoing.shape[1:])
            for k in range(1, layer.count):
                target = layer.number(k)
                layer.push(wires, outgoing.at[s, target], rows_out.at[me, s], ports[s][k], k)
            load(outgoing.at[s, me], rows_out.at[me, s])
            next(chain, None)
        for _ in chain:
            pass
        for s in range(nz):
            yield
            for k in range(1, layer.count):
                wires.arrived(rows_out.at[layer.number(k, -1), s], ports[s][k], "z")

    def tops():
        z_ports = [wires.port() for _ in range(nz)]
        x_ports = [wires.port() for _ in range(nx)]
        mine = load(top, tops_out.at[0, 0])
        waited.add(id(mine))
        wires.push(top, tops_out.at[0, 1], z_ports[1], "z")
        for s in range(1, nz):
            yield
            wires.arrived(tops_out.at[0, s], z_ports[s], "z")
            if s + 1 < nz:
                wires.push(tops_out.at[0, s], tops_out.at[0, s + 1], z_ports[s + 1], "z")
        mine.wait()
        wires.push(tops_out.at[0], tops_out.at[1], x_ports[1], "x")
        for s in range(1, nx):
            yield
            wires.arrived(tops_out.at[s], x_ports[s], "x")
            if s + 1 < nx:
                wires.push(tops_out.at[s], tops_out.at[s + 1], x_ports[s + 1], "x")

    def array_chain(src, dst, dim, x_first):
        place = (rows_of if dim == 0 else columns_of)(src.shape[dim])
        gather = BlockGather(wires, src, dst, place, x_first)
        load(src, gather.at(0, 0))
        yield from gather.chain()

    first = main()
    next(first)
    others = [array_chain(a, b, *mode) for a, b, mode in zip(shards, wholes, plan)]
    weave(first, others + [tops()], 1)
    for copy in used:
        if id(copy) not in waited:
            copy.wait()
    wires.drain()


def whole_array(w, dim):
    size = list(w.shape)
    size[dim] *= lax.axis_size("z") * lax.axis_size("x")
    return jax.ShapeDtypeStruct(tuple(size), w.dtype)


def dispatch(partial, tokens, gain, router, member, picks, top, units, shards, plan):
    nz, nx, ny, nc = (lax.axis_size(a) for a in AXES)
    seqs, local_len, features = tokens.shape
    rows = seqs * local_len
    layer = nx * ny * nc
    shape = jax.ShapeDtypeStruct
    extended = features + 2 * EXPERTS
    part = pltpu.VMEM((seqs, ny, local_len, features), narrow)
    return pl.pallas_call(
        functools.partial(dispatch_kernel, plan=plan),
        out_shape=[
            shape((rows, features), wide),
            shape((rows, EXPERTS), wide),
            shape((rows, features), narrow),
            shape((seqs, ny, nc, local_len, features), narrow),
            shape((layer, nz, units, SLOTS, extended), narrow),
            shape((nx, nz) + top.shape, wide),
            *[whole_array(w, dim) for w, (dim, _) in zip(shards, plan)],
        ],
        in_specs=[ANY] + [VMEM] * 6 + [ANY] * len(shards),
        out_specs=[VMEM, VMEM, VMEM, ANY, ANY, VMEM] + [ANY] * len(shards),
        scratch_shapes=[
            part, part, part,
            pltpu.VMEM((seqs, local_len, features), narrow),
            pltpu.VMEM((nz, rows, extended), narrow),
            pltpu.VMEM((nz, layer, units, SLOTS, extended), narrow),
            pltpu.SemaphoreType.DMA((256,)),
            pltpu.SemaphoreType.DMA((256,)),
            pltpu.SemaphoreType.DMA((32,)),
        ],
        compiler_params=pltpu.CompilerParams(
            collective_id=2, has_side_effects=True, vmem_limit_bytes=48 * 1024 * 1024
        ),
        cost_estimate=costs(80),
    )(partial, tokens, gain, router, member, picks, top, *shards)


def return_kernel(
    returned, partial, shared_partial, residual, gates, router, gain, grads, picks, *rest, modes,
):
    count = len(modes)
    partials, rest = rest[:count], rest[count:]
    residual_grad_out, group_out, logit_out, gain_out, shared_out, *rest = rest
    outs, rest = rest[:count], rest[count:]
    own, other, came, sh_own, sh_other, sh_came, back, line, own_grad, *rest = rest
    buffers, rest = rest[: 3 * count], rest[3 * count :]
    send, recv, local = rest
    nz, nx = lax.axis_size("z"), lax.axis_size("x")
    seqs, local_len, features = grads.shape
    rows = seqs * local_len
    layer = Layer()
    layer.greet()
    wires = Wires(send, recv)
    used = []

    def load(src, dst):
        copy = pltpu.make_async_copy(src, dst, local.at[len(used)])
        used.append(copy)
        copy.start()
        return copy

    queue = Queue()
    scatters = [
        BlockScatter(
            wires, load, partials[i],
            (rows_of if dim == 0 else columns_of)(partials[i].shape[dim] // (nz * nx)), axes,
            *buffers[3 * i : 3 * i + 3], outs[i],
        )
        for i, (dim, axes) in enumerate(modes)
    ]

    def main():
        me = layer.number(0)
        ports = [[wires.port() for _ in range(layer.count)] for _ in range(nz)]
        z_ports = [wires.port() for _ in range(nz)]
        order = [*range(1, nz), 0]
        own_copies = {}
        for s in order:
            for k in range(1, layer.count):
                layer.push(
                    wires, returned.at[layer.number(k), s], back.at[s, me], ports[s][k], k
                )
            own_copies[s] = load(returned.at[me, s], back.at[s, me])
        shared = group_sum_chain(wires, partial, own, other, came, load)
        next(shared)
        yield
        extended = back.shape[-1]
        total = None
        for s in order:
            for k in range(1, layer.count):
                wires.arrived(back.at[s, layer.number(k, -1)], ports[s][k], "z")
            own_copies[s].wait()
            term = dot(picks[s], back[s].reshape(picks.shape[2], extended))
            if s != 1:
                last = (s or nz) - 1
                yield
                wires.arrived(line.at[1, last - 1], z_ports[last], "z")
                term = term + line[1, last - 1].astype(wide)
            if s:
                line[0, s - 1] = term.astype(narrow)
                wires.push(line.at[0, s - 1], line.at[1, s - 1], z_ports[s], "z")
            else:
                total = term
            next(shared, None)
        for _ in shared:
            pass
        lanes = total[:, features:]
        gate_grad = lanes[:, :EXPERTS] + lanes[:, EXPERTS:]
        weight = gates[...]
        logit_grad = (
            weight * (gate_grad - jnp.sum(weight * gate_grad, axis=1, keepdims=True))
        ).astype(narrow)
        logit_out[...] = logit_grad
        mid = total[:, :features] + own[:, 0].astype(wide).reshape(rows, features)
        mid = mid + dot_nt(logit_grad, router[...])
        _, normed, inverse = norm_rows(residual[...], gain[...])
        grad = grads[...].astype(wide).reshape(rows, features)
        grad = grad + norm_input_back(mid, normed, inverse, gain[...])
        residual_grad_out[...] = grad
        own_grad[...] = grad.astype(narrow).reshape(grads.shape)
        gather = GroupGather(wires, own_grad, group_out)
        gather.start()
        mine = load(own_grad, group_out.at[:, 0, 0])
        gain_out[...] = jnp.sum(mid * normed, axis=0, keepdims=True)
        yield from gather.chain()
        mine.wait()

    def shared_sum():
        yield from group_sum_chain(wires, shared_partial, sh_own, sh_other, sh_came, load)
        shared_out[...] = sh_own[:, 0]

    first = main()
    next(first)
    for s in scatters:
        s.start(queue)
    queue.go(2)
    weave(first, [s.chain() for s in scatters] + [shared_sum()], 1)
    wires.drain()


def come_back(
    returned, partial, shared_partial, residual, gates, router, gain, grads, picks, partials, modes
):
    nz, nx, ny, nc = (lax.axis_size(a) for a in AXES)
    seqs, local_len, features = grads.shape
    rows = seqs * local_len
    shape = jax.ShapeDtypeStruct
    extended = returned.shape[-1]
    part = pltpu.VMEM((seqs, ny, local_len, features), narrow)
    shards = []
    for p, (dim, _) in zip(partials, modes):
        size = list(p.shape)
        size[dim] //= nz * nx
        shards.append(tuple(size))
    scratch = [
        part, part, part, part, part, part,
        pltpu.VMEM((nz, nx * ny * nc) + returned.shape[2:], narrow),
        pltpu.VMEM((2, nz - 1, rows, extended), narrow),
        pltpu.VMEM((seqs, local_len, features), narrow),
    ]
    for size, (_, axes) in zip(shards, modes):
        scratch += scatter_scratch(size, axes)
    scratch += [
        pltpu.SemaphoreType.DMA((256,)),
        pltpu.SemaphoreType.DMA((256,)),
        pltpu.SemaphoreType.DMA((96,)),
    ]
    return pl.pallas_call(
        functools.partial(return_kernel, modes=modes),
        out_shape=[
            shape((rows, features), wide),
            shape((seqs, ny, nc, local_len, features), narrow),
            shape((rows, EXPERTS), narrow),
            shape((1, features), wide),
            shape(grads.shape, narrow),
            *[shape(size, wide) for size in shards],
        ],
        in_specs=[ANY, ANY, ANY] + [VMEM] * 6 + [ANY] * len(partials),
        out_specs=[VMEM, ANY, VMEM, VMEM, VMEM] + [VMEM] * len(partials),
        scratch_shapes=scratch,
        compiler_params=pltpu.CompilerParams(
            collective_id=3, has_side_effects=True, vmem_limit_bytes=56 * 1024 * 1024
        ),
        cost_estimate=costs(100),
    )(returned, partial, shared_partial, residual, gates, router, gain, grads, picks, *partials)


def expert_kernel(
    rows_in, grads_in, wg, wu, wd, *rest, split, plan,
):
    count = len(plan)
    shards, rest = rest[:count], rest[count:]
    returned, outputs, gated, lin_gate, lin_up, *rest = rest
    wholes, rest = rest[:count], rest[count:]
    (
        rows, grads, bg, bu, bd, act, gated_buf, gate_buf, up_buf, dots,
        back_stage, out_stage, send, recv, local, turn,
    ) = rest
    nz, nx, ny, nc = (lax.axis_size(a) for a in AXES)
    nb = nz * nx
    layer = nx * ny * nc
    units, features, hidden = wg.shape
    first_unit = (
        (lax.axis_index("z") * nx + lax.axis_index("x")) * ny + lax.axis_index("y")
    ) * nc + lax.axis_index("core")
    first_unit = first_unit * units
    per = min(layer, max(1, 512 // (nz * SLOTS)))
    block = per * nz * SLOTS
    blocks = layer // per
    wires = Wires(send, recv)
    if count:
        greet(("z", "x"))
    used = []

    def load(src, dst):
        copy = pltpu.make_async_copy(src, dst, local.at[len(used)])
        used.append(copy)
        copy.start()
        return copy

    gathers = [
        BlockGather(
            wires, src, dst, (rows_of if dim == 0 else columns_of)(src.shape[dim]), x_first
        )
        for src, dst, (dim, x_first) in zip(shards, wholes, plan)
    ]

    def transfers():
        for g in gathers:
            g.forward(0, 0)
        yield
        plans = [g.rounds() for g in gathers]
        for step in range(max([len(p) for p in plans] + [0])):
            for g, p in zip(gathers, plans):
                for slot in p[step] if step < len(p) else []:
                    g.take(*slot)
                    yield

    moving = transfers()
    next(moving, None)

    def tick():
        next(moving, None)

    def fetch(a):
        slot = a % rows.shape[0]
        return [
            load(rows_in.at[:, :, a], rows.at[slot]),
            load(wg.at[a], bg.at[slot]),
            load(wu.at[a], bu.at[slot]),
            load(grads_in.at[:, :, a], grads.at[slot]),
            load(wd.at[a], bd.at[slot]),
        ]

    fetched = fetch(0)
    kept = [load(g.src, g.at(0, 0)) for g in gathers]

    def pump(low, high, body, copies):
        @pl.loop(low, high)
        def _(i):
            slot = lax.rem(i, 2)

            @pl.when(i >= 2)
            def _():
                for copy in copies(i - 2, slot):
                    copy.wait()

            body(i, slot)
            for copy in copies(i, slot):
                copy.start()

    def settle(total, copies):
        for i in range(max(0, total - 2), total):
            for copy in copies(i, i % 2):
                copy.wait()

    saved, extra_copy = [], None
    for a in range(units):
        slot_a = a % rows.shape[0]
        expert = (first_unit + a) // split
        for copy in fetched[:3]:
            copy.wait()
        waiting = fetched[3:]

        def weights_of(b):
            extra = rows[slot_a, pl.ds(b * per, per), :, :, features:].astype(wide)
            extra = extra.reshape(block, 2 * EXPERTS)
            lane = lax.broadcasted_iota(jnp.int32, extra.shape, 1)
            mine = (lane == expert) | (lane == expert + EXPERTS)
            return jnp.sum(jnp.where(mine, extra, 0.0), axis=1, keepdims=True)

        def row_block(ref, b, columns):
            return ref[slot_a, pl.ds(b * per, per), :, :, columns].reshape(block, -1)

        for copy in waiting:
            copy.wait()
        if a + 1 < units:
            fetched = fetch(a + 1)

        def forward(b, cols):
            span = pl.ds(pl.multiple_of(b * block, block), block)
            picked = row_block(rows, b, slice(0, features))
            lin = dot(picked, bg[slot_a, :, cols])
            up = dot(picked, bu[slot_a, :, cols])
            grad = dot_nt(row_block(grads, b, slice(None)), bd[slot_a, cols, :]) * weights_of(b)
            s = jax.nn.sigmoid(lin)
            silu = lin * s
            value = (silu * up).astype(narrow)
            act[span, cols] = value
            gated_buf[span, cols] = (value.astype(wide) * weights_of(b)).astype(narrow)
            gate_buf[span, cols] = (grad * up * (s * (1.0 + lin * (1.0 - s)))).astype(narrow)
            up_buf[span, cols] = (grad * silu).astype(narrow)

        full = hidden // 256
        for copy in saved:
            copy.wait()

        @pl.loop(0, blocks)
        def _(b):
            @pl.loop(0, full)
            def _(i):
                forward(b, pl.ds(pl.multiple_of(i * 256, 256), 256))

            if hidden % 256:
                forward(b, pl.ds(full * 256, hidden % 256))

        saved = [
            load(src, dst.at[a])
            for src, dst in ((gated_buf, gated), (gate_buf, lin_gate), (up_buf, lin_up))
        ]
        tick()
        tick()
        dots[...] = jnp.zeros(dots.shape, wide)

        def spread(i):
            return pl.ds(pl.multiple_of(i * 256, 256), 256)

        def back_copies(i, slot):
            return [
                pltpu.make_async_copy(
                    back_stage.at[slot], returned.at[:, :, a, :, spread(i)], turn.at[0, slot]
                ),
                pltpu.make_async_copy(
                    out_stage.at[slot], outputs.at[:, :, a, :, spread(i)], turn.at[1, slot]
                ),
            ]

        def backward(i, slot):
            @pl.loop(0, blocks)
            def _(b):
                span = pl.ds(pl.multiple_of(b * block, block), block)
                cols = spread(i)
                out = dot(act[span, :], bd[slot_a, :, cols])
                dots[span, :] += jnp.sum(
                    out * row_block(grads, b, cols).astype(wide), axis=1, keepdims=True
                )
                shaped = (per, nz, SLOTS, 256)
                out_stage[slot, pl.ds(b * per, per)] = (
                    (out * weights_of(b)).astype(narrow).reshape(shaped)
                )
                inward = dot_nt(gate_buf[span, :], bg[slot_a, cols, :]) + dot_nt(
                    up_buf[span, :], bu[slot_a, cols, :]
                )
                back_stage[slot, pl.ds(b * per, per)] = inward.astype(narrow).reshape(shaped)

        chunks = features // 256
        for part in range(4):
            pump(part * chunks // 4, (part + 1) * chunks // 4, backward, back_copies)
            tick()
        settle(chunks, back_copies)

        @pl.loop(0, blocks)
        def _(b):
            span = pl.ds(pl.multiple_of(b * block, block), block)
            lane = lax.broadcasted_iota(jnp.int32, (block, 2 * EXPERTS), 1)
            value = dots[span, :]
            high = value.astype(narrow).astype(wide)
            lanes = jnp.where(lane == expert, high, 0.0)
            lanes = jnp.where(lane == expert + EXPERTS, value - high, lanes)
            rest_ = lanes.astype(narrow).reshape(per, nz, SLOTS, 2 * EXPERTS)
            back_stage[0, pl.ds(b * per, per), :, :, : 2 * EXPERTS] = rest_

        extra_copy = load(
            back_stage.at[0, :, :, :, : 2 * EXPERTS], returned.at[:, :, a, :, features:]
        )
        extra_copy.wait()
    for copy in saved:
        copy.wait()
    for _ in moving:
        pass
    for copy in kept:
        copy.wait()
    wires.drain()


def run_experts(rows_in, grads_in, wg, wu, wd, shards, plan, split):
    nz, nx, ny, nc = (lax.axis_size(a) for a in AXES)
    nb = nz * nx
    units, features, hidden = wg.shape
    layer = nx * ny * nc
    total = nz * layer * SLOTS
    shape = jax.ShapeDtypeStruct
    extended = rows_in.shape[-1]

    slots = min(units, 2)
    lines = (layer, nz, SLOTS)
    return pl.pallas_call(
        functools.partial(expert_kernel, split=split, plan=plan),
        out_shape=[
            shape(rows_in.shape, narrow),
            shape(grads_in.shape, narrow),
            *[shape((units, total, hidden), narrow)] * 3,
            *[whole_array(w, dim) for w, (dim, _) in zip(shards, plan)],
        ],
        in_specs=[ANY] * (5 + len(shards)),
        out_specs=[ANY] * (5 + len(shards)),
        scratch_shapes=[
            pltpu.VMEM((slots,) + lines + (extended,), narrow),
            pltpu.VMEM((slots,) + lines + (features,), narrow),
            pltpu.VMEM((slots, features, hidden), narrow),
            pltpu.VMEM((slots, features, hidden), narrow),
            pltpu.VMEM((slots, hidden, features), narrow),
            pltpu.VMEM((total, hidden), narrow),
            pltpu.VMEM((total, hidden), narrow),
            pltpu.VMEM((total, hidden), narrow),
            pltpu.VMEM((total, hidden), narrow),
            pltpu.VMEM((total, 1), wide),
            pltpu.VMEM((2,) + lines + (256,), narrow),
            pltpu.VMEM((2,) + lines + (256,), narrow),
            pltpu.SemaphoreType.DMA((64,)),
            pltpu.SemaphoreType.DMA((64,)),
            pltpu.SemaphoreType.DMA((32,)),
            pltpu.SemaphoreType.DMA((4, 2)),
        ],
        compiler_params=pltpu.CompilerParams(
            collective_id=4 if shards else None, has_side_effects=bool(shards),
            vmem_limit_bytes=60 * 1024 * 1024,
        ),
        cost_estimate=costs(80),
    )(rows_in, grads_in, wg, wu, wd, *shards)


def unit_grads_kernel(rows, grads, gated, lin_gate, lin_up, gate_out, up_out, down_out):
    picked = rows[...].reshape(gated.shape[1], rows.shape[-1])
    gate_out[0] = dot_tn(picked, lin_gate[0])
    up_out[0] = dot_tn(picked, lin_up[0])
    down_out[0] = dot_tn(gated[0], grads[...].reshape(gated.shape[1], grads.shape[-1]))


def unit_grads(rows, grads, gated, lin_gate, lin_up):
    layer, nz, units, _, features = grads.shape
    _, total, hidden = gated.shape
    step = 512 if total <= 512 else 128
    lines = (layer, nz, 1, SLOTS, step)
    shape = jax.ShapeDtypeStruct
    line_spec = pl.BlockSpec(lines, lambda a, i: (0, 0, a, 0, i))
    unit_spec = pl.BlockSpec((1, total, hidden), lambda a, i: (a, 0, 0))
    wide_spec = pl.BlockSpec((1, step, hidden), lambda a, i: (a, i, 0))
    return pl.pallas_call(
        unit_grads_kernel,
        grid=(units, features // step),
        in_specs=[line_spec, line_spec, unit_spec, unit_spec, unit_spec],
        out_specs=[wide_spec, wide_spec, pl.BlockSpec((1, hidden, step), lambda a, i: (a, 0, i))],
        out_shape=[
            shape((units, features, hidden), wide),
            shape((units, features, hidden), wide),
            shape((units, hidden, features), wide),
        ],
        cost_estimate=costs(35),
        compiler_params=pltpu.CompilerParams(vmem_limit_bytes=61 * 1024 * 1024),
    )(rows, grads, gated, lin_gate, lin_up)


def per_device(
    tokens, attn_gain, w_query, w_latent, latent_gain, w_expand, w_output, ffn_gain, w_router,
    w_shared_gate, w_shared_up, w_shared_down, w_gate, w_up, w_down, routes, clip_limit, out_grad,
):
    seqs, local_len, features = tokens.shape
    rows = seqs * local_len
    qk = NOPE + RD
    nz, nx, ny, nc = (lax.axis_size(a) for a in ("z", "x", "y", "core"))
    zi, xi, yi, ci = (lax.axis_index(a) for a in ("z", "x", "y", "core"))
    nb, nu = nz * nx, ny * nc
    layer = nx * nu
    heads = H // nu
    group = nu * rows
    all_rows = nb * group
    upd = w_gate.shape[0]
    split = upd * nz * layer // EXPERTS
    scale = qk ** (-0.5)
    GROUP = ("y", "core")
    ALL = ("z", "x", "y", "core")
    LAYER = ("x", "y", "core")

    def scatter_blk(whole, dim):
        size = whole.shape[dim] // nb
        blocks = []
        for sz in range(nz):
            for sx in range(nx):
                owner = ((zi + nz - sz) % nz) * nx + (xi + nx - sx) % nx
                blocks.append(lax.dynamic_slice_in_dim(whole, owner * size, size, dim))
        return tree_sum(blocks, ("z", "x"))

    def group_gather(value):
        return jnp.concatenate(
            [p.reshape(seqs, local_len, -1) for p in flat_ring(value, GROUP)], axis=1
        ).reshape(group, -1)

    def group_scatter(value):
        blocks = value.reshape(seqs, nu, local_len, -1)
        return tree_sum([blocks[:, i].reshape(rows, -1) for i in range(nu)], GROUP)

    def group_sum(value):
        for axis in GROUP:
            items = ring(value, axis)
            value = sum(item.astype(wide) for item in items)
        return value

    def device_positions(blk, u):
        return (blk * nu + u) * local_len + jnp.arange(local_len, dtype=jnp.int32)

    local_pos = device_positions(zi * nx + xi, yi * nc + ci)
    group_pos = jnp.concatenate(
        [
            device_positions(zi * nx + xi, (yi + ny - sy) % ny * nc + (ci + nc - sc) % nc)
            for sy in range(ny)
            for sc in range(nc)
        ]
    )
    key_pos = jnp.concatenate(
        [
            device_positions(
                (zi + nz - sz) % nz * nx + (xi + nx - sx) % nx,
                (yi + ny - sy) % ny * nc + (ci + nc - sc) % nc,
            )
            for sc in range(nc)
            for sy in range(ny)
            for sx in range(nx)
            for sz in range(nz)
        ]
    )

    shard = attn_gain.shape[0]
    lat_len = latent_gain.shape[0]
    gains = jnp.concatenate(
        [
            jnp.pad(jnp.stack([attn_gain, ffn_gain]).astype(wide), ((0, 0), (0, KVR - shard))),
            lax.dynamic_update_slice(
                jnp.zeros((1, KVR), wide),
                latent_gain.astype(wide)[None],
                (0, (zi * nx + xi) * lat_len),
            ),
            jnp.zeros((5, KVR), wide),
        ],
        axis=0,
    )
    small = jnp.concatenate([w_latent, w_router], axis=1).reshape(nu, shard // nu, -1)
    route_rows = jnp.swapaxes(routes, 0, 1).reshape(rows, TOP)
    cos_local, sin_local = rotary_tables(jnp.tile(local_pos, seqs))
    (
        gains_all, small_all, query_w, expand_w, output_w,
        hidden_group, grad_group, picks, own_member, grad_slots, latents, _, latent_all,
    ) = start(
        tokens, out_grad, cos_local, sin_local, gains, small,
        jnp.pad(route_rows, ((0, 0), (0, 128 - TOP)), constant_values=-1),
        (w_query, w_expand, w_output), upd, split,
    )
    blk = ("z", "x")
    grad_slots, later_gate, later_up, later_down = lax.optimization_barrier(
        (grad_slots, w_shared_gate, w_shared_up, w_shared_down)
    )
    gate_w = lax.all_gather(later_gate, blk, axis=0, tiled=True)
    up_w = lax.all_gather(later_up, blk, axis=0, tiled=True)
    down_w = lax.all_gather(later_down, blk, axis=1, tiled=True)
    tokens_local = tokens.reshape(rows, features)
    grad_narrow = out_grad.reshape(rows, features)
    small_whole = small_all.reshape(features, -1)
    latent_w = small_whole[:, : KVR + RD]
    router_w = small_whole[:, KVR + RD :]
    gain_attn = gains_all[:, 0, :shard].reshape(-1)
    gain_ffn = gains_all[:, 1, :shard].reshape(-1)
    gain_latent = jnp.sum(gains_all[:, 2], axis=0)
    inputs = tokens_local.astype(wide)
    _, normed_in, inverse_in = norm_rows(inputs, gain_attn)
    _, normed_lat, inverse_lat = norm_rows(latent_all[:, :KVR], gain_latent)
    length = all_rows // seqs
    latent_keys = latents.reshape(seqs, length, KVR + NOPE)
    latent_rows = latents.reshape(all_rows, KVR + NOPE)
    expand_w = jnp.pad(expand_w, ((0, NOPE), (0, 0)))
    hidden_group = hidden_group.reshape(group, features)
    grad_group = grad_group.reshape(group, features)

    def swap_layer(values):
        return lax.all_to_all(values, LAYER, split_axis=0, concat_axis=0, tiled=True)

    grad_slots = swap_layer(grad_slots)

    reach = nu * local_len
    cos_group, sin_group = rotary_tables(group_pos)
    query_lin = dot(hidden_group, query_w)
    expanded = dot(latent_rows, expand_w, narrow)
    query_pos, keys_pos = group_pos[:, None], key_pos[None, :]
    query_rows, attended, stats = attend(
        query_lin, cos_group, sin_group, expanded, latent_keys, query_pos, keys_pos, seqs, heads
    )
    top = jnp.pad(jnp.max(stats[..., 0], axis=(0, 2))[None], ((0, 7), (0, 128 - heads)))
    split_group = (seqs, ny, nc, local_len, features)
    residual, gates, hidden_mid, hidden_mid_group, expert_slots, tops = dispatch(
        dot(attended, output_w, narrow).reshape(split_group),
        tokens, gain_ffn[None], router_w, own_member, picks, top, upd,
        (), (),
    )
    clip_value = clip_limit[0]
    clip_factor = clip_value / jnp.maximum(jnp.max(tops, axis=(0, 1))[0, :heads], clip_value)
    hidden_mid_group = hidden_mid_group.reshape(group, features)

    returned, outputs, gated, lin_gate, lin_up = run_experts(
        expert_slots, grad_slots, w_gate, w_up, w_down, (), (), split
    )

    shared_gate = dot(hidden_mid_group, gate_w)
    shared_up = dot(hidden_mid_group, up_w)
    shared_act = (jax.nn.silu(shared_gate) * shared_up).astype(narrow)
    shared_partial = dot(shared_act, down_w, narrow)
    shared_act_grad = dot_nt(grad_group, down_w)
    shared_gate_grad = (shared_act_grad * shared_up * silu_slope(shared_gate)).astype(narrow)
    shared_up_grad = (shared_act_grad * jax.nn.silu(shared_gate)).astype(narrow)
    mid_shared = dot_nt(shared_gate_grad, gate_w) + dot_nt(shared_up_grad, up_w)

    usual = ("x", "z")
    def spread_sum(value, dim):
        return lax.psum_scatter(value, blk, scatter_dimension=dim, tiled=True).astype(wide)

    shared_gate_wgrad = dot_tn(hidden_mid_group, shared_gate_grad, narrow)
    shared_up_wgrad, shared_down_wgrad, returned = lax.optimization_barrier(
        (
            dot_tn(hidden_mid_group, shared_up_grad, narrow),
            dot_tn(shared_act, grad_group, narrow),
            returned,
        )
    )
    shared_up_wgrad = spread_sum(shared_up_wgrad, 0)
    shared_down_wgrad = spread_sum(shared_down_wgrad, 1)
    (
        residual_grad, attn_grad, logit_grad, ffn_gain_part, shared_sum, shared_gate_wgrad,
    ) = come_back(
        returned, mid_shared.astype(narrow).reshape(split_group),
        shared_partial.reshape(split_group), residual, gates,
        router_w, gain_ffn[None], out_grad, picks,
        (shared_gate_wgrad,), ((0, usual),),
    )
    attn_grad = attn_grad.reshape(group, features)
    outputs, attn_grad = lax.optimization_barrier((outputs, attn_grad))
    outputs = swap_layer(outputs)
    attended_grad = dot_nt(attn_grad, output_w, narrow)
    attended_grad, shared_up_wgrad = lax.optimization_barrier((attended_grad, shared_up_wgrad))
    output_wgrad = dot_tn(attended, attn_grad, narrow)

    query_lin_grad, expand_grad, rope_partial = attend_back(
        query_rows, cos_group, sin_group, expanded, latent_keys, query_pos, keys_pos, stats,
        attended_grad, seqs, heads,
    )
    hidden_partial = dot_nt(query_lin_grad, query_w, narrow)
    latent_partial = (
        dot_nt(expand_grad, expand_w).reshape(seqs, length, KVR + NOPE)
        + jnp.pad(rope_partial, ((0, 0), (0, 0), (KVR, 0)))
    ).astype(narrow)
    latent_blocks = latent_partial.reshape(seqs, nc, ny, nx, nz, local_len, KVR + NOPE)
    latent_blocks = ring_sum([latent_blocks[:, i] for i in range(nc)], "core").astype(narrow)
    latent_blocks, gated, outputs, late_hidden, late_mid = lax.optimization_barrier(
        (latent_blocks, gated, outputs, hidden_group, hidden_mid_group)
    )
    gated, shared_down_wgrad = lax.optimization_barrier((gated, shared_down_wgrad))
    gate_wgrad, up_wgrad, down_wgrad = unit_grads(expert_slots, grad_slots, gated, lin_gate, lin_up)
    latent_blocks = ring_sum([latent_blocks[:, i] for i in range(ny)], "y").astype(narrow)
    hidden_blocks = hidden_partial.reshape(split_group)
    hidden_blocks = ring_sum([hidden_blocks[:, :, i] for i in range(nc)], "core").astype(narrow)
    hidden_sum = ring_sum([hidden_blocks[:, i] for i in range(ny)], "y").astype(narrow)
    query_wgrad = dot_tn(hidden_group, query_lin_grad, narrow)
    expand_wgrad = dot_tn(latent_rows, expand_grad, narrow)
    uly = yi * nc + ci
    hidden_sum, gate_wgrad, up_wgrad, down_wgrad = lax.optimization_barrier(
        (hidden_sum, gate_wgrad, up_wgrad, down_wgrad)
    )

    def own_columns(values):
        return lax.dynamic_slice_in_dim(
            values.T.reshape(nb, nu, shard // nu, group), uly, 1, 1
        ).reshape(features // nu, group)

    (
        tokens_grad, block_out, latent_wgrad, gain_sums, query_wgrad, expand_wgrad, output_wgrad,
    ) = finish(
        hidden_sum, latent_blocks,
        tokens, residual_grad, small_whole, own_columns(late_hidden), own_columns(late_mid),
        logit_grad, ffn_gain_part, gain_attn[None], gain_latent[None],
        latent_all, cos_local, sin_local, residual,
        shared_sum, picks, outputs,
        (query_wgrad, expand_wgrad[:KVR], output_wgrad),
        ((0, usual), (0, usual), (1, usual)),
    )
    width = KVR + RD
    small_wgrad = latent_wgrad.reshape(shard, -1)
    latent_wgrad, router_wgrad = small_wgrad[:, :width], small_wgrad[:, width:]
    ffn_gain_grad = jnp.sum(gain_sums[:, 1, :shard], axis=0)
    gain_sums = jnp.sum(gain_sums[:, 0], axis=0)
    attn_gain_grad = gain_sums[:shard]
    latent_gain_grad = lax.dynamic_slice_in_dim(
        gain_sums, shard + (zi * nx + xi) * lat_len, lat_len, 0
    )
    return (
        block_out,
        tokens_grad,
        attn_gain_grad,
        query_wgrad,
        latent_wgrad,
        latent_gain_grad,
        expand_wgrad,
        output_wgrad,
        ffn_gain_grad,
        router_wgrad,
        shared_gate_wgrad,
        shared_up_wgrad,
        shared_down_wgrad,
        gate_wgrad,
        up_wgrad,
        down_wgrad,
        clip_factor,
    )


def solution(mesh):
    blocks, group = mesh.shape["blk"], mesh.shape["ulysses"]
    chips = Mesh(
        mesh.devices.reshape(Z_SIZE, blocks // Z_SIZE, group // CORES, CORES),
        ("z", "x", "y", "core"),
    )
    blk, uly, every = ("z", "x"), ("y", "core"), ("z", "x", "y", "core")
    rows = P(None, every, None)
    unit = P(every, None, None)
    return jax.shard_map(
        per_device,
        mesh=chips,
        in_specs=(
            rows, P(blk), P(blk, uly), P(blk, None), P(blk), P(blk, uly), P(uly, blk), P(blk),
            P(blk, None), P(blk, uly), P(blk, uly), P(uly, blk), unit, unit, unit, unit, P(), rows,
        ),
        out_specs=(
            rows, rows, P(blk), P(blk, uly), P(blk, None), P(blk), P(blk, uly), P(uly, blk), P(blk),
            P(blk, None), P(blk, uly), P(blk, uly), P(uly, blk), unit, unit, unit, P(uly),
        ),
        check_vma=False,
    )
```

```python
import functools

import jax
import jax.numpy as jnp
from jax import lax
from jax.experimental import pallas as pl
from jax.experimental.pallas import tpu as pltpu
from jax.sharding import Mesh
from jax.sharding import PartitionSpec as P

H = 16
NOPE = 128
RD = 64
VH = 128
KVR = 512
EXPERTS = 64
TOP = 6
CAP = 14
SLOTS = 16
HEAD_START = 12
Z_SIZE = 4
CORES = 2

epsilon = 1e-06
rope_base = 10000.0
wide = jnp.float32
narrow = jnp.bfloat16


def dot(a, b, out=wide):
    return jnp.dot(a, b, preferred_element_type=out)


def dot_tn(a, b, out=wide):
    return lax.dot_general(a, b, (((0,), (0,)), ((), ())), preferred_element_type=out)


def dot_nt(a, b, out=wide):
    return lax.dot_general(a, b, (((1,), (1,)), ((), ())), preferred_element_type=out)


def norm_rows(values, gain):
    inverse = lax.rsqrt(jnp.mean(values * values, axis=-1, keepdims=True) + epsilon)
    normed = values * inverse
    return (normed * gain, normed, inverse)


def norm_input_back(grad_out, normed, inverse, gain):
    scaled = grad_out * gain
    return inverse * (scaled - normed * jnp.mean(scaled * normed, axis=-1, keepdims=True))


def rotary_tables(positions):
    half_width = RD // 2
    frequency = rope_base ** (-2.0 * jnp.arange(half_width).astype(wide) / RD)
    angles = positions.astype(wide)[:, None] * frequency[None, :]
    return (jnp.cos(angles), jnp.sin(angles))


def rotate(values, cosine, sine):
    half = RD // 2
    a, b = values[..., :half], values[..., half:]
    return jnp.concatenate([a * cosine - b * sine, b * cosine + a * sine], axis=-1)


def unrotate(values, cosine, sine):
    half = RD // 2
    a, b = values[..., :half], values[..., half:]
    return jnp.concatenate([a * cosine + b * sine, b * cosine - a * sine], axis=-1)


def silu_slope(values):
    s = jax.nn.sigmoid(values)
    return s * (1.0 + values * (1.0 - s))


def hop(value, axis):
    n = lax.axis_size(axis)
    return lax.ppermute(value, axis, [(i, (i + 1) % n) for i in range(n)])


def ring(value, axis):
    items = [value]
    for _ in range(lax.axis_size(axis) - 1):
        items.append(hop(items[-1], axis))
    return items


def ring_sum(blocks, axis):
    n = lax.axis_size(axis)
    if n == 1:
        return blocks[0].astype(wide)
    running = hop(blocks[1].astype(narrow), axis)
    for s in range(2, n):
        running = hop((running.astype(wide) + blocks[s].astype(wide)).astype(narrow), axis)
    return running.astype(wide) + blocks[0].astype(wide)


def flat_ring(value, axes):
    items = [value]
    for axis in axes:
        items = [piece for item in items for piece in ring(item, axis)]
    return items


def tree_sum(blocks, axes):
    for axis in reversed(axes):
        n = lax.axis_size(axis)
        blocks = [ring_sum(blocks[i : i + n], axis) for i in range(0, len(blocks), n)]
    return blocks[0]


ANY = pl.BlockSpec(memory_space=pl.ANY)
VMEM = pl.BlockSpec(memory_space=pltpu.VMEM)
MESH = pl.DeviceIdType.MESH
AXES = ("z", "x", "y", "core")


def behind(axis, steps):
    n = lax.axis_size(axis)
    return lax.rem(lax.axis_index(axis) + (n - steps), n)


def ahead(axis):
    n = lax.axis_size(axis)
    return lax.rem(lax.axis_index(axis) + 1, n)


def greet(axes):
    barrier = pltpu.get_barrier_semaphore()
    for axis in axes:
        pl.semaphore_signal(
            barrier, inc=1, device_id={axis: behind(axis, 1)}, device_id_type=MESH
        )
    pl.semaphore_wait(barrier, len(axes))


class Wires:
    def __init__(self, send, recv):
        self.send, self.recv, self.used, self.sent = send, recv, 0, []

    def port(self):
        self.used += 1
        return self.used - 1

    def push(self, src, dst, port, axis):
        copy = pltpu.make_async_remote_copy(
            src_ref=src,
            dst_ref=dst,
            send_sem=self.send.at[port],
            recv_sem=self.recv.at[port],
            device_id={axis: ahead(axis)},
            device_id_type=MESH,
        )
        copy.start()
        self.sent.append(copy)

    def arrived(self, dst, port, axis):
        pltpu.make_async_remote_copy(
            src_ref=dst,
            dst_ref=dst,
            send_sem=self.send.at[port],
            recv_sem=self.recv.at[port],
            device_id={axis: ahead(axis)},
            device_id_type=MESH,
        ).wait_recv()

    def drain(self):
        for copy in self.sent:
            copy.wait_send()


class BlockGather:
    def __init__(self, wires, src, dst, place, x_first):
        self.wires, self.src, self.dst, self.place, self.x_first = wires, src, dst, place, x_first
        self.nz, self.nx = lax.axis_size("z"), lax.axis_size("x")
        self.ports = {
            (sz, sx): wires.port() for sz in range(self.nz) for sx in range(self.nx) if sz or sx
        }

    def at(self, sz, sx):
        return self.place(self.dst, behind("z", sz) * self.nx + behind("x", sx))

    def forward(self, sz, sx):
        src = self.src if sz == 0 and sx == 0 else self.at(sz, sx)
        if self.x_first:
            go_x, go_z = sz == 0, True
        else:
            go_x, go_z = True, sx == 0
        if go_z and sz + 1 < self.nz:
            self.wires.push(src, self.at(sz, sx), self.ports[sz + 1, sx], "z")
        if go_x and sx + 1 < self.nx:
            self.wires.push(src, self.at(sz, sx), self.ports[sz, sx + 1], "x")

    def take(self, sz, sx):
        from_x = sx > 0 and (sz == 0 if self.x_first else True)
        self.wires.arrived(self.at(sz, sx), self.ports[sz, sx], "x" if from_x else "z")
        self.forward(sz, sx)

    def chain(self):
        self.forward(0, 0)
        for slots in self.rounds():
            for slot in slots:
                yield
                self.take(*slot)

    def rounds(self):
        if self.x_first:
            order = [[(0, sx)] for sx in range(1, self.nx)]
            order += [[(sz, sx) for sx in range(self.nx)] for sz in range(1, self.nz)]
            return order
        last = [[(sz, sx) for sz in range(self.nz)] for sx in range(1, self.nx)]
        return [[(sz, 0)] for sz in range(1, self.nz)] + last


def rows_of(size):
    return lambda ref, owner: ref.at[pl.ds(pl.multiple_of(owner * size, size), size)]


def columns_of(size):
    return lambda ref, owner: ref.at[:, pl.ds(pl.multiple_of(owner * size, size), size)]


def start_kernel(
    tokens, grads, cosine, sine, gains, small, routes, w_query, w_expand, w_output,
    gains_out, small_out, query_out, expand_out, output_out,
    group_out, grads_out, picks_out, member_out, slots_out, latents_out, hidden_out, latent_all_out,
    own_latent, own_hidden, routes_line, grads_line, send, recv, local, *, units, split,
):
    nz, nx, ny, nc = (lax.axis_size(a) for a in AXES)
    nb, nu = nz * nx, ny * nc
    me = lax.axis_index("z") * nx + lax.axis_index("x")
    uly = lax.axis_index("y") * nc + lax.axis_index("core")
    seqs, local_len, features = tokens.shape
    rows = seqs * local_len
    greet(AXES)
    wires = Wires(send, recv)
    used, waited = [], set()

    def load(src, dst):
        copy = pltpu.make_async_copy(src, dst, local.at[len(used)])
        used.append(copy)
        copy.start()
        return copy

    def member(sy, sc):
        return behind("y", sy) * nc + behind("core", sc)

    def line_chain(src, dst):
        ports = [wires.port() for _ in range(nz)]
        wires.push(src, dst.at[1], ports[1], "z")
        mine = load(src, dst.at[0])
        for sz in range(1, nz):
            yield
            wires.arrived(dst.at[sz], ports[sz], "z")
            if sz + 1 < nz:
                wires.push(dst.at[sz], dst.at[sz + 1], ports[sz + 1], "z")
        mine.wait()
        waited.add(id(mine))

    def main():
        g_gains = BlockGather(wires, gains, gains_out, lambda ref, owner: ref.at[owner], False)
        g_small = BlockGather(
            wires, small.at[uly], small_out, lambda ref, owner: ref.at[owner, uly], False
        )
        slots = [(0, 0)] + [slot for r in g_small.rounds() for slot in r]
        y_ports = {(slot, sy): wires.port() for slot in slots for sy in range(1, ny)}
        c_ports = {(slot, sy): wires.port() for slot in slots for sy in range(ny)}

        def piece(slot, sy, sc):
            owner = behind("z", slot[0]) * nx + behind("x", slot[1])
            return small_out.at[owner, member(sy, sc)]

        def spread(slot):
            here = piece(slot, 0, 0)
            if ny > 1:
                wires.push(here, here, y_ports[slot, 1], "y")
            wires.push(here, here, c_ports[slot, 0], "core")

        g_small.forward(0, 0)
        g_gains.forward(0, 0)
        mine = [load(small.at[uly], small_out.at[me, uly]), load(gains, gains_out.at[me])]
        yield
        for slots_now in g_small.rounds():
            for slot in slots_now:
                yield
                g_small.take(*slot)
                if mine:
                    for copy in mine:
                        copy.wait()
                    waited.update(id(copy) for copy in mine)
                    mine = []
                    spread((0, 0))
                spread(slot)
                g_gains.take(*slot)
        for sy in range(1, ny):
            for slot in slots:
                yield
                here = piece(slot, sy, 0)
                wires.arrived(here, y_ports[slot, sy], "y")
                if sy + 1 < ny:
                    wires.push(here, here, y_ports[slot, sy + 1], "y")
                wires.push(here, here, c_ports[slot, sy], "core")
        for sy in range(ny):
            for slot in slots:
                wires.arrived(piece(slot, sy, 1), c_ports[slot, sy], "core")
        gain = jnp.concatenate([gains_out[b, 0:1, : features // nb] for b in range(nb)], axis=1)
        latent_gain = sum(gains_out[b, 2:3, :] for b in range(nb))
        x = tokens[...].astype(wide).reshape(rows, features)
        hidden = norm_rows(x, gain)[0].astype(narrow)
        hidden_out[...] = hidden
        own_hidden[...] = hidden.reshape(tokens.shape)
        spread_hidden = GroupGather(wires, own_hidden, group_out)
        spread_hidden.start()
        load(own_hidden, group_out.at[:, 0, 0])
        width = small_out.shape[-1]
        latent_all = dot(hidden, small_out[...].reshape(features, width))[:, : KVR + RD]
        latent_all_out[...] = latent_all
        latent = norm_rows(latent_all[:, :KVR], latent_gain)[0]
        rope = rotate(latent_all[:, KVR:], cosine[...], sine[...])
        own_latent[:, :, KVR:] = jnp.zeros((seqs, local_len, NOPE), narrow)
        own_latent[:, :, :KVR] = latent.astype(narrow).reshape(seqs, local_len, KVR)
        own_latent[:, :, KVR : KVR + RD] = rope.astype(narrow).reshape(seqs, local_len, RD)
        z_ports = [wires.port() for _ in range(nz)]
        x_ports = [wires.port() for _ in range(nx)]
        yx_ports = [[wires.port() for _ in range(nx)] for _ in range(ny)]
        cx_ports = [[wires.port() for _ in range(nx)] for _ in range(ny)]
        wires.push(own_latent, latents_out.at[:, 0, 0, 0, 1], z_ports[1], "z")
        own_place = load(own_latent, latents_out.at[:, 0, 0, 0, 0])
        for sz in range(1, nz):
            yield
            here = latents_out.at[:, 0, 0, 0, sz]
            wires.arrived(here, z_ports[sz], "z")
            if sz + 1 < nz:
                wires.push(here, latents_out.at[:, 0, 0, 0, sz + 1], z_ports[sz + 1], "z")
        own_place.wait()
        waited.add(id(own_place))
        for sx in range(nx):
            block = latents_out.at[:, 0, 0, sx]
            if sx:
                yield
                wires.arrived(block, x_ports[sx], "x")
            if sx + 1 < nx:
                wires.push(block, latents_out.at[:, 0, 0, sx + 1], x_ports[sx + 1], "x")
            if ny > 1:
                wires.push(block, latents_out.at[:, 0, 1, sx], yx_ports[1][sx], "y")
            wires.push(block, latents_out.at[:, 1, 0, sx], cx_ports[0][sx], "core")
        for sy in range(1, ny):
            for sx in range(nx):
                yield
                block = latents_out.at[:, 0, sy, sx]
                wires.arrived(block, yx_ports[sy][sx], "y")
                if sy + 1 < ny:
                    wires.push(block, latents_out.at[:, 0, sy + 1, sx], yx_ports[sy + 1][sx], "y")
                wires.push(block, latents_out.at[:, 1, sy, sx], cx_ports[sy][sx], "core")
        for sy in range(ny):
            for sx in range(nx):
                yield
                wires.arrived(latents_out.at[:, 1, sy, sx], cx_ports[sy][sx], "core")
        yield from spread_hidden.chain()

    def slots_chain():
        yield from line_chain(routes, routes_line)
        yield from line_chain(grads, grads_line)
        count = rows
        earlier = (
            lax.broadcasted_iota(jnp.int32, (count, count), 1)
            < lax.broadcasted_iota(jnp.int32, (count, count), 0)
        ).astype(narrow)
        columns = picks_out.shape[-1]
        expert = lax.broadcasted_iota(jnp.int32, (EXPERTS, columns), 0)
        column = lax.broadcasted_iota(jnp.int32, (EXPERTS, columns), 1)
        unit = column // SLOTS
        if split > 1:
            unit = unit // split
        chosen = (expert == unit + lax.axis_index("z") * (EXPERTS // nz)).astype(narrow)
        slot = lax.rem(lax.broadcasted_iota(jnp.int32, (count, columns), 1), SLOTS)
        names = lax.broadcasted_iota(jnp.int32, (count, EXPERTS), 1)
        for s in range(nz):
            member = sum(
                (routes_line[s, :, j : j + 1] == names).astype(wide) for j in range(TOP)
            )
            if s == 0:
                member_out[...] = member
            rank = dot(earlier, member.astype(narrow))
            code = jnp.where(member > 0, rank, -1.0).astype(narrow)
            pick = (dot(code, chosen) == slot.astype(wide)).astype(narrow)
            picks_out[s] = pick
            row_grads = grads_line[s].reshape(rows, features)
            shaped = (slots_out.shape[0],) + slots_out.shape[2:]
            slots_out[:, s] = dot_tn(pick, row_grads).astype(narrow).reshape(shaped)

    def group_chain(src, dst):
        gather = GroupGather(wires, src, dst)
        gather.start()
        load(src, dst.at[:, 0, 0])
        yield from gather.chain()

    def array_chain(src, dst, place, x_first):
        gather = BlockGather(wires, src, dst, place, x_first)
        load(src, gather.at(0, 0))
        yield from gather.chain()

    first = main()
    next(first)
    others = [
        slots_chain(),
        array_chain(w_query, query_out, rows_of(w_query.shape[0]), False),
        array_chain(w_expand, expand_out, rows_of(w_expand.shape[0]), False),
        array_chain(w_output, output_out, columns_of(w_output.shape[1]), False),
        group_chain(grads, grads_out),
    ]
    for _ in range(HEAD_START):
        next(first)
    weave(first, others, 3)
    wires.drain()
    for copy in used:
        if id(copy) not in waited:
            copy.wait()


def start(tokens, grads, cosine, sine, gains, small, routes, weights, units, split):
    nz, nx, ny, nc = (lax.axis_size(a) for a in AXES)
    nb, nu = nz * nx, ny * nc
    seqs, local_len, features = tokens.shape
    shape = jax.ShapeDtypeStruct

    def whole(w, dim):
        size = list(w.shape)
        size[dim] *= nb
        return shape(tuple(size), w.dtype)

    rows = seqs * local_len
    grouped = (seqs, ny, nc, local_len, features)
    outs = [
        shape((nb,) + gains.shape, wide),
        shape((nb,) + small.shape, narrow),
        *[whole(w, d) for w, d in zip(weights, (0, 0, 1))],
        shape(grouped, narrow),
        shape(grouped, narrow),
        shape((nz, rows, nx * nu * units * SLOTS), narrow),
        shape((rows, EXPERTS), wide),
        shape((nx * nu, nz, units, SLOTS, features), narrow),
        shape((seqs, nc, ny, nx, nz, local_len, KVR + NOPE), narrow),
        shape((seqs * local_len, features), narrow),
        shape((seqs * local_len, KVR + RD), wide),
    ]
    return pl.pallas_call(
        functools.partial(start_kernel, units=units, split=split),
        out_shape=outs,
        in_specs=[VMEM, ANY, VMEM, VMEM, VMEM, VMEM, VMEM] + [ANY] * 3,
        out_specs=[VMEM, VMEM] + [ANY] * 5 + [VMEM] * 3 + [ANY] + [VMEM, VMEM],
        scratch_shapes=[
            pltpu.VMEM((seqs, local_len, KVR + NOPE), narrow),
            pltpu.VMEM(tokens.shape, narrow),
            pltpu.VMEM((nz,) + routes.shape, routes.dtype),
            pltpu.VMEM((nz,) + grads.shape, narrow),
            pltpu.SemaphoreType.DMA((384,)),
            pltpu.SemaphoreType.DMA((384,)),
            pltpu.SemaphoreType.DMA((16,)),
        ],
        compiler_params=pltpu.CompilerParams(
            collective_id=0, has_side_effects=True, vmem_limit_bytes=40 * 1024 * 1024
        ),
        cost_estimate=costs(120),
    )(tokens, grads, cosine, sine, gains, small, routes, *weights)


def scores_of(query, keys, rope, scale):
    return (dot_nt(query[:, :NOPE], keys) + dot_nt(query[:, NOPE:], rope)) * scale


def attend_kernel(
    query, cosine, sine, keys, rope, query_pos, key_pos, query_out, attended, stats, head_lin,
    *, scale, sub,
):
    qk = NOPE + RD
    for head in range(query.shape[1] // qk):

        @pl.when(pl.program_id(1) == head)
        def _(head=head):
            head_lin[:, :qk] = query[:, head * qk : (head + 1) * qk]

    keys_ = keys[:, :NOPE]
    values = keys[:, NOPE:]

    @pl.loop(0, query.shape[0], step=sub)
    def _(first):
        span = pl.ds(pl.multiple_of(first, sub), sub)
        lin = head_lin[span, :]
        turned = rotate(lin[:, NOPE : NOPE + RD], cosine[span, :], sine[span, :])
        query_out[span, :NOPE] = lin[:, :NOPE].astype(narrow)
        query_out[span, NOPE:] = jnp.zeros((sub, NOPE), narrow)
        query_out[span, NOPE : NOPE + RD] = turned.astype(narrow)
        scores = scores_of(query_out[span, :], keys_, rope[0], scale)
        scores = jnp.where(key_pos[...] <= query_pos[span, :], scores, -jnp.inf)
        top = jnp.max(scores, axis=1, keepdims=True)
        raised = jnp.exp(scores - top)
        total = jnp.sum(raised, axis=1, keepdims=True)
        probability = (raised * (1.0 / total)).astype(narrow)
        attended[span, :] = dot(probability, values).astype(narrow)
        stats[0, 0, span, 0:1] = top
        stats[0, 0, span, 1:2] = top + jnp.log(total)


def attend_back_kernel(
    query, cosine, sine, keys, rope, query_pos, key_pos, stats, grads,
    query_grad, expand_grad, rope_grad, key_acc, *, scale, sub,
):
    keys_ = keys[:, :NOPE]
    values = keys[:, NOPE:]
    key_acc[...] = jnp.zeros(key_acc.shape, wide)

    @pl.loop(0, query.shape[0], step=sub)
    def _(first):
        span = pl.ds(pl.multiple_of(first, sub), sub)
        rows = query[span, :]
        scores = scores_of(rows, keys_, rope[0], scale)
        scores = jnp.where(key_pos[...] <= query_pos[span, :], scores, -jnp.inf)
        probability = jnp.exp(scores - stats[0, 0, span, 1:2])
        grad = grads[span, :]
        prob_grad = dot_nt(grad, values)
        weighted = probability * prob_grad
        delta = jnp.sum(weighted, axis=1, keepdims=True)
        score_grad = ((weighted - probability * delta) * scale).astype(narrow)
        back_plain = dot(score_grad, keys_).astype(narrow)
        back_turned = dot(score_grad, rope[0])[:, :RD].astype(narrow).astype(wide)
        turned = unrotate(back_turned, cosine[span, :], sine[span, :]).astype(narrow)
        head_grad = jnp.concatenate([back_plain, turned], axis=1)
        qk = NOPE + RD
        for head in range(query_grad.shape[1] // qk):

            @pl.when(pl.program_id(1) == head)
            def _(head=head):
                query_grad[span, head * qk : (head + 1) * qk] = head_grad

        key_acc[:, : 2 * NOPE] += dot_tn(score_grad, rows)
        key_acc[:, 2 * NOPE :] += dot_tn(probability.astype(narrow), grad)

    expand_grad[:, :NOPE] = key_acc[:, :NOPE].astype(narrow)
    expand_grad[:, NOPE:] = key_acc[:, 2 * NOPE :].astype(narrow)

    @pl.when(pl.program_id(1) == 0)
    def _():
        rope_grad[0] = key_acc[:, NOPE : 2 * NOPE]

    @pl.when(pl.program_id(1) > 0)
    def _():
        rope_grad[0] += key_acc[:, NOPE : 2 * NOPE]


def attention_specs(seqs, heads, reach, length):
    both = NOPE + VH
    return dict(
        query=pl.BlockSpec((reach, both), lambda s, h: (s, h)),
        heads=pl.BlockSpec((reach, heads * (NOPE + RD)), lambda s, h: (s, 0)),
        rope_grad=pl.BlockSpec((1, length, NOPE), lambda s, h: (s, 0, 0)),
        table=pl.BlockSpec((reach, RD // 2), lambda s, h: (0, 0)),
        keys=pl.BlockSpec((length, both), lambda s, h: (s, h)),
        rope=pl.BlockSpec((1, length, NOPE), lambda s, h: (s, 0, KVR // NOPE)),
        query_pos=pl.BlockSpec((reach, 1), lambda s, h: (0, 0)),
        key_pos=pl.BlockSpec((1, length), lambda s, h: (0, 0)),
        head=pl.BlockSpec((reach, VH), lambda s, h: (s, h)),
        stats=pl.BlockSpec((1, 1, reach, 2), lambda s, h: (s, h, 0, 0)),
    )


def attend(query_lin, cosine, sine, keys, rope, query_pos, key_pos, seqs, heads):
    reach, length = query_pos.shape[0], key_pos.shape[1]
    sub = min(reach, max(16, 256 * 2048 // length))
    sp = attention_specs(seqs, heads, reach, length)
    shape = jax.ShapeDtypeStruct
    return pl.pallas_call(
        functools.partial(attend_kernel, scale=(NOPE + RD) ** -0.5, sub=sub),
        grid=(seqs, heads),
        in_specs=[sp[k] for k in ("heads", "table", "table", "keys", "rope", "query_pos", "key_pos")],
        out_specs=[sp["query"], sp["head"], sp["stats"]],
        out_shape=[
            shape((seqs * reach, heads * 2 * NOPE), narrow),
            shape((seqs * reach, heads * VH), narrow),
            shape((seqs, heads, reach, 2), wide),
        ],
        scratch_shapes=[pltpu.VMEM((reach, 2 * NOPE), wide)],
        cost_estimate=costs(16),
        compiler_params=pltpu.CompilerParams(vmem_limit_bytes=61 * 1024 * 1024),
    )(query_lin, cosine, sine, keys, rope, query_pos, key_pos)


def attend_back(query, cosine, sine, keys, rope, query_pos, key_pos, stats, grads, seqs, heads):
    reach, length = query_pos.shape[0], key_pos.shape[1]
    sub = min(reach, max(16, 256 * 2048 // length))
    sp = attention_specs(seqs, heads, reach, length)
    shape = jax.ShapeDtypeStruct
    return pl.pallas_call(
        functools.partial(attend_back_kernel, scale=(NOPE + RD) ** -0.5, sub=sub),
        grid=(seqs, heads),
        in_specs=[
            sp[k]
            for k in (
                "query", "table", "table", "keys", "rope", "query_pos", "key_pos", "stats", "head",
            )
        ],
        out_specs=[sp["heads"], sp["keys"], sp["rope_grad"]],
        cost_estimate=costs(25),
        out_shape=[
            shape((seqs * reach, heads * (NOPE + RD)), narrow),
            shape(keys.shape, narrow),
            shape((seqs, length, NOPE), wide),
        ],
        scratch_shapes=[pltpu.VMEM((length, 2 * NOPE + VH), wide)],
        compiler_params=pltpu.CompilerParams(vmem_limit_bytes=61 * 1024 * 1024),
    )(query, cosine, sine, keys, rope, query_pos, key_pos, stats, grads)


def costs(us):
    return pl.CostEstimate(flops=int(us * 1e9), bytes_accessed=int(us * 1e6), transcendentals=0)


def add_into(target, *terms):
    lead, count = target.shape[:-2], target.shape[-2]
    step = 32 if count % 32 == 0 else 16 if count % 16 == 0 else count
    pieces = count // step
    total = pieces
    for size in lead:
        total *= size

    @pl.loop(0, total)
    def _(i):
        at = []
        rest = i // pieces
        for size in reversed(lead):
            at.insert(0, lax.rem(rest, size))
            rest = rest // size
        span = pl.ds(pl.multiple_of(lax.rem(i, pieces) * step, step), step)
        place = (*at, span, slice(None))
        target[place] = sum(term[place].astype(wide) for term in terms).astype(target.dtype)


class Queue:
    def __init__(self):
        self.items = []

    def add(self, place, thunk):
        self.items.append((place, len(self.items), thunk))
        self.items.sort(key=lambda item: item[:2])

    def go(self, count):
        for _, _, thunk in self.items[:count]:
            thunk()
        del self.items[:count]


class BlockScatter:
    def __init__(self, wires, loads, src, place, axes, acc, first, second, out):
        self.wires, self.loads, self.src, self.place, self.axes = wires, loads, src, place, axes
        self.acc, self.first, self.second, self.out = acc, first, second, out
        self.na, self.nb = (lax.axis_size(a) for a in axes)
        self.ports = {
            (a, b): wires.port() for b in range(self.nb) for a in range(self.na) if a or b
        }
        self.order = [*range(1, self.nb), 0]

    def mine(self, a, b):
        steps = dict(zip(self.axes, (a, b)))
        owner = behind("z", steps["z"]) * lax.axis_size("x") + behind("x", steps["x"])
        return self.place(self.src, owner)

    def slot(self, a, b):
        return self.acc.at[b, max(a - 1, 0)]

    def start(self, queue=None):
        self.loading, self.queue = {}, queue or Queue()
        for place, b in enumerate(self.order):
            self.queue.add(
                place,
                lambda b=b: self.wires.push(
                    self.mine(1, b), self.first.at[b, 0], self.ports[1, b], self.axes[0]
                ),
            )
        if queue is None:
            self.queue.go(self.nb)
        for b in self.order:
            for a in [*range(2, self.na), 0]:
                self.loading[a, b] = self.loads(self.mine(a, b), self.slot(a, b))

    def chain(self):
        wires, (axis_a, axis_b) = self.wires, self.axes
        for b in self.order:
            for a in [*range(2, self.na), 0]:
                came = self.first.at[b, (a or self.na) - 2]
                yield
                wires.arrived(came, self.ports[(a or self.na) - 1, b], axis_a)
                if not a:
                    self.queue.go(1)
                self.loading[a, b].wait()
                add_into(self.slot(a, b), self.slot(a, b), came)
                if a:
                    wires.push(self.slot(a, b), self.first.at[b, a - 1], self.ports[a, b], axis_a)
            if b >= 2:
                yield
                wires.arrived(self.second.at[b - 2], self.ports[0, b - 1], axis_b)
                add_into(self.slot(0, b), self.slot(0, b), self.second.at[b - 2])
            if b >= 1:
                wires.push(self.slot(0, b), self.second.at[b - 1], self.ports[0, b], axis_b)
        yield
        wires.arrived(self.second.at[self.nb - 2], self.ports[0, self.nb - 1], axis_b)
        add_into(self.out, self.slot(0, 0), self.second.at[self.nb - 2])


def scatter_scratch(shard, axes, dtype=narrow):
    na, nb = (lax.axis_size(a) for a in axes)
    return [
        pltpu.VMEM((nb, na - 1) + shard, dtype),
        pltpu.VMEM((nb, na - 1) + shard, dtype),
        pltpu.VMEM((nb - 1,) + shard, dtype),
    ]


class GroupGather:
    def __init__(self, wires, src, dst):
        self.wires, self.src, self.dst = wires, src, dst
        self.ny, self.nc = lax.axis_size("y"), lax.axis_size("core")
        self.ports = [wires.port() for _ in range(self.ny * self.nc)]

    def start(self):
        if self.ny > 1:
            self.wires.push(self.src, self.dst.at[:, 1, 0], self.ports[self.nc], "y")
        self.wires.push(self.src, self.dst.at[:, 0, 1], self.ports[1], "core")

    def chain(self):
        wires, dst, nc = self.wires, self.dst, self.nc
        for sy in range(1, self.ny):
            piece = dst.at[:, sy, 0]
            yield
            wires.arrived(piece, self.ports[sy * nc], "y")
            if sy + 1 < self.ny:
                wires.push(piece, dst.at[:, sy + 1, 0], self.ports[(sy + 1) * nc], "y")
            wires.push(piece, dst.at[:, sy, 1], self.ports[sy * nc + 1], "core")
        for sy in range(self.ny):
            yield
            wires.arrived(dst.at[:, sy, 1], self.ports[sy * nc + 1], "core")


def group_sum_chain(wires, src, own, other, came, load):
    ny = lax.axis_size("y")
    core_ports = [wires.port() for _ in range(ny)]
    y_ports = [wires.port() for _ in range(ny)]
    order = [*range(1, ny), 0]
    for sy in order:
        wires.push(src.at[:, sy, 1], other.at[:, sy], core_ports[sy], "core")
    loading = [load(src.at[:, sy, 0], own.at[:, sy]) for sy in range(ny)]
    for sy in order:
        yield
        wires.arrived(other.at[:, sy], core_ports[sy], "core")
        loading[sy].wait()
        add_into(own.at[:, sy], own.at[:, sy], other.at[:, sy])
        if ny > 1:
            last = (sy or ny) - 1
            if last:
                yield
                wires.arrived(came.at[:, last - 1], y_ports[last], "y")
                add_into(own.at[:, sy], own.at[:, sy], came.at[:, last - 1])
            if sy:
                wires.push(own.at[:, sy], came.at[:, sy - 1], y_ports[sy], "y")


def weave(main, others, share):
    others = list(others)
    running = True
    while running or others:
        if running:
            running = next(main, True) is None
        for _ in range(share if running else max(1, len(others))):
            if others:
                chain = others.pop(0)
                if next(chain, True) is None:
                    others.append(chain)


def finish_kernel(
    hidden_sum, latent_partial, tokens, residual_grad, small, hidden_t, mid_t, logit_grad,
    ffn_gain, gain_attn, gain_latent, latent_all, cosine, sine, residual, shared_sum, picks, slots,
    *rest, modes,
):
    count = len(modes)
    partials, rest = rest[:count], rest[count:]
    tokens_grad, block_out, latent_w_out, gains_out, *rest = rest
    outs, rest = rest[:count], rest[count:]
    (
        lat_own, lat_x, lat_z,
        own_lag, lag_group, wide_acc, lat_wgrad, gain_terms, routed_slots, routed_own, routed_came, *rest,
    ) = rest
    buffers, rest = rest[: 3 * count], rest[3 * count :]
    lw_buffers, g_buffers = rest[:3], rest[3:6]
    send, recv, local = rest[6:]
    nz, nx, ny, nc = (lax.axis_size(a) for a in AXES)
    nb, nu = nz * nx, ny * nc
    uly = lax.axis_index("y") * nc + lax.axis_index("core")
    seqs, local_len, features = tokens.shape
    rows = seqs * local_len
    greet(AXES)
    wires = Wires(send, recv)
    used = []

    def load(src, dst):
        copy = pltpu.make_async_copy(src, dst, local.at[len(used)])
        used.append(copy)
        copy.start()
        return copy

    def blocks_of(size, dim):
        return rows_of(size) if dim == 0 else columns_of(size)

    scatters = [
        BlockScatter(
            wires, load, partials[i], blocks_of(partials[i].shape[dim] // nb, dim), axes,
            *buffers[3 * i : 3 * i + 3], outs[i],
        )
        for i, (dim, axes) in enumerate(modes)
    ]

    def routed_chain():
        ports = [wires.port() for _ in range(nz)]
        loading = {s: load(slots.at[:, s], routed_slots.at[s]) for s in [*range(1, nz), 0]}
        for s in [*range(1, nz), 0]:
            own = routed_own.at[s]
            last = (s or nz) - 1
            yield
            loading[s].wait()
            term = dot(picks[s], routed_slots[s].reshape(picks.shape[2], features))
            routed_own[s] = term.astype(narrow)
            if last:
                wires.arrived(routed_came.at[last - 1], ports[last], "z")
                add_into(own, own, routed_came.at[last - 1])
            if s:
                wires.push(own, routed_came.at[s - 1], ports[s], "z")

    def output_chain():
        yield from routed_chain()
        total = residual[...] + shared_sum[...].astype(wide).reshape(rows, features)
        total = total + routed_own[0].astype(wide)
        block_out[...] = total.astype(narrow).reshape(tokens.shape)

    def latent_chain():
        x_ports = [wires.port() for _ in range(nx)]
        z_ports = [wires.port() for _ in range(nz)]
        wires.push(latent_partial.at[:, 1], lat_x.at[:, 0], x_ports[1], "x")
        order_x = [*range(2, nx), 0]
        loading = {sx: load(latent_partial.at[:, sx], lat_own.at[:, sx]) for sx in order_x}
        yield
        for sx in order_x:
            own, last = lat_own.at[:, sx], (sx or nx) - 1
            yield
            wires.arrived(lat_x.at[:, last - 1], x_ports[last], "x")
            loading[sx].wait()
            add_into(own, own, lat_x.at[:, last - 1])
            if sx:
                wires.push(own, lat_x.at[:, sx - 1], x_ports[sx], "x")
        for sz in [*range(1, nz), 0]:
            own = lat_own.at[:, 0, sz]
            last = (sz or nz) - 1
            if last:
                yield
                wires.arrived(lat_z.at[:, last - 1], z_ports[last], "z")
                add_into(own, own, lat_z.at[:, last - 1])
            if sz:
                wires.push(own, lat_z.at[:, sz - 1], z_ports[sz], "z")

    def main():
        latent = latent_chain()
        next(latent)
        for s in scatters:
            s.start(queue)
        queue.go(3)
        yield
        for _ in latent:
            yield
        width = KVR + RD
        lat = lat_own[:, 0, 0].astype(wide).reshape(rows, KVR + NOPE)[:, :width]
        latent_grad = lat[:, :KVR]
        _, normed, inverse = norm_rows(latent_all[:, :KVR], gain_latent[...])
        lat_in = norm_input_back(latent_grad, normed, inverse, gain_latent[...])
        turned = unrotate(lat[:, KVR:], cosine[...], sine[...])
        own_lag[:, :, KVR:] = jnp.zeros((seqs, local_len, own_lag.shape[-1] - KVR), narrow)
        own_lag[:, :, :KVR] = lat_in.astype(narrow).reshape(seqs, local_len, KVR)
        own_lag[:, :, KVR:width] = turned.astype(narrow).reshape(seqs, local_len, RD)
        wide_acc[...] = dot_nt(own_lag[...].reshape(rows, own_lag.shape[-1]), small[...])
        own_lag[:, :, width:] = logit_grad[...].reshape(seqs, local_len, EXPERTS)
        lag_gather = GroupGather(wires, own_lag, lag_group)
        lag_gather.start()
        own_copy = load(own_lag, lag_group.at[:, 0, 0])
        x = tokens[...].astype(wide).reshape(rows, features)
        _, normed_in, inverse_in = norm_rows(x, gain_attn[...])
        hidden_grad = wide_acc[...] + hidden_sum[...].astype(wide).reshape(rows, features)
        wide_acc[...] = residual_grad[...] + norm_input_back(
            hidden_grad, normed_in, inverse_in, gain_attn[...]
        )
        attn_gain = jnp.sum(hidden_grad * normed_in, axis=0, keepdims=True)
        latent_gain = jnp.sum(latent_grad * normed, axis=0, keepdims=True)
        tokens_grad[...] = wide_acc[...].astype(narrow).reshape(tokens.shape)
        shard = features // nb
        gain_terms[...] = jnp.zeros(gain_terms.shape, wide)
        for b in range(nb):
            gain_terms[b, 0:1, :shard] = attn_gain[:, b * shard : (b + 1) * shard]
            gain_terms[b, 0:1, shard:] = latent_gain
            gain_terms[b, 1:2, :shard] = ffn_gain[:, b * shard : (b + 1) * shard]
        gain_sum = BlockScatter(
            wires, load, gain_terms, lambda ref, owner: ref.at[owner], ("x", "z"), *g_buffers,
            gains_out.at[uly],
        )
        gain_sum.start()
        for _ in lag_gather.chain():
            yield
        own_copy.wait()
        lags = lag_group[...].reshape(nu * rows, own_lag.shape[-1])
        terms = dot(hidden_t[...], lags).astype(narrow)
        lat_wgrad[...] = terms.reshape(lat_wgrad.shape)
        terms = dot(mid_t[...], lags)[:, width:].astype(narrow)
        lat_wgrad[:, :, width:] = terms.reshape(lat_wgrad.shape[:2] + (EXPERTS,))
        w_sum = BlockScatter(
            wires, load, lat_wgrad, lambda ref, owner: ref.at[owner], ("x", "z"), *lw_buffers,
            latent_w_out.at[uly],
        )
        w_sum.start()
        chains = [gain_sum.chain(), w_sum.chain()]
        while chains:
            chain = chains.pop(0)
            if next(chain, True) is None:
                chains.append(chain)
                yield
        outs_ = (latent_w_out, gains_out)
        y_ports = [[wires.port() for _ in range(ny)] for _ in outs_]
        c_ports = [[wires.port() for _ in range(ny)] for _ in outs_]
        member = lambda sy, sc: behind("y", sy) * nc + behind("core", sc)
        for ref, yp, cp in zip(outs_, y_ports, c_ports):
            here = ref.at[uly]
            if ny > 1:
                wires.push(here, here, yp[1], "y")
            wires.push(here, here, cp[0], "core")
        for sy in range(1, ny):
            for ref, yp, cp in zip(outs_, y_ports, c_ports):
                piece = ref.at[member(sy, 0)]
                yield
                wires.arrived(piece, yp[sy], "y")
                if sy + 1 < ny:
                    wires.push(piece, piece, yp[sy + 1], "y")
                wires.push(piece, piece, cp[sy], "core")
        for sy in range(ny):
            for ref, cp in zip(outs_, c_ports):
                yield
                wires.arrived(ref.at[member(sy, 1)], cp[sy], "core")

    queue = Queue()
    weave(main(), [s.chain() for s in scatters] + [output_chain()], 1)
    wires.drain()


def finish(
    hidden_sum, latent_partial, tokens, residual_grad, small, hidden_t, mid_t, logit_grad,
    ffn_gain, gain_attn, gain_latent, latent_all, cosine, sine, residual, shared_sum, picks, slots,
    partials, modes,
):
    nz, nx, ny, nc = (lax.axis_size(a) for a in AXES)
    nb, nu = nz * nx, ny * nc
    seqs, local_len, features = tokens.shape
    rows = seqs * local_len
    shape = jax.ShapeDtypeStruct
    shards = []
    for p, (dim, _) in zip(partials, modes):
        size = list(p.shape)
        size[dim] //= nb
        shards.append(tuple(size))
    width, shard = KVR + RD, features // nb
    padded = small.shape[-1]
    few = lambda n: max(n - 1, 1)
    scratch = [
        pltpu.VMEM((seqs, nx, nz, local_len, KVR + NOPE), narrow),
        pltpu.VMEM((seqs, few(nx), nz, local_len, KVR + NOPE), narrow),
        pltpu.VMEM((seqs, few(nz), local_len, KVR + NOPE), narrow),
        pltpu.VMEM((seqs, local_len, padded), narrow),
        pltpu.VMEM((seqs, ny, nc, local_len, padded), narrow),
        pltpu.VMEM((rows, features), wide),
        pltpu.VMEM((nb, shard // nu, padded), narrow),
        pltpu.VMEM((nb, 8, shard + KVR), wide),
        pltpu.VMEM((nz, nx * nu, *slots.shape[2:]), narrow),
        pltpu.VMEM((nz, rows, features), narrow),
        pltpu.VMEM((few(nz), rows, features), narrow),
    ]
    for size, (_, axes) in zip(shards, modes):
        scratch += scatter_scratch(size, axes)
    scratch += scatter_scratch((shard // nu, padded), ("x", "z"))
    scratch += scatter_scratch((8, shard + KVR), ("x", "z"), wide)
    scratch += [
        pltpu.SemaphoreType.DMA((256,)),
        pltpu.SemaphoreType.DMA((256,)),
        pltpu.SemaphoreType.DMA((256,)),
    ]
    return pl.pallas_call(
        functools.partial(finish_kernel, modes=modes),
        out_shape=[
            shape(tokens.shape, narrow),
            shape(tokens.shape, narrow),
            shape((nu, shard // nu, padded), wide),
            shape((nu, 8, shard + KVR), wide),
            *[shape(size, wide) for size in shards],
        ],
        in_specs=[VMEM, ANY] + [VMEM] * 15 + [ANY] * (1 + len(partials)),
        out_specs=[VMEM] * (4 + len(partials)),
        scratch_shapes=scratch,
        compiler_params=pltpu.CompilerParams(
            collective_id=1, has_side_effects=True, vmem_limit_bytes=62 * 1024 * 1024
        ),
        cost_estimate=costs(190),
    )(
        hidden_sum, latent_partial, tokens, residual_grad, small, hidden_t, mid_t, logit_grad,
        ffn_gain, gain_attn, gain_latent, latent_all, cosine, sine, residual, shared_sum, picks, slots,
        *partials,
    )


class Layer:
    def __init__(self):
        self.sizes = [lax.axis_size(a) for a in AXES[1:]]
        self.count = self.sizes[0] * self.sizes[1] * self.sizes[2]

    def offsets(self, k):
        _, ny, nc = self.sizes
        return k // (ny * nc), k // nc % ny, k % nc

    def device(self, k, sign=1):
        return {
            axis: lax.rem(lax.axis_index(axis) + (sign * d) % n, n)
            for axis, d, n in zip(AXES[1:], self.offsets(k), self.sizes)
        }

    def number(self, k, sign=1):
        where = self.device(k, sign)
        return (where["x"] * self.sizes[1] + where["y"]) * self.sizes[2] + where["core"]

    def greet(self):
        barrier = pltpu.get_barrier_semaphore()
        for k in range(1, self.count):
            pl.semaphore_signal(barrier, inc=1, device_id=self.device(k), device_id_type=MESH)
        pl.semaphore_signal(
            barrier, inc=1, device_id={"z": behind("z", 1)}, device_id_type=MESH
        )
        pl.semaphore_wait(barrier, self.count)

    def push(self, wires, src, dst, port, k):
        copy = pltpu.make_async_remote_copy(
            src_ref=src,
            dst_ref=dst,
            send_sem=wires.send.at[port],
            recv_sem=wires.recv.at[port],
            device_id=self.device(k),
            device_id_type=MESH,
        )
        copy.start()
        wires.sent.append(copy)


def dispatch_kernel(
    partial, tokens, gain, router, member, picks, top, *rest, plan,
):
    count = len(plan)
    shards, rest = rest[:count], rest[count:]
    residual_out, gates_out, hidden_out, group_out, rows_out, tops_out, *rest = rest
    wholes, rest = rest[:count], rest[count:]
    own, other, came, hidden, line, outgoing, send, recv, local = rest
    nz, nx = lax.axis_size("z"), lax.axis_size("x")
    seqs, local_len, features = tokens.shape
    rows = seqs * local_len
    layer = Layer()
    layer.greet()
    wires = Wires(send, recv)
    used, waited = [], set()

    def load(src, dst):
        copy = pltpu.make_async_copy(src, dst, local.at[len(used)])
        used.append(copy)
        copy.start()
        return copy

    def main():
        for _ in group_sum_chain(wires, partial, own, other, came, load):
            yield
        waited.update(id(copy) for copy in used[: own.shape[1]])
        residual = tokens[...].astype(wide).reshape(rows, features)
        residual = residual + own[:, 0].astype(wide).reshape(rows, features)
        residual_out[...] = residual
        normed = norm_rows(residual, gain[...])[0].astype(narrow)
        hidden_out[...] = normed
        hidden[...] = normed.reshape(tokens.shape)
        line[0, :, :features] = normed
        logits = jnp.where(member[...] > 0, dot(normed, router[...]), -jnp.inf)
        raised = jnp.exp(logits - jnp.max(logits, axis=1, keepdims=True))
        gates = raised / jnp.sum(raised, axis=1, keepdims=True)
        gates_out[...] = gates
        high = gates.astype(narrow).astype(wide)
        line[0, :, features:] = jnp.concatenate([high, gates - high], axis=1).astype(narrow)
        z_ports = [wires.port() for _ in range(nz)]
        wires.push(line.at[0], line.at[1], z_ports[1], "z")
        gather = GroupGather(wires, hidden, group_out)
        gather.start()
        load(hidden, group_out.at[:, 0, 0])
        ports = [[wires.port() for _ in range(layer.count)] for _ in range(nz)]
        me = layer.number(0)
        chain = gather.chain()
        for s in range(nz):
            if s:
                yield
                wires.arrived(line.at[s], z_ports[s], "z")
                if s + 1 < nz:
                    wires.push(line.at[s], line.at[s + 1], z_ports[s + 1], "z")
            outgoing[s] = dot_tn(picks[s], line[s]).astype(narrow).reshape(outgoing.shape[1:])
            for k in range(1, layer.count):
                target = layer.number(k)
                layer.push(wires, outgoing.at[s, target], rows_out.at[me, s], ports[s][k], k)
            load(outgoing.at[s, me], rows_out.at[me, s])
            next(chain, None)
        for _ in chain:
            pass
        for s in range(nz):
            yield
            for k in range(1, layer.count):
                wires.arrived(rows_out.at[layer.number(k, -1), s], ports[s][k], "z")

    def tops():
        z_ports = [wires.port() for _ in range(nz)]
        x_ports = [wires.port() for _ in range(nx)]
        mine = load(top, tops_out.at[0, 0])
        waited.add(id(mine))
        wires.push(top, tops_out.at[0, 1], z_ports[1], "z")
        for s in range(1, nz):
            yield
            wires.arrived(tops_out.at[0, s], z_ports[s], "z")
            if s + 1 < nz:
                wires.push(tops_out.at[0, s], tops_out.at[0, s + 1], z_ports[s + 1], "z")
        mine.wait()
        wires.push(tops_out.at[0], tops_out.at[1], x_ports[1], "x")
        for s in range(1, nx):
            yield
            wires.arrived(tops_out.at[s], x_ports[s], "x")
            if s + 1 < nx:
                wires.push(tops_out.at[s], tops_out.at[s + 1], x_ports[s + 1], "x")

    def array_chain(src, dst, dim, x_first):
        place = (rows_of if dim == 0 else columns_of)(src.shape[dim])
        gather = BlockGather(wires, src, dst, place, x_first)
        load(src, gather.at(0, 0))
        yield from gather.chain()

    first = main()
    next(first)
    others = [array_chain(a, b, *mode) for a, b, mode in zip(shards, wholes, plan)]
    weave(first, others + [tops()], 1)
    for copy in used:
        if id(copy) not in waited:
            copy.wait()
    wires.drain()


def whole_array(w, dim):
    size = list(w.shape)
    size[dim] *= lax.axis_size("z") * lax.axis_size("x")
    return jax.ShapeDtypeStruct(tuple(size), w.dtype)


def dispatch(partial, tokens, gain, router, member, picks, top, units, shards, plan):
    nz, nx, ny, nc = (lax.axis_size(a) for a in AXES)
    seqs, local_len, features = tokens.shape
    rows = seqs * local_len
    layer = nx * ny * nc
    shape = jax.ShapeDtypeStruct
    extended = features + 2 * EXPERTS
    part = pltpu.VMEM((seqs, ny, local_len, features), narrow)
    return pl.pallas_call(
        functools.partial(dispatch_kernel, plan=plan),
        out_shape=[
            shape((rows, features), wide),
            shape((rows, EXPERTS), wide),
            shape((rows, features), narrow),
            shape((seqs, ny, nc, local_len, features), narrow),
            shape((layer, nz, units, SLOTS, extended), narrow),
            shape((nx, nz) + top.shape, wide),
            *[whole_array(w, dim) for w, (dim, _) in zip(shards, plan)],
        ],
        in_specs=[ANY] + [VMEM] * 6 + [ANY] * len(shards),
        out_specs=[VMEM, VMEM, VMEM, ANY, ANY, VMEM] + [ANY] * len(shards),
        scratch_shapes=[
            part, part, part,
            pltpu.VMEM((seqs, local_len, features), narrow),
            pltpu.VMEM((nz, rows, extended), narrow),
            pltpu.VMEM((nz, layer, units, SLOTS, extended), narrow),
            pltpu.SemaphoreType.DMA((256,)),
            pltpu.SemaphoreType.DMA((256,)),
            pltpu.SemaphoreType.DMA((32,)),
        ],
        compiler_params=pltpu.CompilerParams(
            collective_id=2, has_side_effects=True, vmem_limit_bytes=48 * 1024 * 1024
        ),
        cost_estimate=costs(80),
    )(partial, tokens, gain, router, member, picks, top, *shards)


def return_kernel(
    returned, partial, shared_partial, residual, gates, router, gain, grads, picks, *rest, modes,
):
    count = len(modes)
    partials, rest = rest[:count], rest[count:]
    residual_grad_out, group_out, logit_out, gain_out, shared_out, *rest = rest
    outs, rest = rest[:count], rest[count:]
    own, other, came, sh_own, sh_other, sh_came, back, line, own_grad, *rest = rest
    buffers, rest = rest[: 3 * count], rest[3 * count :]
    send, recv, local = rest
    nz, nx = lax.axis_size("z"), lax.axis_size("x")
    seqs, local_len, features = grads.shape
    rows = seqs * local_len
    layer = Layer()
    layer.greet()
    wires = Wires(send, recv)
    used = []

    def load(src, dst):
        copy = pltpu.make_async_copy(src, dst, local.at[len(used)])
        used.append(copy)
        copy.start()
        return copy

    queue = Queue()
    scatters = [
        BlockScatter(
            wires, load, partials[i],
            (rows_of if dim == 0 else columns_of)(partials[i].shape[dim] // (nz * nx)), axes,
            *buffers[3 * i : 3 * i + 3], outs[i],
        )
        for i, (dim, axes) in enumerate(modes)
    ]

    def main():
        me = layer.number(0)
        ports = [[wires.port() for _ in range(layer.count)] for _ in range(nz)]
        z_ports = [wires.port() for _ in range(nz)]
        order = [*range(1, nz), 0]
        own_copies = {}
        for s in order:
            for k in range(1, layer.count):
                layer.push(
                    wires, returned.at[layer.number(k), s], back.at[s, me], ports[s][k], k
                )
            own_copies[s] = load(returned.at[me, s], back.at[s, me])
        shared = group_sum_chain(wires, partial, own, other, came, load)
        next(shared)
        yield
        extended = back.shape[-1]
        total = None
        for s in order:
            for k in range(1, layer.count):
                wires.arrived(back.at[s, layer.number(k, -1)], ports[s][k], "z")
            own_copies[s].wait()
            term = dot(picks[s], back[s].reshape(picks.shape[2], extended))
            if s != 1:
                last = (s or nz) - 1
                yield
                wires.arrived(line.at[1, last - 1], z_ports[last], "z")
                term = term + line[1, last - 1].astype(wide)
            if s:
                line[0, s - 1] = term.astype(narrow)
                wires.push(line.at[0, s - 1], line.at[1, s - 1], z_ports[s], "z")
            else:
                total = term
            next(shared, None)
        for _ in shared:
            pass
        lanes = total[:, features:]
        gate_grad = lanes[:, :EXPERTS] + lanes[:, EXPERTS:]
        weight = gates[...]
        logit_grad = (
            weight * (gate_grad - jnp.sum(weight * gate_grad, axis=1, keepdims=True))
        ).astype(narrow)
        logit_out[...] = logit_grad
        mid = total[:, :features] + own[:, 0].astype(wide).reshape(rows, features)
        mid = mid + dot_nt(logit_grad, router[...])
        _, normed, inverse = norm_rows(residual[...], gain[...])
        grad = grads[...].astype(wide).reshape(rows, features)
        grad = grad + norm_input_back(mid, normed, inverse, gain[...])
        residual_grad_out[...] = grad
        own_grad[...] = grad.astype(narrow).reshape(grads.shape)
        gather = GroupGather(wires, own_grad, group_out)
        gather.start()
        mine = load(own_grad, group_out.at[:, 0, 0])
        gain_out[...] = jnp.sum(mid * normed, axis=0, keepdims=True)
        yield from gather.chain()
        mine.wait()

    def shared_sum():
        yield from group_sum_chain(wires, shared_partial, sh_own, sh_other, sh_came, load)
        shared_out[...] = sh_own[:, 0]

    first = main()
    next(first)
    for s in scatters:
        s.start(queue)
    queue.go(2)
    weave(first, [s.chain() for s in scatters] + [shared_sum()], 1)
    wires.drain()


def come_back(
    returned, partial, shared_partial, residual, gates, router, gain, grads, picks, partials, modes
):
    nz, nx, ny, nc = (lax.axis_size(a) for a in AXES)
    seqs, local_len, features = grads.shape
    rows = seqs * local_len
    shape = jax.ShapeDtypeStruct
    extended = returned.shape[-1]
    part = pltpu.VMEM((seqs, ny, local_len, features), narrow)
    shards = []
    for p, (dim, _) in zip(partials, modes):
        size = list(p.shape)
        size[dim] //= nz * nx
        shards.append(tuple(size))
    scratch = [
        part, part, part, part, part, part,
        pltpu.VMEM((nz, nx * ny * nc) + returned.shape[2:], narrow),
        pltpu.VMEM((2, nz - 1, rows, extended), narrow),
        pltpu.VMEM((seqs, local_len, features), narrow),
    ]
    for size, (_, axes) in zip(shards, modes):
        scratch += scatter_scratch(size, axes)
    scratch += [
        pltpu.SemaphoreType.DMA((256,)),
        pltpu.SemaphoreType.DMA((256,)),
        pltpu.SemaphoreType.DMA((96,)),
    ]
    return pl.pallas_call(
        functools.partial(return_kernel, modes=modes),
        out_shape=[
            shape((rows, features), wide),
            shape((seqs, ny, nc, local_len, features), narrow),
            shape((rows, EXPERTS), narrow),
            shape((1, features), wide),
            shape(grads.shape, narrow),
            *[shape(size, wide) for size in shards],
        ],
        in_specs=[ANY, ANY, ANY] + [VMEM] * 6 + [ANY] * len(partials),
        out_specs=[VMEM, ANY, VMEM, VMEM, VMEM] + [VMEM] * len(partials),
        scratch_shapes=scratch,
        compiler_params=pltpu.CompilerParams(
            collective_id=3, has_side_effects=True, vmem_limit_bytes=56 * 1024 * 1024
        ),
        cost_estimate=costs(100),
    )(returned, partial, shared_partial, residual, gates, router, gain, grads, picks, *partials)


def expert_kernel(
    rows_in, grads_in, wg, wu, wd, *rest, split, plan,
):
    count = len(plan)
    shards, rest = rest[:count], rest[count:]
    returned, outputs, gated, lin_gate, lin_up, *rest = rest
    wholes, rest = rest[:count], rest[count:]
    (
        rows, grads, bg, bu, bd, act, gated_buf, gate_buf, up_buf, dots,
        back_stage, out_stage, send, recv, local, turn,
    ) = rest
    nz, nx, ny, nc = (lax.axis_size(a) for a in AXES)
    nb = nz * nx
    layer = nx * ny * nc
    units, features, hidden = wg.shape
    first_unit = (
        (lax.axis_index("z") * nx + lax.axis_index("x")) * ny + lax.axis_index("y")
    ) * nc + lax.axis_index("core")
    first_unit = first_unit * units
    per = min(layer, max(1, 512 // (nz * SLOTS)))
    block = per * nz * SLOTS
    blocks = layer // per
    wires = Wires(send, recv)
    if count:
        greet(("z", "x"))
    used = []

    def load(src, dst):
        copy = pltpu.make_async_copy(src, dst, local.at[len(used)])
        used.append(copy)
        copy.start()
        return copy

    gathers = [
        BlockGather(
            wires, src, dst, (rows_of if dim == 0 else columns_of)(src.shape[dim]), x_first
        )
        for src, dst, (dim, x_first) in zip(shards, wholes, plan)
    ]

    def transfers():
        for g in gathers:
            g.forward(0, 0)
        yield
        plans = [g.rounds() for g in gathers]
        for step in range(max([len(p) for p in plans] + [0])):
            for g, p in zip(gathers, plans):
                for slot in p[step] if step < len(p) else []:
                    g.take(*slot)
                    yield

    moving = transfers()
    next(moving, None)

    def tick():
        next(moving, None)

    def fetch(a):
        slot = a % rows.shape[0]
        return [
            load(rows_in.at[:, :, a], rows.at[slot]),
            load(wg.at[a], bg.at[slot]),
            load(wu.at[a], bu.at[slot]),
            load(grads_in.at[:, :, a], grads.at[slot]),
            load(wd.at[a], bd.at[slot]),
        ]

    fetched = fetch(0)
    kept = [load(g.src, g.at(0, 0)) for g in gathers]

    def pump(low, high, body, copies):
        @pl.loop(low, high)
        def _(i):
            slot = lax.rem(i, 2)

            @pl.when(i >= 2)
            def _():
                for copy in copies(i - 2, slot):
                    copy.wait()

            body(i, slot)
            for copy in copies(i, slot):
                copy.start()

    def settle(total, copies):
        for i in range(max(0, total - 2), total):
            for copy in copies(i, i % 2):
                copy.wait()

    saved, extra_copy = [], None
    for a in range(units):
        slot_a = a % rows.shape[0]
        expert = (first_unit + a) // split
        for copy in fetched[:3]:
            copy.wait()
        waiting = fetched[3:]

        def weights_of(b):
            extra = rows[slot_a, pl.ds(b * per, per), :, :, features:].astype(wide)
            extra = extra.reshape(block, 2 * EXPERTS)
            lane = lax.broadcasted_iota(jnp.int32, extra.shape, 1)
            mine = (lane == expert) | (lane == expert + EXPERTS)
            return jnp.sum(jnp.where(mine, extra, 0.0), axis=1, keepdims=True)

        def row_block(ref, b, columns):
            return ref[slot_a, pl.ds(b * per, per), :, :, columns].reshape(block, -1)

        for copy in waiting:
            copy.wait()
        if a + 1 < units:
            fetched = fetch(a + 1)

        def forward(b, cols):
            span = pl.ds(pl.multiple_of(b * block, block), block)
            picked = row_block(rows, b, slice(0, features))
            lin = dot(picked, bg[slot_a, :, cols])
            up = dot(picked, bu[slot_a, :, cols])
            grad = dot_nt(row_block(grads, b, slice(None)), bd[slot_a, cols, :]) * weights_of(b)
            s = jax.nn.sigmoid(lin)
            silu = lin * s
            value = (silu * up).astype(narrow)
            act[span, cols] = value
            gated_buf[span, cols] = (value.astype(wide) * weights_of(b)).astype(narrow)
            gate_buf[span, cols] = (grad * up * (s * (1.0 + lin * (1.0 - s)))).astype(narrow)
            up_buf[span, cols] = (grad * silu).astype(narrow)

        full = hidden // 256
        for copy in saved:
            copy.wait()

        @pl.loop(0, blocks)
        def _(b):
            @pl.loop(0, full)
            def _(i):
                forward(b, pl.ds(pl.multiple_of(i * 256, 256), 256))

            if hidden % 256:
                forward(b, pl.ds(full * 256, hidden % 256))

        saved = [
            load(src, dst.at[a])
            for src, dst in ((gated_buf, gated), (gate_buf, lin_gate), (up_buf, lin_up))
        ]
        tick()
        tick()
        dots[...] = jnp.zeros(dots.shape, wide)

        def spread(i):
            return pl.ds(pl.multiple_of(i * 256, 256), 256)

        def back_copies(i, slot):
            return [
                pltpu.make_async_copy(
                    back_stage.at[slot], returned.at[:, :, a, :, spread(i)], turn.at[0, slot]
                ),
                pltpu.make_async_copy(
                    out_stage.at[slot], outputs.at[:, :, a, :, spread(i)], turn.at[1, slot]
                ),
            ]

        def backward(i, slot):
            @pl.loop(0, blocks)
            def _(b):
                span = pl.ds(pl.multiple_of(b * block, block), block)
                cols = spread(i)
                out = dot(act[span, :], bd[slot_a, :, cols])
                dots[span, :] += jnp.sum(
                    out * row_block(grads, b, cols).astype(wide), axis=1, keepdims=True
                )
                shaped = (per, nz, SLOTS, 256)
                out_stage[slot, pl.ds(b * per, per)] = (
                    (out * weights_of(b)).astype(narrow).reshape(shaped)
                )
                inward = dot_nt(gate_buf[span, :], bg[slot_a, cols, :]) + dot_nt(
                    up_buf[span, :], bu[slot_a, cols, :]
                )
                back_stage[slot, pl.ds(b * per, per)] = inward.astype(narrow).reshape(shaped)

        chunks = features // 256
        for part in range(4):
            pump(part * chunks // 4, (part + 1) * chunks // 4, backward, back_copies)
            tick()
        settle(chunks, back_copies)

        @pl.loop(0, blocks)
        def _(b):
            span = pl.ds(pl.multiple_of(b * block, block), block)
            lane = lax.broadcasted_iota(jnp.int32, (block, 2 * EXPERTS), 1)
            value = dots[span, :]
            high = value.astype(narrow).astype(wide)
            lanes = jnp.where(lane == expert, high, 0.0)
            lanes = jnp.where(lane == expert + EXPERTS, value - high, lanes)
            rest_ = lanes.astype(narrow).reshape(per, nz, SLOTS, 2 * EXPERTS)
            back_stage[0, pl.ds(b * per, per), :, :, : 2 * EXPERTS] = rest_

        extra_copy = load(
            back_stage.at[0, :, :, :, : 2 * EXPERTS], returned.at[:, :, a, :, features:]
        )
        extra_copy.wait()
    for copy in saved:
        copy.wait()
    for _ in moving:
        pass
    for copy in kept:
        copy.wait()
    wires.drain()


def run_experts(rows_in, grads_in, wg, wu, wd, shards, plan, split):
    nz, nx, ny, nc = (lax.axis_size(a) for a in AXES)
    nb = nz * nx
    units, features, hidden = wg.shape
    layer = nx * ny * nc
    total = nz * layer * SLOTS
    shape = jax.ShapeDtypeStruct
    extended = rows_in.shape[-1]

    slots = min(units, 2)
    lines = (layer, nz, SLOTS)
    return pl.pallas_call(
        functools.partial(expert_kernel, split=split, plan=plan),
        out_shape=[
            shape(rows_in.shape, narrow),
            shape(grads_in.shape, narrow),
            *[shape((units, total, hidden), narrow)] * 3,
            *[whole_array(w, dim) for w, (dim, _) in zip(shards, plan)],
        ],
        in_specs=[ANY] * (5 + len(shards)),
        out_specs=[ANY] * (5 + len(shards)),
        scratch_shapes=[
            pltpu.VMEM((slots,) + lines + (extended,), narrow),
            pltpu.VMEM((slots,) + lines + (features,), narrow),
            pltpu.VMEM((slots, features, hidden), narrow),
            pltpu.VMEM((slots, features, hidden), narrow),
            pltpu.VMEM((slots, hidden, features), narrow),
            pltpu.VMEM((total, hidden), narrow),
            pltpu.VMEM((total, hidden), narrow),
            pltpu.VMEM((total, hidden), narrow),
            pltpu.VMEM((total, hidden), narrow),
            pltpu.VMEM((total, 1), wide),
            pltpu.VMEM((2,) + lines + (256,), narrow),
            pltpu.VMEM((2,) + lines + (256,), narrow),
            pltpu.SemaphoreType.DMA((64,)),
            pltpu.SemaphoreType.DMA((64,)),
            pltpu.SemaphoreType.DMA((32,)),
            pltpu.SemaphoreType.DMA((4, 2)),
        ],
        compiler_params=pltpu.CompilerParams(
            collective_id=4 if shards else None, has_side_effects=bool(shards),
            vmem_limit_bytes=60 * 1024 * 1024,
        ),
        cost_estimate=costs(80),
    )(rows_in, grads_in, wg, wu, wd, *shards)


def unit_grads_kernel(rows, grads, gated, lin_gate, lin_up, gate_out, up_out, down_out):
    picked = rows[...].reshape(gated.shape[1], rows.shape[-1])
    gate_out[0] = dot_tn(picked, lin_gate[0])
    up_out[0] = dot_tn(picked, lin_up[0])
    down_out[0] = dot_tn(gated[0], grads[...].reshape(gated.shape[1], grads.shape[-1]))


def unit_grads(rows, grads, gated, lin_gate, lin_up):
    layer, nz, units, _, features = grads.shape
    _, total, hidden = gated.shape
    step = 512 if total <= 512 else 128
    lines = (layer, nz, 1, SLOTS, step)
    shape = jax.ShapeDtypeStruct
    line_spec = pl.BlockSpec(lines, lambda a, i: (0, 0, a, 0, i))
    unit_spec = pl.BlockSpec((1, total, hidden), lambda a, i: (a, 0, 0))
    wide_spec = pl.BlockSpec((1, step, hidden), lambda a, i: (a, i, 0))
    return pl.pallas_call(
        unit_grads_kernel,
        grid=(units, features // step),
        in_specs=[line_spec, line_spec, unit_spec, unit_spec, unit_spec],
        out_specs=[wide_spec, wide_spec, pl.BlockSpec((1, hidden, step), lambda a, i: (a, 0, i))],
        out_shape=[
            shape((units, features, hidden), wide),
            shape((units, features, hidden), wide),
            shape((units, hidden, features), wide),
        ],
        cost_estimate=costs(35),
        compiler_params=pltpu.CompilerParams(vmem_limit_bytes=61 * 1024 * 1024),
    )(rows, grads, gated, lin_gate, lin_up)


def per_device(
    tokens, attn_gain, w_query, w_latent, latent_gain, w_expand, w_output, ffn_gain, w_router,
    w_shared_gate, w_shared_up, w_shared_down, w_gate, w_up, w_down, routes, clip_limit, out_grad,
):
    seqs, local_len, features = tokens.shape
    rows = seqs * local_len
    qk = NOPE + RD
    nz, nx, ny, nc = (lax.axis_size(a) for a in ("z", "x", "y", "core"))
    zi, xi, yi, ci = (lax.axis_index(a) for a in ("z", "x", "y", "core"))
    nb, nu = nz * nx, ny * nc
    layer = nx * nu
    heads = H // nu
    group = nu * rows
    all_rows = nb * group
    upd = w_gate.shape[0]
    split = upd * nz * layer // EXPERTS
    scale = qk ** (-0.5)
    GROUP = ("y", "core")
    ALL = ("z", "x", "y", "core")
    LAYER = ("x", "y", "core")

    def scatter_blk(whole, dim):
        size = whole.shape[dim] // nb
        blocks = []
        for sz in range(nz):
            for sx in range(nx):
                owner = ((zi + nz - sz) % nz) * nx + (xi + nx - sx) % nx
                blocks.append(lax.dynamic_slice_in_dim(whole, owner * size, size, dim))
        return tree_sum(blocks, ("z", "x"))

    def group_gather(value):
        return jnp.concatenate(
            [p.reshape(seqs, local_len, -1) for p in flat_ring(value, GROUP)], axis=1
        ).reshape(group, -1)

    def group_scatter(value):
        blocks = value.reshape(seqs, nu, local_len, -1)
        return tree_sum([blocks[:, i].reshape(rows, -1) for i in range(nu)], GROUP)

    def group_sum(value):
        for axis in GROUP:
            items = ring(value, axis)
            value = sum(item.astype(wide) for item in items)
        return value

    def device_positions(blk, u):
        return (blk * nu + u) * local_len + jnp.arange(local_len, dtype=jnp.int32)

    local_pos = device_positions(zi * nx + xi, yi * nc + ci)
    group_pos = jnp.concatenate(
        [
            device_positions(zi * nx + xi, (yi + ny - sy) % ny * nc + (ci + nc - sc) % nc)
            for sy in range(ny)
            for sc in range(nc)
        ]
    )
    key_pos = jnp.concatenate(
        [
            device_positions(
                (zi + nz - sz) % nz * nx + (xi + nx - sx) % nx,
                (yi + ny - sy) % ny * nc + (ci + nc - sc) % nc,
            )
            for sc in range(nc)
            for sy in range(ny)
            for sx in range(nx)
            for sz in range(nz)
        ]
    )

    shard = attn_gain.shape[0]
    lat_len = latent_gain.shape[0]
    gains = jnp.concatenate(
        [
            jnp.pad(jnp.stack([attn_gain, ffn_gain]).astype(wide), ((0, 0), (0, KVR - shard))),
            lax.dynamic_update_slice(
                jnp.zeros((1, KVR), wide),
                latent_gain.astype(wide)[None],
                (0, (zi * nx + xi) * lat_len),
            ),
            jnp.zeros((5, KVR), wide),
        ],
        axis=0,
    )
    small = jnp.concatenate([w_latent, w_router], axis=1).reshape(nu, shard // nu, -1)
    route_rows = jnp.swapaxes(routes, 0, 1).reshape(rows, TOP)
    cos_local, sin_local = rotary_tables(jnp.tile(local_pos, seqs))
    (
        gains_all, small_all, query_w, expand_w, output_w,
        hidden_group, grad_group, picks, own_member, grad_slots, latents, _, latent_all,
    ) = start(
        tokens, out_grad, cos_local, sin_local, gains, small,
        jnp.pad(route_rows, ((0, 0), (0, 128 - TOP)), constant_values=-1),
        (w_query, w_expand, w_output), upd, split,
    )
    blk = ("z", "x")
    grad_slots, later_gate, later_up, later_down = lax.optimization_barrier(
        (grad_slots, w_shared_gate, w_shared_up, w_shared_down)
    )
    gate_w = lax.all_gather(later_gate, blk, axis=0, tiled=True)
    up_w = lax.all_gather(later_up, blk, axis=0, tiled=True)
    down_w = lax.all_gather(later_down, blk, axis=1, tiled=True)
    tokens_local = tokens.reshape(rows, features)
    grad_narrow = out_grad.reshape(rows, features)
    small_whole = small_all.reshape(features, -1)
    latent_w = small_whole[:, : KVR + RD]
    router_w = small_whole[:, KVR + RD :]
    gain_attn = gains_all[:, 0, :shard].reshape(-1)
    gain_ffn = gains_all[:, 1, :shard].reshape(-1)
    gain_latent = jnp.sum(gains_all[:, 2], axis=0)
    inputs = tokens_local.astype(wide)
    _, normed_in, inverse_in = norm_rows(inputs, gain_attn)
    _, normed_lat, inverse_lat = norm_rows(latent_all[:, :KVR], gain_latent)
    length = all_rows // seqs
    latent_keys = latents.reshape(seqs, length, KVR + NOPE)
    latent_rows = latents.reshape(all_rows, KVR + NOPE)
    expand_w = jnp.pad(expand_w, ((0, NOPE), (0, 0)))
    hidden_group = hidden_group.reshape(group, features)
    grad_group = grad_group.reshape(group, features)

    def swap_layer(values):
        return lax.all_to_all(values, LAYER, split_axis=0, concat_axis=0, tiled=True)

    grad_slots = swap_layer(grad_slots)

    reach = nu * local_len
    cos_group, sin_group = rotary_tables(group_pos)
    query_lin = dot(hidden_group, query_w)
    expanded = dot(latent_rows, expand_w, narrow)
    query_pos, keys_pos = group_pos[:, None], key_pos[None, :]
    query_rows, attended, stats = attend(
        query_lin, cos_group, sin_group, expanded, latent_keys, query_pos, keys_pos, seqs, heads
    )
    top = jnp.pad(jnp.max(stats[..., 0], axis=(0, 2))[None], ((0, 7), (0, 128 - heads)))
    split_group = (seqs, ny, nc, local_len, features)
    residual, gates, hidden_mid, hidden_mid_group, expert_slots, tops = dispatch(
        dot(attended, output_w, narrow).reshape(split_group),
        tokens, gain_ffn[None], router_w, own_member, picks, top, upd,
        (), (),
    )
    clip_value = clip_limit[0]
    clip_factor = clip_value / jnp.maximum(jnp.max(tops, axis=(0, 1))[0, :heads], clip_value)
    hidden_mid_group = hidden_mid_group.reshape(group, features)

    returned, outputs, gated, lin_gate, lin_up = run_experts(
        expert_slots, grad_slots, w_gate, w_up, w_down, (), (), split
    )

    shared_gate = dot(hidden_mid_group, gate_w)
    shared_up = dot(hidden_mid_group, up_w)
    shared_act = (jax.nn.silu(shared_gate) * shared_up).astype(narrow)
    shared_partial = dot(shared_act, down_w, narrow)
    shared_act_grad = dot_nt(grad_group, down_w)
    shared_gate_grad = (shared_act_grad * shared_up * silu_slope(shared_gate)).astype(narrow)
    shared_up_grad = (shared_act_grad * jax.nn.silu(shared_gate)).astype(narrow)
    mid_shared = dot_nt(shared_gate_grad, gate_w) + dot_nt(shared_up_grad, up_w)

    usual = ("x", "z")
    def spread_sum(value, dim):
        return lax.psum_scatter(value, blk, scatter_dimension=dim, tiled=True).astype(wide)

    shared_gate_wgrad = dot_tn(hidden_mid_group, shared_gate_grad, narrow)
    shared_up_wgrad, shared_down_wgrad, returned = lax.optimization_barrier(
        (
            dot_tn(hidden_mid_group, shared_up_grad, narrow),
            dot_tn(shared_act, grad_group, narrow),
            returned,
        )
    )
    shared_up_wgrad = spread_sum(shared_up_wgrad, 0)
    shared_down_wgrad = spread_sum(shared_down_wgrad, 1)
    (
        residual_grad, attn_grad, logit_grad, ffn_gain_part, shared_sum, shared_gate_wgrad,
    ) = come_back(
        returned, mid_shared.astype(narrow).reshape(split_group),
        shared_partial.reshape(split_group), residual, gates,
        router_w, gain_ffn[None], out_grad, picks,
        (shared_gate_wgrad,), ((0, usual),),
    )
    attn_grad = attn_grad.reshape(group, features)
    outputs, attn_grad = lax.optimization_barrier((outputs, attn_grad))
    outputs = swap_layer(outputs)
    attended_grad = dot_nt(attn_grad, output_w, narrow)
    attended_grad, shared_up_wgrad = lax.optimization_barrier((attended_grad, shared_up_wgrad))
    output_wgrad = dot_tn(attended, attn_grad, narrow)

    query_lin_grad, expand_grad, rope_partial = attend_back(
        query_rows, cos_group, sin_group, expanded, latent_keys, query_pos, keys_pos, stats,
        attended_grad, seqs, heads,
    )
    hidden_partial = dot_nt(query_lin_grad, query_w, narrow)
    latent_partial = (
        dot_nt(expand_grad, expand_w, narrow).reshape(seqs, length, KVR + NOPE)
        + jnp.pad(rope_partial.astype(narrow), ((0, 0), (0, 0), (KVR, 0)))
    )
    latent_blocks = latent_partial.reshape(seqs, nc, ny, nx, nz, local_len, KVR + NOPE)
    latent_blocks = ring_sum([latent_blocks[:, i] for i in range(nc)], "core").astype(narrow)
    latent_blocks, gated, outputs, late_hidden, late_mid = lax.optimization_barrier(
        (latent_blocks, gated, outputs, hidden_group, hidden_mid_group)
    )
    gated, shared_down_wgrad = lax.optimization_barrier((gated, shared_down_wgrad))
    gate_wgrad, up_wgrad, down_wgrad = unit_grads(expert_slots, grad_slots, gated, lin_gate, lin_up)
    latent_blocks = ring_sum([latent_blocks[:, i] for i in range(ny)], "y").astype(narrow)
    hidden_blocks = hidden_partial.reshape(split_group)
    hidden_blocks = ring_sum([hidden_blocks[:, :, i] for i in range(nc)], "core").astype(narrow)
    hidden_sum = ring_sum([hidden_blocks[:, i] for i in range(ny)], "y").astype(narrow)
    query_wgrad = dot_tn(hidden_group, query_lin_grad, narrow)
    expand_wgrad = dot_tn(latent_rows, expand_grad, narrow)
    uly = yi * nc + ci
    hidden_sum, gate_wgrad, up_wgrad, down_wgrad = lax.optimization_barrier(
        (hidden_sum, gate_wgrad, up_wgrad, down_wgrad)
    )

    def own_columns(values):
        return lax.dynamic_slice_in_dim(
            values.T.reshape(nb, nu, shard // nu, group), uly, 1, 1
        ).reshape(features // nu, group)

    (
        tokens_grad, block_out, latent_wgrad, gain_sums, query_wgrad, expand_wgrad, output_wgrad,
    ) = finish(
        hidden_sum, latent_blocks,
        tokens, residual_grad, small_whole, own_columns(late_hidden), own_columns(late_mid),
        logit_grad, ffn_gain_part, gain_attn[None], gain_latent[None],
        latent_all, cos_local, sin_local, residual,
        shared_sum, picks, outputs,
        (query_wgrad, expand_wgrad[:KVR], output_wgrad),
        ((0, usual), (0, usual), (1, usual)),
    )
    width = KVR + RD
    small_wgrad = latent_wgrad.reshape(shard, -1)
    latent_wgrad, router_wgrad = small_wgrad[:, :width], small_wgrad[:, width:]
    ffn_gain_grad = jnp.sum(gain_sums[:, 1, :shard], axis=0)
    gain_sums = jnp.sum(gain_sums[:, 0], axis=0)
    attn_gain_grad = gain_sums[:shard]
    latent_gain_grad = lax.dynamic_slice_in_dim(
        gain_sums, shard + (zi * nx + xi) * lat_len, lat_len, 0
    )
    return (
        block_out,
        tokens_grad,
        attn_gain_grad,
        query_wgrad,
        latent_wgrad,
        latent_gain_grad,
        expand_wgrad,
        output_wgrad,
        ffn_gain_grad,
        router_wgrad,
        shared_gate_wgrad,
        shared_up_wgrad,
        shared_down_wgrad,
        gate_wgrad,
        up_wgrad,
        down_wgrad,
        clip_factor,
    )


def solution(mesh):
    blocks, group = mesh.shape["blk"], mesh.shape["ulysses"]
    chips = Mesh(
        mesh.devices.reshape(Z_SIZE, blocks // Z_SIZE, group // CORES, CORES),
        ("z", "x", "y", "core"),
    )
    blk, uly, every = ("z", "x"), ("y", "core"), ("z", "x", "y", "core")
    rows = P(None, every, None)
    unit = P(every, None, None)
    return jax.shard_map(
        per_device,
        mesh=chips,
        in_specs=(
            rows, P(blk), P(blk, uly), P(blk, None), P(blk), P(blk, uly), P(uly, blk), P(blk),
            P(blk, None), P(blk, uly), P(blk, uly), P(uly, blk), unit, unit, unit, unit, P(), rows,
        ),
        out_specs=(
            rows, rows, P(blk), P(blk, uly), P(blk, None), P(blk), P(blk, uly), P(uly, blk), P(blk),
            P(blk, None), P(blk, uly), P(blk, uly), P(uly, blk), unit, unit, unit, P(uly),
        ),
        check_vma=False,
    )
```
